32 devices in a mesh: led: 8 (over z, core), tile: 4 (over y, x).
Axes of the slice: x: 2, y: 2, z: 4, core: 2. Of those that a mesh axis runs over, the one named last changes fastest.
Arguments:
- spectrum: float32 [16, 8, 4, 8, 65536], P(None, None, 'tile', 'led'), may hold values from -6 to 6
- intensities: bfloat16 [8, 1024, 1024], P('led', 'tile'), may hold values from 0 to 2
- led_of_slot: int32 [8], replicated, may hold values from 0 to 7, each once
- row_offset: int32 [8], replicated, may hold values from 0 to 120
- col_offset: int32 [8], replicated, may hold values from 0 to 56
- tile_mask: int32 [8, 8, 8], replicated, may hold values 0 or 1
- aberration: float32 [5], replicated, may hold values from -1.5 to 1.5
Outputs:
- updated: float32 [16, 8, 4, 8, 65536], P(None, None, 'tile', 'led')
The draws below stay inside these ranges and needn't reach their ends.
Inputs may be any that keep to these rules, and one draw needn't show every extreme that they name: `led_of_slot`: every LED is imaged in exactly one slot.
All inputs are finite; a program needn't handle non-finite values.
Results may differ from the reference program's by a relative error of at most 0.0003.
Values sent between devices are 32-bit elements; how exact they have to be, the bound alone decides.
No kernel may reach another device: no remote copies, remote signals or barrier semaphores. Data moves between devices by JAX's collectives and lax.ppermute only.
A program may use at most 192 MiB of HBM per device.

```python
import jax
import jax.numpy as jnp
from jax import lax

M = 1024
TILE = 128
GR = 16
GC = 8
L_DEV = 1
TW = 8
BAND = 256
CU = 128
LEDS = 8
N_LED = 8
N_TILE = 4


def with_ends(result, rng, least, top_value):
    longest = result.shape.index(max(result.shape))
    spots = []
    for shift in (0, 1):
        where = [jax.random.randint(jax.random.fold_in(rng, axis), (), 0, length) for axis, length in enumerate(result.shape)]
        where[longest] = (where[longest] + shift) % result.shape[longest]
        spots.append(tuple(where))
    return result.at[spots[0]].set(least).at[spots[1]].set(top_value)


def block_levels(key, shape, split, least, top_value):
    gain, own = 1.0, jax.random.fold_in(key, 6)
    for dim, blocks in split:
        steps = jnp.exp(jax.random.uniform(jax.random.fold_in(own, dim), (blocks,), jnp.float32, least / len(split), top_value / len(split)))
        gain = gain * jnp.repeat(steps, shape[dim] // blocks).reshape([-1 if axis == dim else 1 for axis in range(len(shape))])
    return gain


def bell_draw(key, dims, scale, limit, cuts=(), kind=jnp.bfloat16):
    entries = jax.random.normal(key, dims, jnp.float32) * scale
    if len(cuts) > 0:
        entries = block_levels(key, dims, cuts, -0.22, 0.18) * entries
    return jnp.clip(entries, min=-limit, max=limit).astype(kind)


def setup_inputs(seed: int = 0) -> dict:
    keys = jax.random.split(jax.random.key(seed), 8)
    return {
        "spectrum": bell_draw(keys[0], (GR, GC, N_TILE, N_LED, 2 * BAND * CU), 1.0, 6.0, ((2, 4), (3, 8)), jnp.float32),
        "intensities": jnp.clip(2.0 * jax.random.uniform(keys[1], (LEDS, M, M), jnp.float32) ** block_levels(keys[1], (LEDS, M, M), ((0, 8), (1, 4)), -0.2, 0.2), 0.0, 2.0).astype(jnp.bfloat16),
        "led_of_slot": jax.random.permutation(keys[2], LEDS).astype(jnp.int32),
        "row_offset": with_ends(jax.random.randint(keys[3], (LEDS,), 0, GR * TW - TW + 1), jax.random.fold_in(keys[3], 1), 0, GR * TW - TW).astype(jnp.int32),
        "col_offset": with_ends(jax.random.randint(keys[4], (LEDS,), 0, GC * TW - TW + 1), jax.random.fold_in(keys[4], 1), 0, GC * TW - TW).astype(jnp.int32),
        "tile_mask": with_ends((jax.random.randint(keys[5], (LEDS, TW, TW), 0, 4) < 3).astype(jnp.int32), jax.random.fold_in(keys[5], 1), 0, 1),
        "aberration": jnp.clip(jax.random.uniform(keys[6], (5,), jnp.float32, -1.5, 1.5), -1.5, 1.5),
    }


STEP_SIZE = 0.25


def aberration_phase(aberration, coord_p, coord_q):
    radial = coord_p * coord_p + coord_q * coord_q
    return (aberration[0] * (2.0 * radial - 1.0)
            + aberration[1] * (coord_p * coord_p - coord_q * coord_q)
            + aberration[2] * (2.0 * coord_p * coord_q)
            + aberration[3] * ((3.0 * radial - 2.0) * coord_p)
            + aberration[4] * ((3.0 * radial - 2.0) * coord_q))


def reference(spectrum, intensities, led_of_slot, row_offset, col_offset, tile_mask, aberration):
    band_rows = M // N_TILE
    unit_cols = M // N_LED
    pieces = spectrum.reshape(GR, GC, N_TILE, N_LED, 2, band_rows, unit_cols)
    whole_field = jnp.transpose(pieces, (4, 0, 2, 5, 1, 3, 6)).reshape(2, GR * M, GC * M)
    halfway = M // 2
    coords = (jnp.arange(M, dtype=jnp.int32) - halfway).astype(jnp.float32) / halfway
    phase_map = aberration_phase(aberration, coords[:, None], coords[None, :])
    phase_cos = jnp.cos(phase_map)
    phase_sin = jnp.sin(phase_map)
    blocks = jnp.arange(M, dtype=jnp.int32) // TILE

    def one_slot(grad_sum, slot_index):
        led_index = led_of_slot[slot_index]
        row_start = (row_offset[led_index] * TILE).astype(jnp.int32)
        col_start = (col_offset[led_index] * TILE).astype(jnp.int32)
        anchor = jnp.zeros((), jnp.int32)
        window = lax.dynamic_slice(whole_field, (anchor, row_start, col_start), (2, M, M))
        gate_map = tile_mask[led_index].astype(jnp.float32)[blocks][:, blocks]
        pupil_map = gate_map * (phase_cos + 1j * phase_sin)
        masked_field = pupil_map * (window[0] + 1j * window[1])
        wave_field = jnp.fft.ifft2(masked_field) * M
        measured = intensities[slot_index].astype(jnp.float32).T
        excess = jnp.real(wave_field) ** 2 + jnp.imag(wave_field) ** 2 - measured
        back_field = jnp.fft.fft2(excess * wave_field) / M
        grad_piece = jnp.conj(pupil_map) * back_field
        current = lax.dynamic_slice(grad_sum, (anchor, row_start, col_start), (2, M, M))
        current = current + jnp.stack([jnp.real(grad_piece), jnp.imag(grad_piece)]).astype(grad_sum.dtype)
        return lax.dynamic_update_slice(grad_sum, current, (anchor, row_start, col_start)), None

    grad_sum, _ = lax.scan(one_slot, jnp.zeros_like(whole_field), jnp.arange(L_DEV * N_LED, dtype=jnp.int32))
    updated = whole_field - STEP_SIZE * grad_sum
    updated = updated.reshape(2, GR, N_TILE, band_rows, GC, N_LED, unit_cols)
    return jnp.transpose(updated, (1, 4, 2, 5, 0, 3, 6)).reshape(spectrum.shape)
```

```python
import functools
import math

import jax
import jax.numpy as jnp
import numpy as np
from jax import lax
from jax.experimental import pallas as pl
from jax.experimental.pallas import tpu as pltpu
from jax.sharding import PartitionSpec as P

M = 1024
TILE = 128
GR = 16
GC = 8
L_DEV = 1


STEP_SIZE = 0.25
HIGHEST_MODE = lax.Precision.HIGHEST


def aberration_phase(aberration, coord_p, coord_q):
    radial = coord_p * coord_p + coord_q * coord_q
    return (
        aberration[0] * (2.0 * radial - 1.0)
        + aberration[1] * (coord_p * coord_p - coord_q * coord_q)
        + aberration[2] * (2.0 * coord_p * coord_q)
        + aberration[3] * ((3.0 * radial - 2.0) * coord_p)
        + aberration[4] * ((3.0 * radial - 2.0) * coord_q)
    )


def dft_table(length):
    index_run = jnp.arange(length, dtype=jnp.int32)
    column_run = jnp.arange(2 * length, dtype=jnp.int32)
    product_mod = index_run[:, None] * (column_run % length)[None, :] % length
    shifted = (column_run >= length).astype(jnp.float32) * (0.5 * math.pi)
    angles = product_mod.astype(jnp.float32) * (2.0 * math.pi / length) - shifted[None, :]
    return jnp.cos(angles)


def small_tables(rows_len, cols_len, modulus, sign):
    first_run = jnp.arange(rows_len, dtype=jnp.int32)
    second_run = jnp.arange(cols_len, dtype=jnp.int32)
    product_mod = first_run[:, None] * second_run[None, :] % modulus
    angles = product_mod.astype(jnp.float32) * (2.0 * math.pi / modulus)
    return (jnp.cos(angles), sign * jnp.sin(angles))


def factor_dft(real_part, imag_part, sign):
    length = real_part.shape[-1]
    first = 1 << (length.bit_length() - 1) // 2
    second = length // first
    leading = real_part.shape[:-1]
    cos_first, sin_first = small_tables(first, first, first, sign)
    cos_second, sin_second = small_tables(second, second, second, sign)
    twid_cos, twid_sin = small_tables(first, second, length, sign)
    flat_re = real_part.reshape(-1, first, second)
    flat_im = imag_part.reshape(-1, first, second)

    def section_one(data, table):
        return jnp.einsum("rab,ak->rkb", data, table, precision=HIGHEST_MODE)

    def section_two(data, table):
        return jnp.einsum("rkb,bl->rlk", data, table, precision=HIGHEST_MODE)

    mid_re = section_one(flat_re, cos_first) - section_one(flat_im, sin_first)
    mid_im = section_one(flat_im, cos_first) + section_one(flat_re, sin_first)
    turned_re = mid_re * twid_cos[None] - mid_im * twid_sin[None]
    turned_im = mid_re * twid_sin[None] + mid_im * twid_cos[None]
    out_re = section_two(turned_re, cos_second) - section_two(turned_im, sin_second)
    out_im = section_two(turned_im, cos_second) + section_two(turned_re, sin_second)
    return (out_re.reshape(leading + (length,)), out_im.reshape(leading + (length,)))


def times_table(operand, transform):
    return jnp.dot(operand, transform, precision=HIGHEST_MODE, preferred_element_type=jnp.float32)


def pupil_parts(aberration, tile_gate, row_window, col_window):
    halfway = M // 2
    coord_p = ((row_window - halfway).astype(jnp.float32) / halfway)[:, None]
    coord_q = ((col_window - halfway).astype(jnp.float32) / halfway)[None, :]
    phase_map = aberration_phase(aberration, coord_p, coord_q)
    tiles_side = tile_gate.shape[0]
    tile_ids = jnp.arange(tiles_side, dtype=jnp.int32)
    pick_rows = ((row_window // TILE)[:, None] == tile_ids[None, :]).astype(jnp.float32)
    pick_cols = (tile_ids[:, None] == (col_window // TILE)[None, :]).astype(jnp.float32)
    gate_map = times_table(times_table(pick_rows, tile_gate.astype(jnp.float32)), pick_cols)
    return (gate_map * jnp.cos(phase_map), gate_map * jnp.sin(phase_map))


def stack_blocks(real_part, imag_part, tile_count, band_rows):
    slots_now = real_part.shape[0]
    rows_now = real_part.shape[1]
    stacked = jnp.stack(
        [
            real_part.reshape(slots_now, rows_now, tile_count, band_rows),
            imag_part.reshape(slots_now, rows_now, tile_count, band_rows),
        ],
        axis=3,
    )
    return stacked.reshape(slots_now, rows_now, tile_count, 2 * band_rows)


def finish_rows(rows_back, pupil_re, pupil_im, row_first, row_count, led_count, unit_cols):
    image_side = rows_back.shape[0]
    part_re = jnp.transpose(rows_back[:, 0, row_first : row_first + row_count])
    part_im = jnp.transpose(rows_back[:, 1, row_first : row_first + row_count])
    grad_re, grad_im = factor_dft(part_re, part_im, -1.0)
    grad_re = grad_re / image_side
    grad_im = grad_im / image_side
    out_re = pupil_re * grad_re + pupil_im * grad_im
    out_im = pupil_re * grad_im - pupil_im * grad_re
    stacked = jnp.stack([out_re, out_im]).reshape(2, row_count, led_count, unit_cols)
    return jnp.transpose(stacked, (2, 0, 1, 3)).reshape(led_count, 2 * row_count * unit_cols)


def general_shards(spectrum, intensities, led_of_slot, row_offset, col_offset, tile_mask, aberration):
    tile_count = lax.axis_size("tile")
    led_count = lax.axis_size("led")
    band_rows = M // tile_count
    unit_cols = M // led_count
    piece_cells = band_rows * unit_cols
    led_here = lax.axis_index("led")
    tile_here = lax.axis_index("tile")
    transform = dft_table(M)
    row_start = row_offset[led_of_slot] * TILE
    col_start = col_offset[led_of_slot] * TILE
    row_pos = tile_here * band_rows + jnp.arange(band_rows, dtype=jnp.int32)
    first_col_here = led_here * unit_cols
    row_group = (row_start[:, None] + (row_pos[None, :] - row_start[:, None]) % M) // M
    col_group = (col_start + (first_col_here - col_start) % M) // M
    row_group = row_group.reshape(led_count, L_DEV, band_rows)
    col_group = col_group.reshape(led_count, L_DEV, 1)
    line_ids = (
        (row_group * GC + col_group) * band_rows
        + jnp.arange(band_rows, dtype=jnp.int32)[None, None, :]
    ).reshape(-1)
    local_lines = jnp.transpose(
        spectrum.reshape(GR, GC, 2, band_rows, unit_cols), (0, 1, 3, 2, 4)
    ).reshape(GR * GC * band_rows, 2 * unit_cols)
    taken = local_lines[line_ids].reshape(led_count, L_DEV, band_rows, 2, unit_cols)
    outgoing = jnp.transpose(taken, (0, 1, 3, 2, 4)).reshape(led_count, L_DEV, 2 * piece_cells)
    incoming = lax.all_to_all(outgoing, "led", split_axis=0, concat_axis=0, tiled=True)
    col_all = jnp.arange(M, dtype=jnp.int32)
    slot_index = led_here * L_DEV + 0
    led_index = led_of_slot[slot_index]
    first_row = row_offset[led_index] * TILE
    first_col = col_offset[led_index] * TILE
    pupil_re, pupil_im = pupil_parts(
        aberration, tile_mask[led_index], (row_pos - first_row) % M, (col_all - first_col) % M
    )
    window = incoming[:, 0].reshape(led_count, 2, band_rows, unit_cols)
    window = jnp.transpose(window, (1, 2, 0, 3)).reshape(2, band_rows, M)
    field_re = pupil_re * window[0] - pupil_im * window[1]
    field_im = pupil_re * window[1] + pupil_im * window[0]
    fields = [jnp.stack([field_re, field_im])]
    pupils = (pupil_re, pupil_im)
    stacked_fields = jnp.stack(fields).reshape(L_DEV * 2 * band_rows, M)
    mixed = times_table(stacked_fields, transform).reshape(L_DEV, 2, band_rows, 2 * M)
    along_re = mixed[:, 0, :, :M] - mixed[:, 1, :, M:]
    along_im = mixed[:, 0, :, M:] + mixed[:, 1, :, :M]
    outbound = stack_blocks(along_re, along_im, tile_count, band_rows)
    columns = lax.all_to_all(outbound, "tile", split_axis=2, concat_axis=1, tiled=True).reshape(
        L_DEV, M, 2 * band_rows
    )
    flipped = jnp.swapaxes(columns, 1, 2)
    wave_re, wave_im = factor_dft(flipped[:, :band_rows], flipped[:, band_rows:], 1.0)
    wave_re = wave_re / M
    wave_im = wave_im / M
    measured = intensities.astype(jnp.float32)
    excess = wave_re * wave_re + wave_im * wave_im - measured
    back_re, back_im = factor_dft(excess * wave_re, excess * wave_im, -1.0)
    inbound = stack_blocks(back_re, back_im, tile_count, band_rows)
    rows_back = lax.all_to_all(inbound, "tile", split_axis=2, concat_axis=1, tiled=True).reshape(
        L_DEV, M, 2, band_rows
    )
    outgoing_all = jnp.stack(
        [finish_rows(rows_back[0], pupils[0], pupils[1], 0, band_rows, led_count, unit_cols)],
        axis=1,
    )
    received = lax.all_to_all(outgoing_all, "led", split_axis=0, concat_axis=0, tiled=True)
    grad_lines = jnp.transpose(
        received.reshape(led_count, L_DEV, 2, band_rows, unit_cols), (0, 1, 3, 2, 4)
    ).reshape(led_count * L_DEV * band_rows, 2 * unit_cols)
    grad_sum = jax.ops.segment_sum(grad_lines, line_ids, num_segments=GR * GC * band_rows)
    grad_sum = jnp.transpose(grad_sum.reshape(GR, GC, band_rows, 2, unit_cols), (0, 1, 3, 2, 4))
    updated = spectrum - STEP_SIZE * grad_sum.reshape(spectrum.shape)
    return updated


QUARTER = M // 4
HALF_LANES = 64
LANES = 128
SUB = 128
CHUNKS = 2
ANY = pl.ANY
F32 = jnp.float32
BF16 = jnp.bfloat16


def split_table(values):
    high = values.astype(np.float32).astype(jnp.bfloat16)
    low = (values - high.astype(np.float64)).astype(np.float32).astype(jnp.bfloat16)
    return high, low


def quarter_tables():
    grid_b = np.arange(QUARTER)[:, None]
    grid_k = np.arange(QUARTER)[None, :]
    swapped = grid_k ^ HALF_LANES
    row_fwd, row_bwd, col_fwd, col_bwd = [], [], [], []
    for step in range(4):
        lanes = swapped if step % 2 else grid_k
        angle = 2.0 * math.pi * (grid_b * (step + 4 * lanes) % M) / M
        cos, sin = np.cos(angle) / 32.0, np.sin(angle) / 32.0
        for stacked, out in (
            (np.concatenate([cos, sin], 0), row_fwd),
            (np.concatenate([cos.T, -sin.T], 0), row_bwd),
        ):
            high, low = split_table(stacked)
            out.append(np.concatenate([high, high, low], 0))
        angle = 2.0 * math.pi * (grid_b * (step + 4 * grid_k) % M) / M
        cos, sin = np.cos(angle) / 32.0, np.sin(angle) / 32.0
        for stacked, out in (
            (np.concatenate([cos.T, sin.T], 1), col_fwd),
            (np.concatenate([cos, -sin], 1), col_bwd),
        ):
            high, low = split_table(stacked)
            out.append(np.concatenate([high, high, low], 1))
    return [np.stack(t) for t in (row_fwd, row_bwd, col_fwd, col_bwd)]


def halves(x):
    high = x.astype(BF16)
    low = (x - high.astype(F32)).astype(BF16)
    return high, low


def right_product(re, im, table):
    re_high, re_low = halves(re)
    im_high, im_low = halves(im)
    top = jnp.concatenate([re_high, -im_high, re_low, -im_low, re_high, -im_high], axis=1)
    bottom = jnp.concatenate([im_high, re_high, im_low, re_low, im_high, re_high], axis=1)
    return (
        jnp.dot(top, table, preferred_element_type=F32),
        jnp.dot(bottom, table, preferred_element_type=F32),
    )


def left_product(re, im, table):
    re_high, re_low = halves(re)
    im_high, im_low = halves(im)
    left = jnp.concatenate([re_high, -im_high, re_low, -im_low, re_high, -im_high], axis=0)
    right = jnp.concatenate([im_high, re_high, im_low, re_low, im_high, re_high], axis=0)
    return (
        jnp.dot(table, left, preferred_element_type=F32),
        jnp.dot(table, right, preferred_element_type=F32),
    )


def butterfly(parts, sign):
    (r0, i0), (r1, i1), (r2, i2), (r3, i3) = parts
    sr, si, dr, di = r0 + r2, i0 + i2, r0 - r2, i0 - i2
    tr, ti, er, ei = r1 + r3, i1 + i3, r1 - r3, i1 - i3
    if sign > 0:
        return ((sr + tr, si + ti), (dr - ei, di + er), (sr - tr, si - ti), (dr + ei, di - er))
    return ((sr + tr, si + ti), (dr + ei, di - er), (sr - tr, si - ti), (dr - ei, di + er))


def cos_sin(angle):
    turns = jnp.floor(angle * (2.0 / math.pi) + 0.5)
    rest = ((angle - turns * 1.5703125) - turns * 4.837512969970703125e-4) - turns * 7.549789948768648e-8
    square = rest * rest
    sine = rest + rest * square * (
        -1.6666654611e-1 + square * (8.3321608736e-3 - square * 1.9515295891e-4)
    )
    cosine = 1.0 - 0.5 * square + square * square * (
        4.166664568298827e-2 + square * (-1.388731625493765e-3 + square * 2.443315711809948e-5)
    )
    quarter = turns.astype(jnp.int32) & 3
    odd = (quarter & 1) == 1
    cos_out = jnp.where(odd, sine, cosine)
    sin_out = jnp.where(odd, cosine, sine)
    cos_out = jnp.where((quarter == 1) | (quarter == 2), -cos_out, cos_out)
    sin_out = jnp.where(quarter >= 2, -sin_out, sin_out)
    return cos_out, sin_out


def piece_row(slot, row_first, col_first, band, lead, row_off, col_off):
    led = lead[slot]
    row_start = row_off[led] * TILE
    col_start = col_off[led] * TILE
    row_group = (row_start + ((row_first - row_start) & (M - 1))) // M
    col_group = (col_start + ((col_first - col_start) & (M - 1))) // M
    return (row_group * GC + col_group) * (2 * band)


def start_all(copies):
    for copy in copies:
        copy.start()


def wait_all(copies):
    for copy in copies:
        copy.wait()


def gather_kernel(sizes, chunk, lead, row_off, col_off, spectrum, *refs):
    leds, tiles, band, rows = sizes
    outs, sems = refs[:-1], refs[-1]
    me, tile = lax.axis_index("led"), lax.axis_index("tile")
    copies = []
    for shift in range(leds):
        slot = lax.rem(me + shift, leds)
        base = piece_row(slot, tile * band + chunk * rows, me * LANES, band, lead, row_off, col_off)
        for part in range(2):
            first = pl.multiple_of(base + part * band + chunk * rows, 8)
            copies.append(
                pltpu.make_async_copy(
                    spectrum.at[pl.ds(first, rows)], outs[shift].at[part], sems.at[shift, part]
                )
            )
    start_all(copies)
    wait_all(copies)


def prepare_kernel(sizes, lead, row_off, col_off, mask, aberration, intensities, pupil, images, turned):
    leds, tiles, band, rows = sizes
    me, tile = lax.axis_index("led"), lax.axis_index("tile")
    led = lead[me]
    line = lax.broadcasted_iota(jnp.int32, (band, band), 0)
    place = lax.broadcasted_iota(jnp.int32, (band, band), 1)
    residue = 2 * (place // LANES) + (((place // HALF_LANES) & 1) ^ (tile & 1))
    wanted = residue + 4 * (place & (HALF_LANES - 1))
    chosen = (line == wanted).astype(BF16)
    for block in range(M // QUARTER):
        columns = lax.dot_general(
            intensities[:, block * QUARTER : (block + 1) * QUARTER],
            chosen,
            (((0,), (0,)), ((), ())),
            preferred_element_type=F32,
        )
        for side in range(band // LANES):
            turned[side, block * QUARTER : (block + 1) * QUARTER, :] = columns[
                :, side * LANES : (side + 1) * LANES
            ]
    for part in range(4):
        for side in range(band // LANES):
            images[part * QUARTER : (part + 1) * QUARTER, side * LANES : (side + 1) * LANES] = turned[
                side, pl.ds(part, QUARTER, 4), :
            ]
    half = M // 2
    run_p = lax.broadcasted_iota(jnp.int32, (TILE, TILE), 0)
    run_q = lax.broadcasted_iota(jnp.int32, (TILE, TILE), 1)
    tile_rows = band // TILE
    for i in range(tile_rows):
        row_tile = (tile * tile_rows + i - row_off[led]) & (M // TILE - 1)
        coord_p = (run_p + (row_tile * TILE - half)).astype(F32) / half
        for j in range(M // TILE):
            col_tile = (j - col_off[led]) & (M // TILE - 1)
            coord_q = (run_q + (col_tile * TILE - half)).astype(F32) / half
            gate = mask[led, row_tile, col_tile].astype(F32)
            cosine, sine = cos_sin(aberration_phase(aberration, coord_p, coord_q))
            where = (slice(i * TILE, (i + 1) * TILE), slice(j * TILE, (j + 1) * TILE))
            pupil[(0,) + where] = gate * cosine
            pupil[(1,) + where] = gate * sine


def forward_kernel(sizes, chunk, table, pupil, *refs):
    leds, tiles, band, rows = sizes
    pieces, refs = refs[:leds], refs[leds:]
    outs, refs = refs[:tiles], refs[tiles:]
    table_v, pupil_v, window, result, sems, sems_out = refs
    me, tile = lax.axis_index("led"), lax.axis_index("tile")
    copies = []
    for shift in range(leds):
        first = pl.multiple_of(lax.rem(me - shift + leds, leds) * LANES, LANES)
        copies.append(
            pltpu.make_async_copy(pieces[shift], window.at[:, :, pl.ds(first, LANES)], sems.at[shift])
        )
    copies.append(
        pltpu.make_async_copy(pupil.at[:, chunk * rows : (chunk + 1) * rows], pupil_v, sems.at[leds])
    )
    copies.append(pltpu.make_async_copy(table, table_v, sems.at[leds + 1]))
    start_all(copies)
    wait_all(copies)
    parts = []
    for a in range(4):
        cells = slice(a * QUARTER, (a + 1) * QUARTER)
        gate_re, gate_im = pupil_v[0, :, cells], pupil_v[1, :, cells]
        cell_re, cell_im = window[0, :, cells], window[1, :, cells]
        parts.append((gate_re * cell_re - gate_im * cell_im, gate_re * cell_im + gate_im * cell_re))
    mixed = butterfly(parts, 1)
    lines = [right_product(re, im, table_v[k]) for k, (re, im) in enumerate(mixed)]
    lane = lax.broadcasted_iota(jnp.int32, (rows, LANES), 1)
    for other in range(tiles):
        block = slice((other // 2) * LANES, (other // 2 + 1) * LANES)
        for part in range(2):
            for pair in range(2):
                first, second = lines[2 * pair][part][:, block], lines[2 * pair + 1][part][:, block]
                if other % 2:
                    first, second = second, first
                result[other, part, :, pair * LANES : (pair + 1) * LANES] = jnp.where(
                    lane < HALF_LANES, first, second
                )
    copies = [
        pltpu.make_async_copy(result.at[tile ^ shift], outs[shift], sems_out.at[shift])
        for shift in range(tiles)
    ]
    start_all(copies)
    wait_all(copies)


def middle_kernel(sizes, table, table_back, images, *refs):
    leds, tiles, band, rows = sizes
    chunks = band // rows
    blocks, refs = refs[: chunks * tiles], refs[chunks * tiles :]
    outs, refs = refs[: chunks * tiles], refs[chunks * tiles :]
    table_v, back_v, images_v, field, residual, sems, sems_out = refs
    tile = lax.axis_index("tile")
    copies = []
    for chunk in range(chunks):
        for shift in range(tiles):
            where = chunk * tiles + shift
            copies.append(
                pltpu.make_async_copy(
                    blocks[where],
                    field.at[tile ^ shift, :, chunk * rows : (chunk + 1) * rows],
                    sems.at[where],
                )
            )
    count = chunks * tiles
    copies.append(pltpu.make_async_copy(table, table_v, sems.at[count]))
    copies.append(pltpu.make_async_copy(images, images_v, sems.at[count + 1]))
    copies.append(pltpu.make_async_copy(table_back, back_v, sems.at[count + 2]))
    start_all(copies)
    wait_all(copies)
    mixed = butterfly([(field[a, 0], field[a, 1]) for a in range(4)], 1)
    for k, (re, im) in enumerate(mixed):
        wave_re, wave_im = left_product(re, im, table_v[k])
        measured = images_v[k * QUARTER : (k + 1) * QUARTER, :]
        excess = wave_re * wave_re + wave_im * wave_im - measured
        back_re, back_im = left_product(excess * wave_re, excess * wave_im, back_v[k])
        residual[k, 0] = back_re
        residual[k, 1] = back_im
    mixed = butterfly([(residual[k, 0], residual[k, 1]) for k in range(4)], -1)
    for a, (re, im) in enumerate(mixed):
        field[a, 0] = re
        field[a, 1] = im
    copies = []
    for chunk in range(chunks):
        for shift in range(tiles):
            where = chunk * tiles + shift
            copies.append(
                pltpu.make_async_copy(
                    field.at[tile ^ shift, :, chunk * rows : (chunk + 1) * rows],
                    outs[where],
                    sems_out.at[where],
                )
            )
    start_all(copies)
    wait_all(copies)


def backward_kernel(sizes, chunk, table, pupil, *refs):
    leds, tiles, band, rows = sizes
    blocks, refs = refs[:tiles], refs[tiles:]
    outs, refs = refs[:leds], refs[leds:]
    table_v, pupil_v, lines, result, sems, sems_out = refs
    me, tile = lax.axis_index("led"), lax.axis_index("tile")
    copies = [
        pltpu.make_async_copy(blocks[shift], lines.at[tile ^ shift], sems.at[shift])
        for shift in range(tiles)
    ]
    copies.append(
        pltpu.make_async_copy(pupil.at[:, chunk * rows : (chunk + 1) * rows], pupil_v, sems.at[tiles])
    )
    copies.append(pltpu.make_async_copy(table, table_v, sems.at[tiles + 1]))
    start_all(copies)
    wait_all(copies)
    lane = lax.broadcasted_iota(jnp.int32, (rows, LANES), 1)
    parts = []
    for k in range(4):
        cells = slice((k // 2) * LANES, (k // 2 + 1) * LANES)
        both = []
        for part in range(2):
            joined = []
            for pair in range(tiles // 2):
                first, second = lines[2 * pair, part, :, cells], lines[2 * pair + 1, part, :, cells]
                if k % 2:
                    first, second = second, first
                joined.append(jnp.where(lane < HALF_LANES, first, second))
            both.append(jnp.concatenate(joined, axis=1))
        parts.append(right_product(both[0], both[1], table_v[k]))
    for a, (re, im) in enumerate(butterfly(parts, -1)):
        cells = slice(a * QUARTER, (a + 1) * QUARTER)
        gate_re, gate_im = pupil_v[0, :, cells], pupil_v[1, :, cells]
        result[0, :, cells] = gate_re * re + gate_im * im
        result[1, :, cells] = gate_re * im - gate_im * re
    copies = []
    for shift in range(leds):
        first = pl.multiple_of(lax.rem(me + shift, leds) * LANES, LANES)
        copies.append(
            pltpu.make_async_copy(
                result.at[:, :, pl.ds(first, LANES)], outs[shift], sems_out.at[shift]
            )
        )
    start_all(copies)
    wait_all(copies)


def update_kernel(sizes, chunk, lead, row_off, col_off, spectrum, buffer, *refs):
    leds, tiles, band, rows = sizes
    pieces, refs = refs[:leds], refs[leds:]
    updated, grads, cells, sems, sems_in, sems_out = refs
    me, tile = lax.axis_index("led"), lax.axis_index("tile")
    bases = [
        piece_row(slot, tile * band + chunk * rows, me * LANES, band, lead, row_off, col_off)
        for slot in range(leds)
    ]
    copies = []
    for shift in range(leds):
        slot = lax.rem(me - shift + leds, leds)
        copies.append(pltpu.make_async_copy(pieces[shift], grads.at[slot], sems.at[shift]))
    for slot in range(leds):
        for part in range(2):
            first = pl.multiple_of(bases[slot] + part * band + chunk * rows, 8)
            copies.append(
                pltpu.make_async_copy(
                    spectrum.at[pl.ds(first, rows)], cells.at[slot, part], sems_in.at[slot, part]
                )
            )
    start_all(copies)
    wait_all(copies)
    firsts = []
    for slot in range(leds):
        is_first = jnp.bool_(True)
        for earlier in range(slot):
            is_first = jnp.logical_and(is_first, bases[earlier] != bases[slot])
        firsts.append(is_first)
        for later in range(slot + 1, leds):

            @pl.when(jnp.logical_and(is_first, bases[later] == bases[slot]))
            def _():
                grads[slot] = grads[slot] + grads[later]

        cells[slot] = cells[slot] - STEP_SIZE * grads[slot]
    for waiting in (False, True):
        for slot in range(leds):

            @pl.when(firsts[slot])
            def _():
                for part in range(2):
                    first = pl.multiple_of(bases[slot] + part * band + chunk * rows, 8)
                    copy = pltpu.make_async_copy(
                        cells.at[slot, part], updated.at[pl.ds(first, rows)], sems_out.at[slot, part]
                    )
                    if waiting:
                        copy.wait()
                    else:
                        copy.start()


COPY_PARTS = 16


def copy_kernel(spectrum, copied, sems):
    lines = spectrum.shape[0] // COPY_PARTS
    copies = [
        pltpu.make_async_copy(
            spectrum.at[pl.ds(n * lines, lines)], copied.at[pl.ds(n * lines, lines)], sems.at[n]
        )
        for n in range(COPY_PARTS)
    ]
    start_all(copies)
    wait_all(copies)


def call(kernel, name, ins, outs, scratch, flops=0, moved=0, aliases=None, vmem=16):
    return pl.pallas_call(
        kernel,
        name=name,
        out_shape=outs,
        in_specs=[pl.BlockSpec(memory_space=place) for place in ins],
        out_specs=jax.tree.map(lambda _: pl.BlockSpec(memory_space=ANY), outs),
        scratch_shapes=scratch,
        input_output_aliases=aliases or {},
        cost_estimate=pl.CostEstimate(flops=flops, bytes_accessed=moved, transcendentals=0),
        compiler_params=pltpu.CompilerParams(vmem_limit_bytes=vmem * 2**20),
    )


def unit_shards(spectrum, intensities, led_of_slot, row_offset, col_offset, tile_mask, aberration):
    tiles = lax.axis_size("tile")
    leds = lax.axis_size("led")
    band = M // tiles
    rows = band // CHUNKS
    sizes = (leds, tiles, band, rows)
    row_fwd, row_bwd, col_fwd, col_bwd = (jnp.asarray(t) for t in quarter_tables())
    flat = spectrum.reshape(-1, LANES)
    smem, vmem = pltpu.SMEM, pltpu.VMEM
    dma = pltpu.SemaphoreType.DMA
    f32 = lambda *shape: jax.ShapeDtypeStruct(shape, F32)
    part = functools.partial

    def over_led(arrays):
        moved = [arrays[0]]
        for shift in range(1, leds):
            moved.append(
                lax.ppermute(arrays[shift], "led", [(i, (i + shift) % leds) for i in range(leds)])
            )
        return moved

    def over_tile(arrays):
        moved = [arrays[0]]
        for shift in range(1, tiles):
            moved.append(lax.ppermute(arrays[shift], "tile", [(i, i ^ shift) for i in range(tiles)]))
        return moved

    piece = f32(2, rows, LANES)
    taken = [
        call(
            part(gather_kernel, sizes, chunk), f"gather_{chunk}", [smem] * 3 + [ANY], [piece] * leds,
            [dma((leds, 2))], moved=4 * leds * piece.size * 2,
        )(led_of_slot, row_offset, col_offset, flat)
        for chunk in range(CHUNKS)
    ]
    arrived = [over_led(arrays) for arrays in taken]
    pupil, images = pl.pallas_call(
        part(prepare_kernel, sizes),
        name="prepare",
        out_shape=[f32(2, band, M), f32(M, band)],
        in_specs=[pl.BlockSpec(memory_space=smem)] * 5 + [pl.BlockSpec(memory_space=vmem)],
        out_specs=[pl.BlockSpec(memory_space=vmem)] * 2,
        scratch_shapes=[pltpu.VMEM((band // LANES, M, LANES), F32)],
        compiler_params=pltpu.CompilerParams(vmem_limit_bytes=24 * 2**20),
        cost_estimate=pl.CostEstimate(flops=2 * 10**9, bytes_accessed=4 * 10**6, transcendentals=0),
    )(led_of_slot, row_offset, col_offset, tile_mask, aberration, intensities[0])
    copied = call(
        copy_kernel, "copy_spectrum", [ANY], f32(*flat.shape), [dma((COPY_PARTS,))], moved=8 * flat.size
    )(flat)
    block = f32(2, rows, band)
    table_shape = (4, 6 * QUARTER, QUARTER)
    received = []
    for chunk in range(CHUNKS):
        lines = call(
            part(forward_kernel, sizes, chunk), f"forward_{chunk}", [ANY] * (2 + leds), [block] * tiles,
            [
                pltpu.VMEM(table_shape, BF16), pltpu.VMEM((2, rows, M), F32),
                pltpu.VMEM((2, rows, M), F32), pltpu.VMEM((tiles, 2, rows, band), F32),
                dma((leds + 2,)), dma((tiles,)),
            ],
            flops=24 * rows * M * QUARTER, moved=2**23, vmem=40,
        )(row_fwd, pupil, *arrived[chunk])
        received += over_tile(lines)
    count = CHUNKS * tiles
    returned = call(
        part(middle_kernel, sizes), "middle", [ANY] * (3 + count), [block] * count,
        [
            pltpu.VMEM((4, QUARTER, 6 * QUARTER), BF16), pltpu.VMEM((4, QUARTER, 6 * QUARTER), BF16),
            pltpu.VMEM((M, band), F32), pltpu.VMEM((4, 2, QUARTER, band), F32),
            pltpu.VMEM((4, 2, QUARTER, band), F32), dma((count + 3,)), dma((count,)),
        ],
        flops=48 * band * M * QUARTER, moved=2**24, vmem=48,
    )(col_fwd, col_bwd, images, *received)
    updated = copied
    for chunk in range(CHUNKS):
        lines = over_tile(returned[chunk * tiles : (chunk + 1) * tiles])
        pieces = call(
            part(backward_kernel, sizes, chunk), f"backward_{chunk}", [ANY] * (2 + tiles), [piece] * leds,
            [
                pltpu.VMEM(table_shape, BF16), pltpu.VMEM((2, rows, M), F32),
                pltpu.VMEM((tiles, 2, rows, band), F32), pltpu.VMEM((2, rows, M), F32),
                dma((tiles + 2,)), dma((leds,)),
            ],
            flops=24 * rows * M * QUARTER, moved=2**23, vmem=40,
        )(row_bwd, pupil, *lines)
        updated = call(
            part(update_kernel, sizes, chunk), f"update_{chunk}", [smem] * 3 + [ANY] * (2 + leds),
            f32(*flat.shape),
            [
                pltpu.VMEM((leds, 2, rows, LANES), F32), pltpu.VMEM((leds, 2, rows, LANES), F32),
                dma((leds,)), dma((leds, 2)), dma((leds, 2)),
            ],
            moved=2**22, aliases={4: 0},
        )(led_of_slot, row_offset, col_offset, flat, updated, *over_led(pieces))
    return updated.reshape(spectrum.shape)


def solution(mesh):
    placed = (P(None, None, "tile", "led", None), P("led", "tile", None), P(), P(), P(), P(), P())
    whole_units = mesh.shape["tile"] == 4 and M // mesh.shape["led"] == LANES
    return jax.shard_map(
        unit_shards if whole_units else general_shards,
        mesh=mesh,
        in_specs=placed,
        out_specs=P(None, None, "tile", "led", None),
        check_vma=False,
    )
```

```python
import functools
import math

import jax
import jax.numpy as jnp
import numpy as np
from jax import lax
from jax.experimental import pallas as pl
from jax.experimental.pallas import tpu as pltpu
from jax.sharding import PartitionSpec as P

M = 1024
TILE = 128
GR = 16
GC = 8
L_DEV = 1


STEP_SIZE = 0.25
HIGHEST_MODE = lax.Precision.HIGHEST


def aberration_phase(aberration, coord_p, coord_q):
    radial = coord_p * coord_p + coord_q * coord_q
    return (
        aberration[0] * (2.0 * radial - 1.0)
        + aberration[1] * (coord_p * coord_p - coord_q * coord_q)
        + aberration[2] * (2.0 * coord_p * coord_q)
        + aberration[3] * ((3.0 * radial - 2.0) * coord_p)
        + aberration[4] * ((3.0 * radial - 2.0) * coord_q)
    )


def dft_table(length):
    index_run = jnp.arange(length, dtype=jnp.int32)
    column_run = jnp.arange(2 * length, dtype=jnp.int32)
    product_mod = index_run[:, None] * (column_run % length)[None, :] % length
    shifted = (column_run >= length).astype(jnp.float32) * (0.5 * math.pi)
    angles = product_mod.astype(jnp.float32) * (2.0 * math.pi / length) - shifted[None, :]
    return jnp.cos(angles)


def small_tables(rows_len, cols_len, modulus, sign):
    first_run = jnp.arange(rows_len, dtype=jnp.int32)
    second_run = jnp.arange(cols_len, dtype=jnp.int32)
    product_mod = first_run[:, None] * second_run[None, :] % modulus
    angles = product_mod.astype(jnp.float32) * (2.0 * math.pi / modulus)
    return (jnp.cos(angles), sign * jnp.sin(angles))


def factor_dft(real_part, imag_part, sign):
    length = real_part.shape[-1]
    first = 1 << (length.bit_length() - 1) // 2
    second = length // first
    leading = real_part.shape[:-1]
    cos_first, sin_first = small_tables(first, first, first, sign)
    cos_second, sin_second = small_tables(second, second, second, sign)
    twid_cos, twid_sin = small_tables(first, second, length, sign)
    flat_re = real_part.reshape(-1, first, second)
    flat_im = imag_part.reshape(-1, first, second)

    def section_one(data, table):
        return jnp.einsum("rab,ak->rkb", data, table, precision=HIGHEST_MODE)

    def section_two(data, table):
        return jnp.einsum("rkb,bl->rlk", data, table, precision=HIGHEST_MODE)

    mid_re = section_one(flat_re, cos_first) - section_one(flat_im, sin_first)
    mid_im = section_one(flat_im, cos_first) + section_one(flat_re, sin_first)
    turned_re = mid_re * twid_cos[None] - mid_im * twid_sin[None]
    turned_im = mid_re * twid_sin[None] + mid_im * twid_cos[None]
    out_re = section_two(turned_re, cos_second) - section_two(turned_im, sin_second)
    out_im = section_two(turned_im, cos_second) + section_two(turned_re, sin_second)
    return (out_re.reshape(leading + (length,)), out_im.reshape(leading + (length,)))


def times_table(operand, transform):
    return jnp.dot(operand, transform, precision=HIGHEST_MODE, preferred_element_type=jnp.float32)


def pupil_parts(aberration, tile_gate, row_window, col_window):
    halfway = M // 2
    coord_p = ((row_window - halfway).astype(jnp.float32) / halfway)[:, None]
    coord_q = ((col_window - halfway).astype(jnp.float32) / halfway)[None, :]
    phase_map = aberration_phase(aberration, coord_p, coord_q)
    tiles_side = tile_gate.shape[0]
    tile_ids = jnp.arange(tiles_side, dtype=jnp.int32)
    pick_rows = ((row_window // TILE)[:, None] == tile_ids[None, :]).astype(jnp.float32)
    pick_cols = (tile_ids[:, None] == (col_window // TILE)[None, :]).astype(jnp.float32)
    gate_map = times_table(times_table(pick_rows, tile_gate.astype(jnp.float32)), pick_cols)
    return (gate_map * jnp.cos(phase_map), gate_map * jnp.sin(phase_map))


def stack_blocks(real_part, imag_part, tile_count, band_rows):
    slots_now = real_part.shape[0]
    rows_now = real_part.shape[1]
    stacked = jnp.stack(
        [
            real_part.reshape(slots_now, rows_now, tile_count, band_rows),
            imag_part.reshape(slots_now, rows_now, tile_count, band_rows),
        ],
        axis=3,
    )
    return stacked.reshape(slots_now, rows_now, tile_count, 2 * band_rows)


def finish_rows(rows_back, pupil_re, pupil_im, row_first, row_count, led_count, unit_cols):
    image_side = rows_back.shape[0]
    part_re = jnp.transpose(rows_back[:, 0, row_first : row_first + row_count])
    part_im = jnp.transpose(rows_back[:, 1, row_first : row_first + row_count])
    grad_re, grad_im = factor_dft(part_re, part_im, -1.0)
    grad_re = grad_re / image_side
    grad_im = grad_im / image_side
    out_re = pupil_re * grad_re + pupil_im * grad_im
    out_im = pupil_re * grad_im - pupil_im * grad_re
    stacked = jnp.stack([out_re, out_im]).reshape(2, row_count, led_count, unit_cols)
    return jnp.transpose(stacked, (2, 0, 1, 3)).reshape(led_count, 2 * row_count * unit_cols)


def general_shards(spectrum, intensities, led_of_slot, row_offset, col_offset, tile_mask, aberration):
    tile_count = lax.axis_size("tile")
    led_count = lax.axis_size("led")
    band_rows = M // tile_count
    unit_cols = M // led_count
    piece_cells = band_rows * unit_cols
    led_here = lax.axis_index("led")
    tile_here = lax.axis_index("tile")
    transform = dft_table(M)
    row_start = row_offset[led_of_slot] * TILE
    col_start = col_offset[led_of_slot] * TILE
    row_pos = tile_here * band_rows + jnp.arange(band_rows, dtype=jnp.int32)
    first_col_here = led_here * unit_cols
    row_group = (row_start[:, None] + (row_pos[None, :] - row_start[:, None]) % M) // M
    col_group = (col_start + (first_col_here - col_start) % M) // M
    row_group = row_group.reshape(led_count, L_DEV, band_rows)
    col_group = col_group.reshape(led_count, L_DEV, 1)
    line_ids = (
        (row_group * GC + col_group) * band_rows
        + jnp.arange(band_rows, dtype=jnp.int32)[None, None, :]
    ).reshape(-1)
    local_lines = jnp.transpose(
        spectrum.reshape(GR, GC, 2, band_rows, unit_cols), (0, 1, 3, 2, 4)
    ).reshape(GR * GC * band_rows, 2 * unit_cols)
    taken = local_lines[line_ids].reshape(led_count, L_DEV, band_rows, 2, unit_cols)
    outgoing = jnp.transpose(taken, (0, 1, 3, 2, 4)).reshape(led_count, L_DEV, 2 * piece_cells)
    incoming = lax.all_to_all(outgoing, "led", split_axis=0, concat_axis=0, tiled=True)
    col_all = jnp.arange(M, dtype=jnp.int32)
    slot_index = led_here * L_DEV + 0
    led_index = led_of_slot[slot_index]
    first_row = row_offset[led_index] * TILE
    first_col = col_offset[led_index] * TILE
    pupil_re, pupil_im = pupil_parts(
        aberration, tile_mask[led_index], (row_pos - first_row) % M, (col_all - first_col) % M
    )
    window = incoming[:, 0].reshape(led_count, 2, band_rows, unit_cols)
    window = jnp.transpose(window, (1, 2, 0, 3)).reshape(2, band_rows, M)
    field_re = pupil_re * window[0] - pupil_im * window[1]
    field_im = pupil_re * window[1] + pupil_im * window[0]
    fields = [jnp.stack([field_re, field_im])]
    pupils = (pupil_re, pupil_im)
    stacked_fields = jnp.stack(fields).reshape(L_DEV * 2 * band_rows, M)
    mixed = times_table(stacked_fields, transform).reshape(L_DEV, 2, band_rows, 2 * M)
    along_re = mixed[:, 0, :, :M] - mixed[:, 1, :, M:]
    along_im = mixed[:, 0, :, M:] + mixed[:, 1, :, :M]
    outbound = stack_blocks(along_re, along_im, tile_count, band_rows)
    columns = lax.all_to_all(outbound, "tile", split_axis=2, concat_axis=1, tiled=True).reshape(
        L_DEV, M, 2 * band_rows
    )
    flipped = jnp.swapaxes(columns, 1, 2)
    wave_re, wave_im = factor_dft(flipped[:, :band_rows], flipped[:, band_rows:], 1.0)
    wave_re = wave_re / M
    wave_im = wave_im / M
    measured = intensities.astype(jnp.float32)
    excess = wave_re * wave_re + wave_im * wave_im - measured
    back_re, back_im = factor_dft(excess * wave_re, excess * wave_im, -1.0)
    inbound = stack_blocks(back_re, back_im, tile_count, band_rows)
    rows_back = lax.all_to_all(inbound, "tile", split_axis=2, concat_axis=1, tiled=True).reshape(
        L_DEV, M, 2, band_rows
    )
    outgoing_all = jnp.stack(
        [finish_rows(rows_back[0], pupils[0], pupils[1], 0, band_rows, led_count, unit_cols)],
        axis=1,
    )
    received = lax.all_to_all(outgoing_all, "led", split_axis=0, concat_axis=0, tiled=True)
    grad_lines = jnp.transpose(
        received.reshape(led_count, L_DEV, 2, band_rows, unit_cols), (0, 1, 3, 2, 4)
    ).reshape(led_count * L_DEV * band_rows, 2 * unit_cols)
    grad_sum = jax.ops.segment_sum(grad_lines, line_ids, num_segments=GR * GC * band_rows)
    grad_sum = jnp.transpose(grad_sum.reshape(GR, GC, band_rows, 2, unit_cols), (0, 1, 3, 2, 4))
    updated = spectrum - STEP_SIZE * grad_sum.reshape(spectrum.shape)
    return updated


QUARTER = M // 4
HALF_LANES = 64
LANES = 128
SUB = 128
FORWARD_CUTS = (4, 4)
COPY_FIRST = False
EARLY = (0,)
COST = 1
SECOND_AFTER = ()
FORWARD_LED = (False, False)
BACKWARD_LED = (True, False)
FORWARD_TILE = (True, False)
BACKWARD_TILE = (False, False)
BACKWARD_CUTS = (4, 4)
MIDDLE_VMEM = 20
ROW_VMEM = 14
ANY = pl.ANY
HBM = pltpu.HBM
F32 = jnp.float32
BF16 = jnp.bfloat16


def split_table(values):
    high = values.astype(np.float32).astype(jnp.bfloat16)
    low = (values - high.astype(np.float64)).astype(np.float32).astype(jnp.bfloat16)
    return high, low


def quarter_tables():
    grid_b = np.arange(QUARTER)[:, None]
    grid_k = np.arange(QUARTER)[None, :]
    swapped = grid_k ^ HALF_LANES
    row_fwd, row_bwd, col_fwd, col_bwd = [], [], [], []
    for step in range(4):
        lanes = swapped if step % 2 else grid_k
        angle = 2.0 * math.pi * (grid_b * (step + 4 * lanes) % M) / M
        cos, sin = np.cos(angle) / 32.0, np.sin(angle) / 32.0
        for stacked, out in (
            (np.concatenate([cos, sin], 0), row_fwd),
            (np.concatenate([cos.T, -sin.T], 0), row_bwd),
        ):
            high, low = split_table(stacked)
            out.append(np.concatenate([high, low], 0))
        angle = 2.0 * math.pi * (grid_b * (step + 4 * grid_k) % M) / M
        cos, sin = np.cos(angle) / 32.0, np.sin(angle) / 32.0
        for stacked, out in (
            (np.concatenate([cos.T, sin.T], 1), col_fwd),
            (np.concatenate([cos, -sin], 1), col_bwd),
        ):
            high, low = split_table(stacked)
            out.append(np.concatenate([high, low], 1))
    return [np.stack(t) for t in (row_fwd, row_bwd, col_fwd, col_bwd)]


def halves(x):
    high = x.astype(BF16)
    low = (x - high.astype(F32)).astype(BF16)
    return high, low


def right_product(re, im, table):
    re_high, re_low = halves(re)
    im_high, im_low = halves(im)
    table = jnp.concatenate([table[: 2 * QUARTER], table], axis=0)
    top = jnp.concatenate([re_high, -im_high, re_low, -im_low, re_high, -im_high], axis=1)
    bottom = jnp.concatenate([im_high, re_high, im_low, re_low, im_high, re_high], axis=1)
    return (
        jnp.dot(top, table, preferred_element_type=F32),
        jnp.dot(bottom, table, preferred_element_type=F32),
    )


def left_product(re, im, table):
    re_high, re_low = halves(re)
    im_high, im_low = halves(im)
    table = jnp.concatenate([table[:, : 2 * QUARTER], table], axis=1)
    left = jnp.concatenate([re_high, -im_high, re_low, -im_low, re_high, -im_high], axis=0)
    right = jnp.concatenate([im_high, re_high, im_low, re_low, im_high, re_high], axis=0)
    return (
        jnp.dot(table, left, preferred_element_type=F32),
        jnp.dot(table, right, preferred_element_type=F32),
    )


def butterfly(parts, sign):
    (r0, i0), (r1, i1), (r2, i2), (r3, i3) = parts
    sr, si, dr, di = r0 + r2, i0 + i2, r0 - r2, i0 - i2
    tr, ti, er, ei = r1 + r3, i1 + i3, r1 - r3, i1 - i3
    if sign > 0:
        return ((sr + tr, si + ti), (dr - ei, di + er), (sr - tr, si - ti), (dr + ei, di - er))
    return ((sr + tr, si + ti), (dr + ei, di - er), (sr - tr, si - ti), (dr - ei, di + er))


def cos_sin(angle):
    turns = jnp.floor(angle * (2.0 / math.pi) + 0.5)
    rest = ((angle - turns * 1.5703125) - turns * 4.837512969970703125e-4) - turns * 7.549789948768648e-8
    square = rest * rest
    sine = rest + rest * square * (
        -1.6666654611e-1 + square * (8.3321608736e-3 - square * 1.9515295891e-4)
    )
    cosine = 1.0 - 0.5 * square + square * square * (
        4.166664568298827e-2 + square * (-1.388731625493765e-3 + square * 2.443315711809948e-5)
    )
    quarter = turns.astype(jnp.int32) & 3
    odd = (quarter & 1) == 1
    cos_out = jnp.where(odd, sine, cosine)
    sin_out = jnp.where(odd, cosine, sine)
    cos_out = jnp.where((quarter == 1) | (quarter == 2), -cos_out, cos_out)
    sin_out = jnp.where(quarter >= 2, -sin_out, sin_out)
    return cos_out, sin_out


def runs_of(band, cuts):
    unit = band // sum(cuts)
    runs, first = [], 0
    for cut in cuts:
        runs.append((first, cut * unit))
        first += cut * unit
    return runs


def spans_of(run):
    first, rows = run
    spans, last = [], first + rows
    while first < last:
        end = min(last, (first // TILE + 1) * TILE)
        spans.append((first, end - first))
        first = end
    return spans


def block_base(slot, row_first, col_first, band, lead, row_off, col_off):
    led = lead[slot]
    row_start = row_off[led] * TILE
    col_start = col_off[led] * TILE
    row_group = (row_start + ((row_first - row_start) & (M - 1))) // M
    col_group = (col_start + ((col_first - col_start) & (M - 1))) // M
    return (row_group * GC + col_group) * (2 * band)


def start_all(copies):
    for copy in copies:
        copy.start()


def wait_all(copies):
    for copy in copies:
        copy.wait()


def gather_kernel(sizes, run, packed, after, lead, row_off, col_off, spectrum, *refs):
    leds, tiles, band = sizes
    outs, (staged, sems_in, sems_out, scalars, sems_scalar) = refs[after:-5], refs[-5:]
    me, tile = lax.axis_index("led"), lax.axis_index("tile")
    copies = [
        pltpu.make_async_copy(ref, scalars.at[n], sems_scalar.at[n])
        for n, ref in enumerate((lead, row_off, col_off))
    ]
    start_all(copies)
    wait_all(copies)
    lead, row_off, col_off = scalars.at[0], scalars.at[1], scalars.at[2]
    spans = spans_of(run)
    arriving = []
    for shift in range(leds):
        slot = shift if packed else lax.rem(me + shift, leds)
        for n, (first, rows) in enumerate(spans):
            base = block_base(slot, tile * band + first, me * LANES, band, lead, row_off, col_off)
            for part in range(2):
                line = pl.multiple_of(base + part * band + first, 8)
                arriving.append(
                    pltpu.make_async_copy(
                        spectrum.at[pl.ds(line, rows)],
                        staged.at[shift, part, first - run[0] : first - run[0] + rows],
                        sems_in.at[shift, n, part],
                    )
                )
    start_all(arriving)
    each = len(spans) * 2
    leaving = []
    for shift in range(leds):
        wait_all(arriving[shift * each : (shift + 1) * each])
        target = outs[0].at[shift] if packed else outs[shift]
        leaving.append(pltpu.make_async_copy(staged.at[shift], target, sems_out.at[shift]))
        leaving[-1].start()
    wait_all(leaving)


def prepare_kernel(sizes, lead, row_off, col_off, mask, aberration, intensities, pupil, images, turned):
    leds, tiles, band = sizes
    me, tile = lax.axis_index("led"), lax.axis_index("tile")
    led = lead[me]
    line = lax.broadcasted_iota(jnp.int32, (band, band), 0)
    place = lax.broadcasted_iota(jnp.int32, (band, band), 1)
    residue = 2 * (place // LANES) + (((place // HALF_LANES) & 1) ^ (tile & 1))
    wanted = residue + 4 * (place & (HALF_LANES - 1))
    chosen = (line == wanted).astype(BF16)
    for block in range(M // QUARTER):
        columns = lax.dot_general(
            intensities[:, block * QUARTER : (block + 1) * QUARTER],
            chosen,
            (((0,), (0,)), ((), ())),
            preferred_element_type=F32,
        )
        for side in range(band // LANES):
            turned[side, block * QUARTER : (block + 1) * QUARTER, :] = columns[
                :, side * LANES : (side + 1) * LANES
            ]
    for part in range(4):
        for side in range(band // LANES):
            images[part * QUARTER : (part + 1) * QUARTER, side * LANES : (side + 1) * LANES] = turned[
                side, pl.ds(part, QUARTER, 4), :
            ]
    half = M // 2
    run_p = lax.broadcasted_iota(jnp.int32, (TILE, TILE), 0)
    run_q = lax.broadcasted_iota(jnp.int32, (TILE, TILE), 1)
    tile_rows = band // TILE
    for i in range(tile_rows):
        row_tile = (tile * tile_rows + i - row_off[led]) & (M // TILE - 1)
        coord_p = (run_p + (row_tile * TILE - half)).astype(F32) / half
        for j in range(M // TILE):
            col_tile = (j - col_off[led]) & (M // TILE - 1)
            coord_q = (run_q + (col_tile * TILE - half)).astype(F32) / half
            gate = mask[led, row_tile, col_tile].astype(F32)
            cosine, sine = cos_sin(aberration_phase(aberration, coord_p, coord_q))
            where = (slice(i * TILE, (i + 1) * TILE), slice(j * TILE, (j + 1) * TILE))
            pupil[(0,) + where] = gate * cosine
            pupil[(1,) + where] = gate * sine


def forward_kernel(sizes, run, packed, piece_count, early, table, pupil, *refs):
    leds, tiles, band = sizes
    run_first, rows = run
    pieces, refs = refs[:piece_count], refs[piece_count + early :]
    count = 1 if packed else tiles
    outs, refs = refs[:count], refs[count:]
    table_v, pupil_v, window, result, sems, sems_out = refs
    me, tile = lax.axis_index("led"), lax.axis_index("tile")
    copies = []
    for shift in range(leds):
        if piece_count == 1:
            piece, first = pieces[0].at[shift], shift * LANES
        else:
            piece = pieces[shift]
            first = pl.multiple_of(lax.rem(me - shift + leds, leds) * LANES, LANES)
        copies.append(
            pltpu.make_async_copy(piece, window.at[:, :, pl.ds(first, LANES)], sems.at[shift])
        )
    copies.append(
        pltpu.make_async_copy(pupil.at[:, run_first : run_first + rows], pupil_v, sems.at[leds])
    )
    copies.append(pltpu.make_async_copy(table, table_v, sems.at[leds + 1]))
    start_all(copies)
    wait_all(copies)
    parts = []
    for a in range(4):
        cells = slice(a * QUARTER, (a + 1) * QUARTER)
        gate_re, gate_im = pupil_v[0, :, cells], pupil_v[1, :, cells]
        cell_re, cell_im = window[0, :, cells], window[1, :, cells]
        parts.append((gate_re * cell_re - gate_im * cell_im, gate_re * cell_im + gate_im * cell_re))
    mixed = butterfly(parts, 1)
    lines = [right_product(re, im, table_v[k]) for k, (re, im) in enumerate(mixed)]
    lane = lax.broadcasted_iota(jnp.int32, (rows, LANES), 1)
    for other in range(tiles):
        block = slice((other // 2) * LANES, (other // 2 + 1) * LANES)
        for part in range(2):
            for pair in range(2):
                first, second = lines[2 * pair][part][:, block], lines[2 * pair + 1][part][:, block]
                if other % 2:
                    first, second = second, first
                result[other, part, :, pair * LANES : (pair + 1) * LANES] = jnp.where(
                    lane < HALF_LANES, first, second
                )
    if packed:
        copies = [pltpu.make_async_copy(result, outs[0], sems_out.at[0])]
    else:
        copies = [
            pltpu.make_async_copy(result.at[tile ^ shift], outs[shift], sems_out.at[shift])
            for shift in range(tiles)
        ]
    start_all(copies)
    wait_all(copies)


def tile_views(stack, run, packed, tile, tiles):
    first, rows = run
    cells = slice(first, first + rows)
    if packed:
        return [stack.at[:, :, cells]]
    return [stack.at[tile ^ shift, :, cells] for shift in range(tiles)]


def middle_kernel(sizes, runs_in, runs_out, table, table_back, images, copied, *refs):
    leds, tiles, band = sizes
    tile = lax.axis_index("tile")
    table_v, back_v, images_v, field, residual, sems, sems_out = refs[-7:]
    views = [v for run, packed in runs_in for v in tile_views(field, run, packed, tile, tiles)]
    leaving = [v for run, packed in runs_out for v in tile_views(field, run, packed, tile, tiles)]
    blocks, outs = refs[: len(views)], refs[len(views) : -7]
    count = len(views)
    copies = [pltpu.make_async_copy(b, v, sems.at[n]) for n, (b, v) in enumerate(zip(blocks, views))]
    copies.append(pltpu.make_async_copy(table, table_v, sems.at[count]))
    copies.append(pltpu.make_async_copy(images, images_v, sems.at[count + 1]))
    copies.append(pltpu.make_async_copy(table_back, back_v, sems.at[count + 2]))
    start_all(copies)
    wait_all(copies)
    mixed = butterfly([(field[a, 0], field[a, 1]) for a in range(4)], 1)
    for k, (re, im) in enumerate(mixed):
        wave_re, wave_im = left_product(re, im, table_v[k])
        measured = images_v[k * QUARTER : (k + 1) * QUARTER, :]
        excess = wave_re * wave_re + wave_im * wave_im - measured
        back_re, back_im = left_product(excess * wave_re, excess * wave_im, back_v[k])
        residual[k, 0] = back_re
        residual[k, 1] = back_im
    mixed = butterfly([(residual[k, 0], residual[k, 1]) for k in range(4)], -1)
    for a, (re, im) in enumerate(mixed):
        field[a, 0] = re
        field[a, 1] = im
    copies = [pltpu.make_async_copy(v, o, sems_out.at[n]) for n, (v, o) in enumerate(zip(leaving, outs))]
    start_all(copies)
    wait_all(copies)


def backward_kernel(sizes, run, packed, led_packed, held, table, pupil, *refs):
    leds, tiles, band = sizes
    run_first, rows = run
    count = 1 if packed else tiles
    blocks, refs = refs[:count], refs[count + held :]
    sent = 1 if led_packed else leds
    outs, refs = refs[:sent], refs[sent + held :]
    table_v, pupil_v, lines, result, sems, sems_out = refs
    me, tile = lax.axis_index("led"), lax.axis_index("tile")
    views = tile_views(lines, (0, rows), packed, tile, tiles)
    copies = [pltpu.make_async_copy(b, v, sems.at[n]) for n, (b, v) in enumerate(zip(blocks, views))]
    copies.append(
        pltpu.make_async_copy(pupil.at[:, run_first : run_first + rows], pupil_v, sems.at[tiles])
    )
    copies.append(pltpu.make_async_copy(table, table_v, sems.at[tiles + 1]))
    start_all(copies)
    wait_all(copies)
    lane = lax.broadcasted_iota(jnp.int32, (rows, LANES), 1)
    parts = []
    for k in range(4):
        cells = slice((k // 2) * LANES, (k // 2 + 1) * LANES)
        both = []
        for part in range(2):
            joined = []
            for pair in range(tiles // 2):
                first, second = lines[2 * pair, part, :, cells], lines[2 * pair + 1, part, :, cells]
                if k % 2:
                    first, second = second, first
                joined.append(jnp.where(lane < HALF_LANES, first, second))
            both.append(jnp.concatenate(joined, axis=1))
        parts.append(right_product(both[0], both[1], table_v[k]))
    for a, (re, im) in enumerate(butterfly(parts, -1)):
        cells = slice(a * QUARTER, (a + 1) * QUARTER)
        gate_re, gate_im = pupil_v[0, :, cells], pupil_v[1, :, cells]
        result[0, :, cells] = gate_re * re + gate_im * im
        result[1, :, cells] = gate_re * im - gate_im * re
    copies = []
    for shift in range(leds):
        if led_packed:
            first, target = shift * LANES, outs[0].at[shift]
        else:
            first = pl.multiple_of(lax.rem(me + shift, leds) * LANES, LANES)
            target = outs[shift]
        copies.append(
            pltpu.make_async_copy(result.at[:, :, pl.ds(first, LANES)], target, sems_out.at[shift])
        )
    start_all(copies)
    wait_all(copies)


def update_kernel(sizes, run, lead, row_off, col_off, spectrum, buffer, *refs):
    leds, tiles, band = sizes
    pieces = refs[:-6]
    updated, grads, cells, sems, sems_in, sems_out = refs[-6:]
    me, tile = lax.axis_index("led"), lax.axis_index("tile")
    run_first = run[0]
    arriving = []
    spans = spans_of(run)
    bases = [
        [
            block_base(slot, tile * band + first, me * LANES, band, lead, row_off, col_off)
            for first, rows in spans
        ]
        for slot in range(leds)
    ]

    def lines_at(ref, slot, n, part):
        first, rows = spans[n]
        return ref.at[pl.ds(pl.multiple_of(bases[slot][n] + part * band + first, 8), rows)]

    def cells_at(slot, n, part):
        first, rows = spans[n]
        return cells.at[slot, part, first - run_first : first - run_first + rows]

    every = [(n, part) for n in range(len(spans)) for part in range(2)]
    for slot in range(leds):
        for n, part in every:
            arriving.append(
                pltpu.make_async_copy(
                    lines_at(spectrum, slot, n, part), cells_at(slot, n, part), sems_in.at[slot, n, part]
                )
            )
    for shift in range(leds):
        if len(pieces) == 1:
            arriving.append(pltpu.make_async_copy(pieces[0].at[shift], grads.at[shift], sems.at[shift]))
        else:
            slot = lax.rem(me - shift + leds, leds)
            arriving.append(pltpu.make_async_copy(pieces[shift], grads.at[slot], sems.at[shift]))
    start_all(arriving)
    shared = jnp.bool_(False)
    is_first = []
    for slot in range(leds):
        is_first.append([jnp.bool_(True)] * len(spans))
        for earlier in range(slot):
            for n in range(len(spans)):
                same = bases[earlier][n] == bases[slot][n]
                shared = jnp.logical_or(shared, same)
                is_first[slot][n] = jnp.logical_and(is_first[slot][n], jnp.logical_not(same))
    wait_all(arriving)

    @pl.when(shared)
    def _():
        for n, (first, rows) in enumerate(spans):
            where = slice(first - run_first, first - run_first + rows)
            for slot in range(leds):
                for later in range(slot + 1, leds):

                    @pl.when(jnp.logical_and(is_first[slot][n], bases[later][n] == bases[slot][n]))
                    def _():
                        grads[slot, :, where] = grads[slot, :, where] + grads[later, :, where]

    for waiting in (False, True):
        for slot in range(leds):
            if not waiting:
                cells[slot] = cells[slot] - STEP_SIZE * grads[slot]
            for n in range(len(spans)):

                @pl.when(is_first[slot][n])
                def _():
                    for part in range(2):
                        copy = pltpu.make_async_copy(
                            cells_at(slot, n, part),
                            lines_at(updated, slot, n, part),
                            sems_out.at[slot, n, part],
                        )
                        if waiting:
                            copy.wait()
                        else:
                            copy.start()


COPY_LINES = 2048
COPY_SLOTS = 8


def copy_kernel(first, lines, after, spectrum, *refs):
    copied, staged, sems_in, sems_out = refs[-4:]
    count = lines // COPY_LINES

    def copy_in(n):
        return pltpu.make_async_copy(
            spectrum.at[pl.ds(first + n * COPY_LINES, COPY_LINES)],
            staged.at[n % COPY_SLOTS],
            sems_in.at[n % COPY_SLOTS],
        )

    def copy_out(n):
        return pltpu.make_async_copy(
            staged.at[n % COPY_SLOTS],
            copied.at[pl.ds(first + n * COPY_LINES, COPY_LINES)],
            sems_out.at[n % COPY_SLOTS],
        )

    lag = COPY_SLOTS // 2
    for n in range(count + lag):
        if n < count:
            if n >= COPY_SLOTS:
                copy_out(n - COPY_SLOTS).wait()
            copy_in(n).start()
        if n >= lag:
            copy_in(n - lag).wait()
            copy_out(n - lag).start()
    for n in range(max(count - COPY_SLOTS, 0), count):
        copy_out(n).wait()


def call(kernel, name, ins, outs, scratch, flops=0, moved=0, aliases=None, vmem=36):
    run = pl.pallas_call(
        kernel,
        name=name,
        out_shape=jax.tree.map(lambda o: HBM(o.shape, o.dtype), outs),
        in_specs=[pl.BlockSpec(memory_space=place) for place in ins],
        out_specs=jax.tree.map(lambda _: pl.BlockSpec(memory_space=HBM), outs),
        scratch_shapes=scratch,
        input_output_aliases=aliases or {},
        cost_estimate=pl.CostEstimate(flops=COST * flops, bytes_accessed=COST * moved, transcendentals=0),
        compiler_params=pltpu.CompilerParams(vmem_limit_bytes=vmem * 2**20),
    )

    def pinned(*arrays):
        return run(
            *(
                pltpu.with_memory_space_constraint(x, HBM) if place == HBM else x
                for place, x in zip(ins, arrays)
            )
        )

    return pinned


def own_first(count):
    return [ANY] if count == 1 else [HBM] + [ANY] * (count - 1)


def unit_shards(spectrum, intensities, led_of_slot, row_offset, col_offset, tile_mask, aberration):
    tiles = lax.axis_size("tile")
    leds = lax.axis_size("led")
    band = M // tiles
    sizes = (leds, tiles, band)
    forward_runs = runs_of(band, FORWARD_CUTS)
    backward_runs = runs_of(band, BACKWARD_CUTS)
    forward_packed = FORWARD_TILE
    backward_packed = BACKWARD_TILE
    row_fwd, row_bwd, col_fwd, col_bwd = (jnp.asarray(t) for t in quarter_tables())
    flat = spectrum.reshape(-1, LANES)
    smem, vmem = pltpu.SMEM, pltpu.VMEM
    dma = pltpu.SemaphoreType.DMA
    part = functools.partial

    def f32(*shape):
        return jax.ShapeDtypeStruct(shape, F32)

    def over_led(arrays, packed):
        if packed:
            return [lax.all_to_all(arrays[0], "led", split_axis=0, concat_axis=0, tiled=True)]
        moved = [arrays[0]]
        for shift in range(1, leds):
            moved.append(
                lax.ppermute(arrays[shift], "led", [(i, (i + shift) % leds) for i in range(leds)])
            )
        return moved

    def over_tile(arrays, packed):
        if packed:
            return [lax.all_to_all(arrays[0], "tile", split_axis=0, concat_axis=0, tiled=True)]
        moved = [arrays[0]]
        for shift in range(1, tiles):
            moved.append(lax.ppermute(arrays[shift], "tile", [(i, i ^ shift) for i in range(tiles)]))
        return moved

    def pieces_of(run, packed):
        if packed:
            return [f32(leds, 2, run[1], LANES)]
        return [f32(2, run[1], LANES)] * leds

    def blocks_of(run, packed):
        if packed:
            return [f32(tiles, 2, run[1], band)]
        return [f32(2, run[1], band)] * tiles

    arrived = []
    for number, (run, packed) in enumerate(zip(forward_runs, FORWARD_LED)):
        after = [arrived[0][shift] for shift in SECOND_AFTER] if number else []
        taken = call(
            part(gather_kernel, sizes, run, packed, len(after)), f"gather_{number}",
            [HBM] * 4 + [ANY] * len(after), pieces_of(run, packed),
            [
                pltpu.VMEM((leds, 2, run[1], LANES), F32), dma((leds, len(spans_of(run)), 2)), dma((leds,)),
                pltpu.SMEM((3, leds), jnp.int32), dma((3,)),
            ],
            moved=2**22, vmem=8,
        )(led_of_slot, row_offset, col_offset, flat, *after)
        arrived.append(over_led(taken, packed))
    pupil, images = pl.pallas_call(
        part(prepare_kernel, sizes),
        name="prepare",
        out_shape=[f32(2, band, M), f32(M, band)],
        in_specs=[pl.BlockSpec(memory_space=smem)] * 5 + [pl.BlockSpec(memory_space=vmem)],
        out_specs=[pl.BlockSpec(memory_space=vmem)] * 2,
        scratch_shapes=[pltpu.VMEM((band // LANES, M, LANES), F32)],
        compiler_params=pltpu.CompilerParams(vmem_limit_bytes=16 * 2**20),
        cost_estimate=pl.CostEstimate(flops=2 * 10**9, bytes_accessed=4 * 10**6, transcendentals=0),
    )(led_of_slot, row_offset, col_offset, tile_mask, aberration, intensities[0])
    def copy_half(number, after, so_far):
        lines = flat.shape[0] // 2
        return call(
            part(copy_kernel, number * lines, lines), f"copy_{number}",
            [HBM] * (2 + len(so_far)), f32(*flat.shape),
            [pltpu.VMEM((COPY_SLOTS, COPY_LINES, LANES), F32), dma((COPY_SLOTS,)), dma((COPY_SLOTS,))],
            moved=4 * flat.size, aliases={2: 0} if so_far else None, vmem=16,
        )(after, flat, *so_far)

    table_shape = (4, 4 * QUARTER, QUARTER)
    received, copied = [], None
    for number, (run, packed, pieces) in enumerate(zip(forward_runs, forward_packed, arrived)):
        rows = run[1]
        early = ([copied] if COPY_FIRST else lines[:1]) if number else []
        if number == 0:
            early = [arrived[1][shift] for shift in EARLY]
        pieces_count = len(pieces)
        lines = call(
            part(forward_kernel, sizes, run, packed, pieces_count, len(early)), f"forward_{run[0]}", [HBM, ANY] + own_first(pieces_count) + [HBM] * len(early),
            blocks_of(run, packed),
            [
                pltpu.VMEM(table_shape, BF16), pltpu.VMEM((2, rows, M), F32),
                pltpu.VMEM((2, rows, M), F32), pltpu.VMEM((tiles, 2, rows, band), F32),
                dma((leds + 2,)), dma((tiles,)),
            ],
            flops=24 * rows * M * QUARTER, moved=2**23, vmem=ROW_VMEM,
        )(row_fwd, pupil, *pieces, *early)
        received += over_tile(lines, packed)
        if number == (0 if COPY_FIRST else 1):
            copied = copy_half(0, lines[0], [])

    arrays_in, arrays_out = len(received), sum(1 if p else tiles for p in backward_packed)
    returned = call(
        part(middle_kernel, sizes, list(zip(forward_runs, forward_packed)), list(zip(backward_runs, backward_packed))),
        "middle", [HBM] * 2 + [ANY, HBM] + [HBM] * arrays_in,
        [b for run, packed in zip(backward_runs, backward_packed) for b in blocks_of(run, packed)],
        [
            pltpu.VMEM((4, QUARTER, 4 * QUARTER), BF16), pltpu.VMEM((4, QUARTER, 4 * QUARTER), BF16),
            pltpu.VMEM((M, band), F32), pltpu.VMEM((4, 2, QUARTER, band), F32),
            pltpu.VMEM((4, 2, QUARTER, band), F32), dma((arrays_in + 3,)), dma((arrays_out,)),
        ],
        flops=48 * band * M * QUARTER, moved=2**24, vmem=MIDDLE_VMEM,
    )(col_fwd, col_bwd, images, copied, *received)
    updated = copy_half(1, returned[0], [copied])
    count = 1 if backward_packed[0] else tiles
    returned, later = returned[:count], returned[count:]
    for number, (run, packed, led_packed) in enumerate(zip(backward_runs, backward_packed, BACKWARD_LED)):
        rows = run[1]
        sent = 1 if led_packed else leds
        lines = over_tile(returned if number == 0 else later, packed)
        held, through = (list(later), [updated]) if number == 0 else ([], [])
        count = len(lines)
        results = call(
            part(backward_kernel, sizes, run, packed, led_packed, len(held + through)), f"backward_{run[0]}",
            [HBM, ANY] + own_first(count) + [ANY] * len(held) + [HBM] * len(through),
            pieces_of(run, led_packed) + [f32(*h.shape) for h in held + through],
            [
                pltpu.VMEM(table_shape, BF16), pltpu.VMEM((2, rows, M), F32),
                pltpu.VMEM((tiles, 2, rows, band), F32), pltpu.VMEM((2, rows, M), F32),
                dma((tiles + 2,)), dma((leds,)),
            ],
            flops=24 * rows * M * QUARTER, moved=2**23, vmem=ROW_VMEM,
            aliases={2 + count + n: sent + n for n in range(len(held + through))},
        )(row_bwd, pupil, *lines, *held, *through)
        pieces, later = over_led(results[:sent], led_packed), results[sent : sent + len(held)]
        updated = results[-1] if through else updated
        spans = len(spans_of(run))
        updated = call(
            part(update_kernel, sizes, run), f"update_{run[0]}", [smem] * 3 + [HBM] * 2 + own_first(sent),
            f32(*flat.shape),
            [
                pltpu.VMEM((leds, 2, rows, LANES), F32), pltpu.VMEM((leds, 2, rows, LANES), F32),
                dma((leds,)), dma((leds, spans, 2)), dma((leds, spans, 2)),
            ],
            moved=2**22, aliases={4: 0}, vmem=16,
        )(led_of_slot, row_offset, col_offset, flat, updated, *pieces)
    return updated.reshape(spectrum.shape)


def solution(mesh):
    placed = (P(None, None, "tile", "led", None), P("led", "tile", None), P(), P(), P(), P(), P())
    whole_units = mesh.shape["tile"] == 4 and M // mesh.shape["led"] == LANES
    return jax.shard_map(
        unit_shards if whole_units else general_shards,
        mesh=mesh,
        in_specs=placed,
        out_specs=P(None, None, "tile", "led", None),
        check_vma=False,
    )
```

```python
import functools
import math

import jax
import jax.numpy as jnp
import numpy as np
from jax import lax
from jax.experimental import pallas as pl
from jax.experimental.pallas import tpu as pltpu
from jax.sharding import PartitionSpec as P

M = 1024
TILE = 128
GR = 16
GC = 8
L_DEV = 1


STEP_SIZE = 0.25
HIGHEST_MODE = lax.Precision.HIGHEST


def aberration_phase(aberration, coord_p, coord_q):
    radial = coord_p * coord_p + coord_q * coord_q
    return (
        aberration[0] * (2.0 * radial - 1.0)
        + aberration[1] * (coord_p * coord_p - coord_q * coord_q)
        + aberration[2] * (2.0 * coord_p * coord_q)
        + aberration[3] * ((3.0 * radial - 2.0) * coord_p)
        + aberration[4] * ((3.0 * radial - 2.0) * coord_q)
    )


def dft_table(length):
    index_run = jnp.arange(length, dtype=jnp.int32)
    column_run = jnp.arange(2 * length, dtype=jnp.int32)
    product_mod = index_run[:, None] * (column_run % length)[None, :] % length
    shifted = (column_run >= length).astype(jnp.float32) * (0.5 * math.pi)
    angles = product_mod.astype(jnp.float32) * (2.0 * math.pi / length) - shifted[None, :]
    return jnp.cos(angles)


def small_tables(rows_len, cols_len, modulus, sign):
    first_run = jnp.arange(rows_len, dtype=jnp.int32)
    second_run = jnp.arange(cols_len, dtype=jnp.int32)
    product_mod = first_run[:, None] * second_run[None, :] % modulus
    angles = product_mod.astype(jnp.float32) * (2.0 * math.pi / modulus)
    return (jnp.cos(angles), sign * jnp.sin(angles))


def factor_dft(real_part, imag_part, sign):
    length = real_part.shape[-1]
    first = 1 << (length.bit_length() - 1) // 2
    second = length // first
    leading = real_part.shape[:-1]
    cos_first, sin_first = small_tables(first, first, first, sign)
    cos_second, sin_second = small_tables(second, second, second, sign)
    twid_cos, twid_sin = small_tables(first, second, length, sign)
    flat_re = real_part.reshape(-1, first, second)
    flat_im = imag_part.reshape(-1, first, second)

    def section_one(data, table):
        return jnp.einsum("rab,ak->rkb", data, table, precision=HIGHEST_MODE)

    def section_two(data, table):
        return jnp.einsum("rkb,bl->rlk", data, table, precision=HIGHEST_MODE)

    mid_re = section_one(flat_re, cos_first) - section_one(flat_im, sin_first)
    mid_im = section_one(flat_im, cos_first) + section_one(flat_re, sin_first)
    turned_re = mid_re * twid_cos[None] - mid_im * twid_sin[None]
    turned_im = mid_re * twid_sin[None] + mid_im * twid_cos[None]
    out_re = section_two(turned_re, cos_second) - section_two(turned_im, sin_second)
    out_im = section_two(turned_im, cos_second) + section_two(turned_re, sin_second)
    return (out_re.reshape(leading + (length,)), out_im.reshape(leading + (length,)))


def times_table(operand, transform):
    return jnp.dot(operand, transform, precision=HIGHEST_MODE, preferred_element_type=jnp.float32)


def pupil_parts(aberration, tile_gate, row_window, col_window):
    halfway = M // 2
    coord_p = ((row_window - halfway).astype(jnp.float32) / halfway)[:, None]
    coord_q = ((col_window - halfway).astype(jnp.float32) / halfway)[None, :]
    phase_map = aberration_phase(aberration, coord_p, coord_q)
    tiles_side = tile_gate.shape[0]
    tile_ids = jnp.arange(tiles_side, dtype=jnp.int32)
    pick_rows = ((row_window // TILE)[:, None] == tile_ids[None, :]).astype(jnp.float32)
    pick_cols = (tile_ids[:, None] == (col_window // TILE)[None, :]).astype(jnp.float32)
    gate_map = times_table(times_table(pick_rows, tile_gate.astype(jnp.float32)), pick_cols)
    return (gate_map * jnp.cos(phase_map), gate_map * jnp.sin(phase_map))


def stack_blocks(real_part, imag_part, tile_count, band_rows):
    slots_now = real_part.shape[0]
    rows_now = real_part.shape[1]
    stacked = jnp.stack(
        [
            real_part.reshape(slots_now, rows_now, tile_count, band_rows),
            imag_part.reshape(slots_now, rows_now, tile_count, band_rows),
        ],
        axis=3,
    )
    return stacked.reshape(slots_now, rows_now, tile_count, 2 * band_rows)


def finish_rows(rows_back, pupil_re, pupil_im, row_first, row_count, led_count, unit_cols):
    image_side = rows_back.shape[0]
    part_re = jnp.transpose(rows_back[:, 0, row_first : row_first + row_count])
    part_im = jnp.transpose(rows_back[:, 1, row_first : row_first + row_count])
    grad_re, grad_im = factor_dft(part_re, part_im, -1.0)
    grad_re = grad_re / image_side
    grad_im = grad_im / image_side
    out_re = pupil_re * grad_re + pupil_im * grad_im
    out_im = pupil_re * grad_im - pupil_im * grad_re
    stacked = jnp.stack([out_re, out_im]).reshape(2, row_count, led_count, unit_cols)
    return jnp.transpose(stacked, (2, 0, 1, 3)).reshape(led_count, 2 * row_count * unit_cols)


def general_shards(spectrum, intensities, led_of_slot, row_offset, col_offset, tile_mask, aberration):
    tile_count = lax.axis_size("tile")
    led_count = lax.axis_size("led")
    band_rows = M // tile_count
    unit_cols = M // led_count
    piece_cells = band_rows * unit_cols
    led_here = lax.axis_index("led")
    tile_here = lax.axis_index("tile")
    transform = dft_table(M)
    row_start = row_offset[led_of_slot] * TILE
    col_start = col_offset[led_of_slot] * TILE
    row_pos = tile_here * band_rows + jnp.arange(band_rows, dtype=jnp.int32)
    first_col_here = led_here * unit_cols
    row_group = (row_start[:, None] + (row_pos[None, :] - row_start[:, None]) % M) // M
    col_group = (col_start + (first_col_here - col_start) % M) // M
    row_group = row_group.reshape(led_count, L_DEV, band_rows)
    col_group = col_group.reshape(led_count, L_DEV, 1)
    line_ids = (
        (row_group * GC + col_group) * band_rows
        + jnp.arange(band_rows, dtype=jnp.int32)[None, None, :]
    ).reshape(-1)
    local_lines = jnp.transpose(
        spectrum.reshape(GR, GC, 2, band_rows, unit_cols), (0, 1, 3, 2, 4)
    ).reshape(GR * GC * band_rows, 2 * unit_cols)
    taken = local_lines[line_ids].reshape(led_count, L_DEV, band_rows, 2, unit_cols)
    outgoing = jnp.transpose(taken, (0, 1, 3, 2, 4)).reshape(led_count, L_DEV, 2 * piece_cells)
    incoming = lax.all_to_all(outgoing, "led", split_axis=0, concat_axis=0, tiled=True)
    col_all = jnp.arange(M, dtype=jnp.int32)
    slot_index = led_here * L_DEV + 0
    led_index = led_of_slot[slot_index]
    first_row = row_offset[led_index] * TILE
    first_col = col_offset[led_index] * TILE
    pupil_re, pupil_im = pupil_parts(
        aberration, tile_mask[led_index], (row_pos - first_row) % M, (col_all - first_col) % M
    )
    window = incoming[:, 0].reshape(led_count, 2, band_rows, unit_cols)
    window = jnp.transpose(window, (1, 2, 0, 3)).reshape(2, band_rows, M)
    field_re = pupil_re * window[0] - pupil_im * window[1]
    field_im = pupil_re * window[1] + pupil_im * window[0]
    fields = [jnp.stack([field_re, field_im])]
    pupils = (pupil_re, pupil_im)
    stacked_fields = jnp.stack(fields).reshape(L_DEV * 2 * band_rows, M)
    mixed = times_table(stacked_fields, transform).reshape(L_DEV, 2, band_rows, 2 * M)
    along_re = mixed[:, 0, :, :M] - mixed[:, 1, :, M:]
    along_im = mixed[:, 0, :, M:] + mixed[:, 1, :, :M]
    outbound = stack_blocks(along_re, along_im, tile_count, band_rows)
    columns = lax.all_to_all(outbound, "tile", split_axis=2, concat_axis=1, tiled=True).reshape(
        L_DEV, M, 2 * band_rows
    )
    flipped = jnp.swapaxes(columns, 1, 2)
    wave_re, wave_im = factor_dft(flipped[:, :band_rows], flipped[:, band_rows:], 1.0)
    wave_re = wave_re / M
    wave_im = wave_im / M
    measured = intensities.astype(jnp.float32)
    excess = wave_re * wave_re + wave_im * wave_im - measured
    back_re, back_im = factor_dft(excess * wave_re, excess * wave_im, -1.0)
    inbound = stack_blocks(back_re, back_im, tile_count, band_rows)
    rows_back = lax.all_to_all(inbound, "tile", split_axis=2, concat_axis=1, tiled=True).reshape(
        L_DEV, M, 2, band_rows
    )
    outgoing_all = jnp.stack(
        [finish_rows(rows_back[0], pupils[0], pupils[1], 0, band_rows, led_count, unit_cols)],
        axis=1,
    )
    received = lax.all_to_all(outgoing_all, "led", split_axis=0, concat_axis=0, tiled=True)
    grad_lines = jnp.transpose(
        received.reshape(led_count, L_DEV, 2, band_rows, unit_cols), (0, 1, 3, 2, 4)
    ).reshape(led_count * L_DEV * band_rows, 2 * unit_cols)
    grad_sum = jax.ops.segment_sum(grad_lines, line_ids, num_segments=GR * GC * band_rows)
    grad_sum = jnp.transpose(grad_sum.reshape(GR, GC, band_rows, 2, unit_cols), (0, 1, 3, 2, 4))
    updated = spectrum - STEP_SIZE * grad_sum.reshape(spectrum.shape)
    return updated


QUARTER = M // 4
HALF_LANES = 64
LANES = 128
SUB = 128
FORWARD_CUTS = (5, 3)
FORWARD_LED = (False, False)
BACKWARD_LED = (True, False)
FORWARD_TILE = (True, False)
BACKWARD_TILE = (False, False)
BACKWARD_CUTS = (4, 4)
MIDDLE_VMEM = 20
ROW_VMEM = 14
ANY = pl.ANY
HBM = pltpu.HBM
TABLES = HBM
COPY_AFTER = 2
FREE_MIDDLE = FREE_BACKWARD = True
F32 = jnp.float32
BF16 = jnp.bfloat16


def split_table(values):
    high = values.astype(np.float32).astype(jnp.bfloat16)
    low = (values - high.astype(np.float64)).astype(np.float32).astype(jnp.bfloat16)
    return high, low


def quarter_tables():
    grid_b = np.arange(QUARTER)[:, None]
    grid_k = np.arange(QUARTER)[None, :]
    swapped = grid_k ^ HALF_LANES
    row_fwd, row_bwd, col_fwd, col_bwd = [], [], [], []
    for step in range(4):
        lanes = swapped if step % 2 else grid_k
        angle = 2.0 * math.pi * (grid_b * (step + 4 * lanes) % M) / M
        cos, sin = np.cos(angle) / 32.0, np.sin(angle) / 32.0
        for stacked, out in (
            (np.concatenate([cos, sin], 0), row_fwd),
            (np.concatenate([cos.T, -sin.T], 0), row_bwd),
        ):
            high, low = split_table(stacked)
            out.append(np.concatenate([high, low], 0))
        angle = 2.0 * math.pi * (grid_b * (step + 4 * grid_k) % M) / M
        cos, sin = np.cos(angle) / 32.0, np.sin(angle) / 32.0
        for stacked, out in (
            (np.concatenate([cos.T, sin.T], 1), col_fwd),
            (np.concatenate([cos, -sin], 1), col_bwd),
        ):
            high, low = split_table(stacked)
            out.append(np.concatenate([high, low], 1))
    return [np.stack(t) for t in (row_fwd, row_bwd, col_fwd, col_bwd)]


def halves(x):
    high = x.astype(BF16)
    low = (x - high.astype(F32)).astype(BF16)
    return high, low


def right_product(re, im, table):
    re_high, re_low = halves(re)
    im_high, im_low = halves(im)
    table = jnp.concatenate([table[: 2 * QUARTER], table], axis=0)
    top = jnp.concatenate([re_high, -im_high, re_low, -im_low, re_high, -im_high], axis=1)
    bottom = jnp.concatenate([im_high, re_high, im_low, re_low, im_high, re_high], axis=1)
    return (
        jnp.dot(top, table, preferred_element_type=F32),
        jnp.dot(bottom, table, preferred_element_type=F32),
    )


def left_product(re, im, table):
    re_high, re_low = halves(re)
    im_high, im_low = halves(im)
    table = jnp.concatenate([table[:, : 2 * QUARTER], table], axis=1)
    left = jnp.concatenate([re_high, -im_high, re_low, -im_low, re_high, -im_high], axis=0)
    right = jnp.concatenate([im_high, re_high, im_low, re_low, im_high, re_high], axis=0)
    return (
        jnp.dot(table, left, preferred_element_type=F32),
        jnp.dot(table, right, preferred_element_type=F32),
    )


def butterfly(parts, sign):
    (r0, i0), (r1, i1), (r2, i2), (r3, i3) = parts
    sr, si, dr, di = r0 + r2, i0 + i2, r0 - r2, i0 - i2
    tr, ti, er, ei = r1 + r3, i1 + i3, r1 - r3, i1 - i3
    if sign > 0:
        return ((sr + tr, si + ti), (dr - ei, di + er), (sr - tr, si - ti), (dr + ei, di - er))
    return ((sr + tr, si + ti), (dr + ei, di - er), (sr - tr, si - ti), (dr - ei, di + er))


def cos_sin(angle):
    turns = jnp.floor(angle * (2.0 / math.pi) + 0.5)
    rest = ((angle - turns * 1.5703125) - turns * 4.837512969970703125e-4) - turns * 7.549789948768648e-8
    square = rest * rest
    sine = rest + rest * square * (
        -1.6666654611e-1 + square * (8.3321608736e-3 - square * 1.9515295891e-4)
    )
    cosine = 1.0 - 0.5 * square + square * square * (
        4.166664568298827e-2 + square * (-1.388731625493765e-3 + square * 2.443315711809948e-5)
    )
    quarter = turns.astype(jnp.int32) & 3
    odd = (quarter & 1) == 1
    cos_out = jnp.where(odd, sine, cosine)
    sin_out = jnp.where(odd, cosine, sine)
    cos_out = jnp.where((quarter == 1) | (quarter == 2), -cos_out, cos_out)
    sin_out = jnp.where(quarter >= 2, -sin_out, sin_out)
    return cos_out, sin_out


def runs_of(band, cuts):
    unit = band // sum(cuts)
    runs, first = [], 0
    for cut in cuts:
        runs.append((first, cut * unit))
        first += cut * unit
    return runs


def spans_of(run):
    first, rows = run
    spans, last = [], first + rows
    while first < last:
        end = min(last, (first // TILE + 1) * TILE)
        spans.append((first, end - first))
        first = end
    return spans


def block_base(slot, row_first, col_first, band, lead, row_off, col_off):
    led = lead[slot]
    row_start = row_off[led] * TILE
    col_start = col_off[led] * TILE
    row_group = (row_start + ((row_first - row_start) & (M - 1))) // M
    col_group = (col_start + ((col_first - col_start) & (M - 1))) // M
    return (row_group * GC + col_group) * (2 * band)


def start_all(copies):
    for copy in copies:
        copy.start()


def wait_all(copies):
    for copy in copies:
        copy.wait()


def gather_kernel(sizes, run, packed, lead, row_off, col_off, spectrum, *refs):
    leds, tiles, band = sizes
    outs, (staged, sems_in, sems_out, scalars, sems_scalar) = refs[:-5], refs[-5:]
    me, tile = lax.axis_index("led"), lax.axis_index("tile")
    copies = [
        pltpu.make_async_copy(ref, scalars.at[n], sems_scalar.at[n])
        for n, ref in enumerate((lead, row_off, col_off))
    ]
    start_all(copies)
    wait_all(copies)
    lead, row_off, col_off = scalars.at[0], scalars.at[1], scalars.at[2]
    spans = spans_of(run)
    arriving = []
    for shift in range(leds):
        slot = shift if packed else lax.rem(me + shift, leds)
        for n, (first, rows) in enumerate(spans):
            base = block_base(slot, tile * band + first, me * LANES, band, lead, row_off, col_off)
            for part in range(2):
                line = pl.multiple_of(base + part * band + first, 8)
                arriving.append(
                    pltpu.make_async_copy(
                        spectrum.at[pl.ds(line, rows)],
                        staged.at[shift, part, first - run[0] : first - run[0] + rows],
                        sems_in.at[shift, n, part],
                    )
                )
    start_all(arriving)
    each = len(spans) * 2
    leaving = []
    for shift in range(leds):
        wait_all(arriving[shift * each : (shift + 1) * each])
        target = outs[0].at[shift] if packed else outs[shift]
        leaving.append(pltpu.make_async_copy(staged.at[shift], target, sems_out.at[shift]))
        leaving[-1].start()
    wait_all(leaving)


def prepare_kernel(sizes, lead, row_off, col_off, mask, aberration, intensities, pupil, images, turned):
    leds, tiles, band = sizes
    me, tile = lax.axis_index("led"), lax.axis_index("tile")
    led = lead[me]
    line = lax.broadcasted_iota(jnp.int32, (band, band), 0)
    place = lax.broadcasted_iota(jnp.int32, (band, band), 1)
    residue = 2 * (place // LANES) + (((place // HALF_LANES) & 1) ^ (tile & 1))
    wanted = residue + 4 * (place & (HALF_LANES - 1))
    chosen = (line == wanted).astype(BF16)
    for block in range(M // QUARTER):
        columns = lax.dot_general(
            intensities[:, block * QUARTER : (block + 1) * QUARTER],
            chosen,
            (((0,), (0,)), ((), ())),
            preferred_element_type=F32,
        )
        for side in range(band // LANES):
            turned[side, block * QUARTER : (block + 1) * QUARTER, :] = columns[
                :, side * LANES : (side + 1) * LANES
            ]
    for part in range(4):
        for side in range(band // LANES):
            images[part * QUARTER : (part + 1) * QUARTER, side * LANES : (side + 1) * LANES] = turned[
                side, pl.ds(part, QUARTER, 4), :
            ]
    half = M // 2
    run_p = lax.broadcasted_iota(jnp.int32, (TILE, TILE), 0)
    run_q = lax.broadcasted_iota(jnp.int32, (TILE, TILE), 1)
    tile_rows = band // TILE
    for i in range(tile_rows):
        row_tile = (tile * tile_rows + i - row_off[led]) & (M // TILE - 1)
        coord_p = (run_p + (row_tile * TILE - half)).astype(F32) / half
        for j in range(M // TILE):
            col_tile = (j - col_off[led]) & (M // TILE - 1)
            coord_q = (run_q + (col_tile * TILE - half)).astype(F32) / half
            gate = mask[led, row_tile, col_tile].astype(F32)
            cosine, sine = cos_sin(aberration_phase(aberration, coord_p, coord_q))
            where = (slice(i * TILE, (i + 1) * TILE), slice(j * TILE, (j + 1) * TILE))
            pupil[(0,) + where] = gate * cosine
            pupil[(1,) + where] = gate * sine


def forward_kernel(sizes, run, packed, piece_count, early, table, pupil, *refs):
    leds, tiles, band = sizes
    run_first, rows = run
    pieces, refs = refs[:piece_count], refs[piece_count + early :]
    count = 1 if packed else tiles
    outs, refs = refs[:count], refs[count:]
    table_v, pupil_v, window, result, sems, sems_out = refs
    me, tile = lax.axis_index("led"), lax.axis_index("tile")
    copies = []
    for shift in range(leds):
        if piece_count == 1:
            piece, first = pieces[0].at[shift], shift * LANES
        else:
            piece = pieces[shift]
            first = pl.multiple_of(lax.rem(me - shift + leds, leds) * LANES, LANES)
        copies.append(
            pltpu.make_async_copy(piece, window.at[:, :, pl.ds(first, LANES)], sems.at[shift])
        )
    copies.append(
        pltpu.make_async_copy(pupil.at[:, run_first : run_first + rows], pupil_v, sems.at[leds])
    )
    tables = [pltpu.make_async_copy(table.at[k], table_v.at[k], sems.at[leds + 1 + k]) for k in range(4)]
    start_all(copies + tables)
    wait_all(copies)
    parts = []
    for a in range(4):
        cells = slice(a * QUARTER, (a + 1) * QUARTER)
        gate_re, gate_im = pupil_v[0, :, cells], pupil_v[1, :, cells]
        cell_re, cell_im = window[0, :, cells], window[1, :, cells]
        parts.append((gate_re * cell_re - gate_im * cell_im, gate_re * cell_im + gate_im * cell_re))
    mixed = butterfly(parts, 1)
    lane = lax.broadcasted_iota(jnp.int32, (rows, LANES), 1)
    lines, leaving = [], []
    for k in range(4):
        tables[k].wait()
        lines.append(right_product(*mixed[k], table_v[k]))
        if k % 2 == 0:
            continue
        places = slice((k // 2) * LANES, (k // 2 + 1) * LANES)
        for other in range(tiles):
            block = slice((other // 2) * LANES, (other // 2 + 1) * LANES)
            for part in range(2):
                first, second = lines[k - 1][part][:, block], lines[k][part][:, block]
                if other % 2:
                    first, second = second, first
                result[other, part, :, places] = jnp.where(lane < HALF_LANES, first, second)
        for shift in range(tiles):
            if packed:
                source, target = result.at[shift], outs[0].at[shift]
            else:
                source, target = result.at[tile ^ shift], outs[shift]
            leaving.append(
                pltpu.make_async_copy(
                    source.at[:, :, places], target.at[:, :, places], sems_out.at[shift, k // 2]
                )
            )
            leaving[-1].start()
    wait_all(leaving)


def tile_views(stack, run, packed, tile, tiles):
    first, rows = run
    cells = slice(first, first + rows)
    if packed:
        return [stack.at[:, :, cells]]
    return [stack.at[tile ^ shift, :, cells] for shift in range(tiles)]


def middle_kernel(sizes, runs_in, runs_out, table, table_back, images, copied, *refs):
    leds, tiles, band = sizes
    tile = lax.axis_index("tile")
    table_v, back_v, images_v, field, residual, sems, sems_out = refs[-7:]
    views = [v for run, packed in runs_in for v in tile_views(field, run, packed, tile, tiles)]
    leaving = [v for run, packed in runs_out for v in tile_views(field, run, packed, tile, tiles)]
    blocks, outs = refs[: len(views)], refs[len(views) : -7]
    count = len(views)
    copies = [pltpu.make_async_copy(b, v, sems.at[n]) for n, (b, v) in enumerate(zip(blocks, views))]
    later = [
        [
            pltpu.make_async_copy(table.at[k], table_v.at[k], sems.at[count + k]),
            pltpu.make_async_copy(
                images.at[k * QUARTER : (k + 1) * QUARTER],
                images_v.at[k * QUARTER : (k + 1) * QUARTER],
                sems.at[count + 4 + k],
            ),
            pltpu.make_async_copy(table_back.at[k], back_v.at[k], sems.at[count + 8 + k]),
        ]
        for k in range(4)
    ]
    start_all(copies)
    for group in later:
        start_all(group)
    wait_all(copies)
    mixed = butterfly([(field[a, 0], field[a, 1]) for a in range(4)], 1)
    for k, (re, im) in enumerate(mixed):
        wait_all(later[k])
        wave_re, wave_im = left_product(re, im, table_v[k])
        measured = images_v[k * QUARTER : (k + 1) * QUARTER, :]
        excess = wave_re * wave_re + wave_im * wave_im - measured
        back_re, back_im = left_product(excess * wave_re, excess * wave_im, back_v[k])
        residual[k, 0] = back_re
        residual[k, 1] = back_im
    mixed = butterfly([(residual[k, 0], residual[k, 1]) for k in range(4)], -1)
    for a, (re, im) in enumerate(mixed):
        field[a, 0] = re
        field[a, 1] = im
    copies = [pltpu.make_async_copy(v, o, sems_out.at[n]) for n, (v, o) in enumerate(zip(leaving, outs))]
    start_all(copies)
    wait_all(copies)


def backward_kernel(sizes, run, packed, led_packed, held, table, pupil, *refs):
    leds, tiles, band = sizes
    run_first, rows = run
    count = 1 if packed else tiles
    blocks, refs = refs[:count], refs[count + held :]
    sent = 1 if led_packed else leds
    outs, refs = refs[:sent], refs[sent + held :]
    table_v, pupil_v, lines, result, sems, sems_out = refs
    me, tile = lax.axis_index("led"), lax.axis_index("tile")
    views = tile_views(lines, (0, rows), packed, tile, tiles)
    copies = [pltpu.make_async_copy(b, v, sems.at[n]) for n, (b, v) in enumerate(zip(blocks, views))]
    gate = pltpu.make_async_copy(pupil.at[:, run_first : run_first + rows], pupil_v, sems.at[tiles])
    tables = [pltpu.make_async_copy(table.at[k], table_v.at[k], sems.at[tiles + 1 + k]) for k in range(4)]
    start_all(copies + tables + [gate])
    wait_all(copies)
    lane = lax.broadcasted_iota(jnp.int32, (rows, LANES), 1)
    parts = []
    for k in range(4):
        cells = slice((k // 2) * LANES, (k // 2 + 1) * LANES)
        both = []
        for part in range(2):
            joined = []
            for pair in range(tiles // 2):
                first, second = lines[2 * pair, part, :, cells], lines[2 * pair + 1, part, :, cells]
                if k % 2:
                    first, second = second, first
                joined.append(jnp.where(lane < HALF_LANES, first, second))
            both.append(jnp.concatenate(joined, axis=1))
        tables[k].wait()
        parts.append(right_product(both[0], both[1], table_v[k]))
    gate.wait()
    copies = []
    for a, (re, im) in enumerate(butterfly(parts, -1)):
        cells = slice(a * QUARTER, (a + 1) * QUARTER)
        gate_re, gate_im = pupil_v[0, :, cells], pupil_v[1, :, cells]
        result[0, :, cells] = gate_re * re + gate_im * im
        result[1, :, cells] = gate_re * im - gate_im * re
        if led_packed:
            for led in range(2 * a, 2 * a + 2):
                copies.append(
                    pltpu.make_async_copy(
                        result.at[:, :, led * LANES : (led + 1) * LANES], outs[0].at[led], sems_out.at[led]
                    )
                )
                copies[-1].start()
    if not led_packed:
        for shift in range(leds):
            first = pl.multiple_of(lax.rem(me + shift, leds) * LANES, LANES)
            copies.append(
                pltpu.make_async_copy(
                    result.at[:, :, pl.ds(first, LANES)], outs[shift], sems_out.at[shift]
                )
            )
        start_all(copies)
    wait_all(copies)


def update_kernel(sizes, run, lead, row_off, col_off, spectrum, buffer, *refs):
    leds, tiles, band = sizes
    pieces = refs[:-6]
    updated, grads, cells, sems, sems_in, sems_out = refs[-6:]
    me, tile = lax.axis_index("led"), lax.axis_index("tile")
    run_first = run[0]
    arriving = []
    spans = spans_of(run)
    bases = [
        [
            block_base(slot, tile * band + first, me * LANES, band, lead, row_off, col_off)
            for first, rows in spans
        ]
        for slot in range(leds)
    ]

    def lines_at(ref, slot, n, part):
        first, rows = spans[n]
        return ref.at[pl.ds(pl.multiple_of(bases[slot][n] + part * band + first, 8), rows)]

    def cells_at(slot, n, part):
        first, rows = spans[n]
        return cells.at[slot, part, first - run_first : first - run_first + rows]

    every = [(n, part) for n in range(len(spans)) for part in range(2)]
    for slot in range(leds):
        for n, part in every:
            arriving.append(
                pltpu.make_async_copy(
                    lines_at(spectrum, slot, n, part), cells_at(slot, n, part), sems_in.at[slot, n, part]
                )
            )
    grads_arriving = []
    for slot in range(leds):
        if len(pieces) == 1:
            piece, place = pieces[0].at[slot], slot
        else:
            piece, place = pieces[slot], lax.rem(me - slot + leds, leds)
        grads_arriving.append(pltpu.make_async_copy(piece, grads.at[place], sems.at[place]))
    start_all(arriving)
    start_all(grads_arriving)
    shared = jnp.bool_(False)
    is_first = []
    for slot in range(leds):
        is_first.append([jnp.bool_(True)] * len(spans))
        for earlier in range(slot):
            for n in range(len(spans)):
                same = bases[earlier][n] == bases[slot][n]
                shared = jnp.logical_or(shared, same)
                is_first[slot][n] = jnp.logical_and(is_first[slot][n], jnp.logical_not(same))
    each = len(every)

    @pl.when(shared)
    def _():
        wait_all(arriving)
        wait_all(grads_arriving)
        for n, (first, rows) in enumerate(spans):
            where = slice(first - run_first, first - run_first + rows)
            for slot in range(leds):
                for later in range(slot + 1, leds):

                    @pl.when(jnp.logical_and(is_first[slot][n], bases[later][n] == bases[slot][n]))
                    def _():
                        grads[slot, :, where] = grads[slot, :, where] + grads[later, :, where]

    for waiting in (False, True):
        for slot in range(leds):
            if not waiting:

                @pl.when(jnp.logical_not(shared))
                def _():
                    wait_all(arriving[slot * each : (slot + 1) * each])
                    source = pieces[0].at[slot] if len(pieces) == 1 else pieces[0]
                    pltpu.make_async_copy(source, grads.at[slot], sems.at[slot]).wait()

                cells[slot] = cells[slot] - STEP_SIZE * grads[slot]
            for n in range(len(spans)):

                @pl.when(is_first[slot][n])
                def _():
                    for part in range(2):
                        copy = pltpu.make_async_copy(
                            cells_at(slot, n, part),
                            lines_at(updated, slot, n, part),
                            sems_out.at[slot, n, part],
                        )
                        if waiting:
                            copy.wait()
                        else:
                            copy.start()


COPY_LINES = 2048
COPY_SLOTS = 8


def copy_kernel(first, lines, after, spectrum, *refs):
    copied, staged, sems_in, sems_out = refs[-4:]
    count = lines // COPY_LINES

    def copy_in(n):
        return pltpu.make_async_copy(
            spectrum.at[pl.ds(first + n * COPY_LINES, COPY_LINES)],
            staged.at[n % COPY_SLOTS],
            sems_in.at[n % COPY_SLOTS],
        )

    def copy_out(n):
        return pltpu.make_async_copy(
            staged.at[n % COPY_SLOTS],
            copied.at[pl.ds(first + n * COPY_LINES, COPY_LINES)],
            sems_out.at[n % COPY_SLOTS],
        )

    lag = COPY_SLOTS // 2
    for n in range(count + lag):
        if n < count:
            if n >= COPY_SLOTS:
                copy_out(n - COPY_SLOTS).wait()
            copy_in(n).start()
        if n >= lag:
            copy_in(n - lag).wait()
            copy_out(n - lag).start()
    for n in range(max(count - COPY_SLOTS, 0), count):
        copy_out(n).wait()


def call(kernel, name, ins, outs, scratch, flops=0, moved=0, aliases=None, vmem=36, free=False):
    run = pl.pallas_call(
        kernel,
        name=name,
        out_shape=outs if free else jax.tree.map(lambda o: HBM(o.shape, o.dtype), outs),
        in_specs=[pl.BlockSpec(memory_space=place) for place in ins],
        out_specs=jax.tree.map(lambda _: pl.BlockSpec(memory_space=ANY if free else HBM), outs),
        scratch_shapes=scratch,
        input_output_aliases=aliases or {},
        cost_estimate=pl.CostEstimate(flops=flops, bytes_accessed=moved, transcendentals=0),
        compiler_params=pltpu.CompilerParams(vmem_limit_bytes=vmem * 2**20),
    )

    def pinned(*arrays):
        return run(
            *(
                pltpu.with_memory_space_constraint(x, HBM) if place == HBM else x
                for place, x in zip(ins, arrays)
            )
        )

    return pinned


def own_first(count, free=False):
    return [ANY] * count if count == 1 or free else [HBM] + [ANY] * (count - 1)


def unit_shards(spectrum, intensities, led_of_slot, row_offset, col_offset, tile_mask, aberration):
    tiles = lax.axis_size("tile")
    leds = lax.axis_size("led")
    band = M // tiles
    sizes = (leds, tiles, band)
    forward_runs = runs_of(band, FORWARD_CUTS)
    backward_runs = runs_of(band, BACKWARD_CUTS)
    forward_packed = FORWARD_TILE
    backward_packed = BACKWARD_TILE
    row_fwd, row_bwd, col_fwd, col_bwd = (jnp.asarray(t) for t in quarter_tables())
    flat = spectrum.reshape(-1, LANES)
    smem, vmem = pltpu.SMEM, pltpu.VMEM
    dma = pltpu.SemaphoreType.DMA
    part = functools.partial

    def f32(*shape):
        return jax.ShapeDtypeStruct(shape, F32)

    def over_led(arrays, packed):
        if packed:
            return [lax.all_to_all(arrays[0], "led", split_axis=0, concat_axis=0, tiled=True)]
        moved = [arrays[0]]
        for shift in range(1, leds):
            moved.append(
                lax.ppermute(arrays[shift], "led", [(i, (i + shift) % leds) for i in range(leds)])
            )
        return moved

    def over_tile(arrays, packed):
        if packed:
            return [lax.all_to_all(arrays[0], "tile", split_axis=0, concat_axis=0, tiled=True)]
        moved = [arrays[0]]
        for shift in range(1, tiles):
            moved.append(lax.ppermute(arrays[shift], "tile", [(i, i ^ shift) for i in range(tiles)]))
        return moved

    def pieces_of(run, packed):
        if packed:
            return [f32(leds, 2, run[1], LANES)]
        return [f32(2, run[1], LANES)] * leds

    def blocks_of(run, packed):
        if packed:
            return [f32(tiles, 2, run[1], band)]
        return [f32(2, run[1], band)] * tiles

    arrived = []
    for number, (run, packed) in enumerate(zip(forward_runs, FORWARD_LED)):
        taken = call(
            part(gather_kernel, sizes, run, packed), f"gather_{number}",
            [HBM] * 4, pieces_of(run, packed),
            [
                pltpu.VMEM((leds, 2, run[1], LANES), F32), dma((leds, len(spans_of(run)), 2)), dma((leds,)),
                pltpu.SMEM((3, leds), jnp.int32), dma((3,)),
            ],
            moved=2**22, vmem=8,
        )(led_of_slot, row_offset, col_offset, flat)
        arrived.append(over_led(taken, packed))
    pupil, images = pl.pallas_call(
        part(prepare_kernel, sizes),
        name="prepare",
        out_shape=[f32(2, band, M), f32(M, band)],
        in_specs=[pl.BlockSpec(memory_space=smem)] * 5 + [pl.BlockSpec(memory_space=vmem)],
        out_specs=[pl.BlockSpec(memory_space=vmem)] * 2,
        scratch_shapes=[pltpu.VMEM((band // LANES, M, LANES), F32)],
        compiler_params=pltpu.CompilerParams(vmem_limit_bytes=16 * 2**20),
        cost_estimate=pl.CostEstimate(flops=2 * 10**9, bytes_accessed=4 * 10**6, transcendentals=0),
    )(led_of_slot, row_offset, col_offset, tile_mask, aberration, intensities[0])
    def copy_part(number, after, so_far, place=HBM, also=()):
        lines = flat.shape[0] // 4
        return call(
            part(copy_kernel, number * lines, lines), f"copy_{number}",
            [place] + [HBM] * (1 + len(so_far) + len(also)), f32(*flat.shape),
            [pltpu.VMEM((COPY_SLOTS, COPY_LINES, LANES), F32), dma((COPY_SLOTS,)), dma((COPY_SLOTS,))],
            moved=2 * flat.size, aliases={2: 0} if so_far else None, vmem=16,
        )(after, flat, *so_far, *also)

    table_shape = (4, 4 * QUARTER, QUARTER)
    received, copied = [], None
    for number, (run, packed, pieces) in enumerate(zip(forward_runs, forward_packed, arrived)):
        rows = run[1]
        so_far = [copied] if number else []
        copied = copy_part(number, lines[0] if number else arrived[0][COPY_AFTER], so_far, HBM if number else ANY, () if number else arrived[1][:1])
        early = [copied]
        pieces_count = len(pieces)
        lines = call(
            part(forward_kernel, sizes, run, packed, pieces_count, len(early)), f"forward_{run[0]}", [TABLES, ANY] + own_first(pieces_count) + [HBM] * len(early),
            blocks_of(run, packed),
            [
                pltpu.VMEM(table_shape, BF16), pltpu.VMEM((2, rows, M), F32),
                pltpu.VMEM((2, rows, M), F32), pltpu.VMEM((tiles, 2, rows, band), F32),
                dma((leds + 5,)), dma((tiles, 2)),
            ],
            flops=24 * rows * M * QUARTER, moved=2**23, vmem=ROW_VMEM,
        )(row_fwd, pupil, *pieces, *early)
        received += over_tile(lines, packed)

    copied = copy_part(2, lines[0], [copied])
    arrays_in, arrays_out = len(received), sum(1 if p else tiles for p in backward_packed)
    returned = call(
        part(middle_kernel, sizes, list(zip(forward_runs, forward_packed)), list(zip(backward_runs, backward_packed))),
        "middle", [TABLES] * 2 + [ANY, HBM] + [HBM] * arrays_in,
        [b for run, packed in zip(backward_runs, backward_packed) for b in blocks_of(run, packed)],
        [
            pltpu.VMEM((4, QUARTER, 4 * QUARTER), BF16), pltpu.VMEM((4, QUARTER, 4 * QUARTER), BF16),
            pltpu.VMEM((M, band), F32), pltpu.VMEM((4, 2, QUARTER, band), F32),
            pltpu.VMEM((4, 2, QUARTER, band), F32), dma((arrays_in + 12,)), dma((arrays_out,)),
        ],
        flops=48 * band * M * QUARTER, moved=2**24, vmem=MIDDLE_VMEM, free=FREE_MIDDLE,
    )(col_fwd, col_bwd, images, copied, *received)
    updated = copy_part(3, returned[0], [copied], ANY if FREE_MIDDLE else HBM)
    count = 1 if backward_packed[0] else tiles
    returned, later = returned[:count], returned[count:]
    for number, (run, packed, led_packed) in enumerate(zip(backward_runs, backward_packed, BACKWARD_LED)):
        rows = run[1]
        sent = 1 if led_packed else leds
        lines = over_tile(returned if number == 0 else later, packed)
        held, through = (list(later), [updated]) if number == 0 else ([], [])
        count = len(lines)
        results = call(
            part(backward_kernel, sizes, run, packed, led_packed, len(held + through)), f"backward_{run[0]}",
            [TABLES, ANY] + own_first(count, FREE_MIDDLE) + [ANY] * len(held) + [HBM] * len(through),
            pieces_of(run, led_packed) + [f32(*h.shape) for h in held + through],
            [
                pltpu.VMEM(table_shape, BF16), pltpu.VMEM((2, rows, M), F32),
                pltpu.VMEM((tiles, 2, rows, band), F32), pltpu.VMEM((2, rows, M), F32),
                dma((tiles + 5,)), dma((leds,)),
            ],
            flops=24 * rows * M * QUARTER, moved=2**23, vmem=ROW_VMEM, free=FREE_BACKWARD and not (led_packed or through),
            aliases={2 + count + n: sent + n for n in range(len(held + through))},
        )(row_bwd, pupil, *lines, *held, *through)
        pieces, later = over_led(results[:sent], led_packed), results[sent : sent + len(held)]
        updated = results[-1] if through else updated
        spans = len(spans_of(run))
        updated = call(
            part(update_kernel, sizes, run), f"update_{run[0]}", [smem] * 3 + [HBM] * 2 + own_first(sent, FREE_BACKWARD and not led_packed),
            f32(*flat.shape),
            [
                pltpu.VMEM((leds, 2, rows, LANES), F32), pltpu.VMEM((leds, 2, rows, LANES), F32),
                dma((leds,)), dma((leds, spans, 2)), dma((leds, spans, 2)),
            ],
            moved=2**22, aliases={4: 0}, vmem=16,
        )(led_of_slot, row_offset, col_offset, flat, updated, *pieces)
    return updated.reshape(spectrum.shape)


def solution(mesh):
    placed = (P(None, None, "tile", "led", None), P("led", "tile", None), P(), P(), P(), P(), P())
    whole_units = mesh.shape["tile"] == 4 and M // mesh.shape["led"] == LANES
    return jax.shard_map(
        unit_shards if whole_units else general_shards,
        mesh=mesh,
        in_specs=placed,
        out_specs=P(None, None, "tile", "led", None),
        check_vma=False,
    )
```

```python
import functools
import math

import jax
import jax.numpy as jnp
import numpy as np
from jax import lax
from jax.experimental import pallas as pl
from jax.experimental.pallas import tpu as pltpu
from jax.sharding import PartitionSpec as P

M = 1024
TILE = 128
GR = 16
GC = 8
L_DEV = 1


STEP_SIZE = 0.25
HIGHEST_MODE = lax.Precision.HIGHEST


def aberration_phase(aberration, coord_p, coord_q):
    radial = coord_p * coord_p + coord_q * coord_q
    return (
        aberration[0] * (2.0 * radial - 1.0)
        + aberration[1] * (coord_p * coord_p - coord_q * coord_q)
        + aberration[2] * (2.0 * coord_p * coord_q)
        + aberration[3] * ((3.0 * radial - 2.0) * coord_p)
        + aberration[4] * ((3.0 * radial - 2.0) * coord_q)
    )


def dft_table(length):
    index_run = jnp.arange(length, dtype=jnp.int32)
    column_run = jnp.arange(2 * length, dtype=jnp.int32)
    product_mod = index_run[:, None] * (column_run % length)[None, :] % length
    shifted = (column_run >= length).astype(jnp.float32) * (0.5 * math.pi)
    angles = product_mod.astype(jnp.float32) * (2.0 * math.pi / length) - shifted[None, :]
    return jnp.cos(angles)


def small_tables(rows_len, cols_len, modulus, sign):
    first_run = jnp.arange(rows_len, dtype=jnp.int32)
    second_run = jnp.arange(cols_len, dtype=jnp.int32)
    product_mod = first_run[:, None] * second_run[None, :] % modulus
    angles = product_mod.astype(jnp.float32) * (2.0 * math.pi / modulus)
    return (jnp.cos(angles), sign * jnp.sin(angles))


def factor_dft(real_part, imag_part, sign):
    length = real_part.shape[-1]
    first = 1 << (length.bit_length() - 1) // 2
    second = length // first
    leading = real_part.shape[:-1]
    cos_first, sin_first = small_tables(first, first, first, sign)
    cos_second, sin_second = small_tables(second, second, second, sign)
    twid_cos, twid_sin = small_tables(first, second, length, sign)
    flat_re = real_part.reshape(-1, first, second)
    flat_im = imag_part.reshape(-1, first, second)

    def section_one(data, table):
        return jnp.einsum("rab,ak->rkb", data, table, precision=HIGHEST_MODE)

    def section_two(data, table):
        return jnp.einsum("rkb,bl->rlk", data, table, precision=HIGHEST_MODE)

    mid_re = section_one(flat_re, cos_first) - section_one(flat_im, sin_first)
    mid_im = section_one(flat_im, cos_first) + section_one(flat_re, sin_first)
    turned_re = mid_re * twid_cos[None] - mid_im * twid_sin[None]
    turned_im = mid_re * twid_sin[None] + mid_im * twid_cos[None]
    out_re = section_two(turned_re, cos_second) - section_two(turned_im, sin_second)
    out_im = section_two(turned_im, cos_second) + section_two(turned_re, sin_second)
    return (out_re.reshape(leading + (length,)), out_im.reshape(leading + (length,)))


def times_table(operand, transform):
    return jnp.dot(operand, transform, precision=HIGHEST_MODE, preferred_element_type=jnp.float32)


def pupil_parts(aberration, tile_gate, row_window, col_window):
    halfway = M // 2
    coord_p = ((row_window - halfway).astype(jnp.float32) / halfway)[:, None]
    coord_q = ((col_window - halfway).astype(jnp.float32) / halfway)[None, :]
    phase_map = aberration_phase(aberration, coord_p, coord_q)
    tiles_side = tile_gate.shape[0]
    tile_ids = jnp.arange(tiles_side, dtype=jnp.int32)
    pick_rows = ((row_window // TILE)[:, None] == tile_ids[None, :]).astype(jnp.float32)
    pick_cols = (tile_ids[:, None] == (col_window // TILE)[None, :]).astype(jnp.float32)
    gate_map = times_table(times_table(pick_rows, tile_gate.astype(jnp.float32)), pick_cols)
    return (gate_map * jnp.cos(phase_map), gate_map * jnp.sin(phase_map))


def stack_blocks(real_part, imag_part, tile_count, band_rows):
    slots_now = real_part.shape[0]
    rows_now = real_part.shape[1]
    stacked = jnp.stack(
        [
            real_part.reshape(slots_now, rows_now, tile_count, band_rows),
            imag_part.reshape(slots_now, rows_now, tile_count, band_rows),
        ],
        axis=3,
    )
    return stacked.reshape(slots_now, rows_now, tile_count, 2 * band_rows)


def finish_rows(rows_back, pupil_re, pupil_im, row_first, row_count, led_count, unit_cols):
    image_side = rows_back.shape[0]
    part_re = jnp.transpose(rows_back[:, 0, row_first : row_first + row_count])
    part_im = jnp.transpose(rows_back[:, 1, row_first : row_first + row_count])
    grad_re, grad_im = factor_dft(part_re, part_im, -1.0)
    grad_re = grad_re / image_side
    grad_im = grad_im / image_side
    out_re = pupil_re * grad_re + pupil_im * grad_im
    out_im = pupil_re * grad_im - pupil_im * grad_re
    stacked = jnp.stack([out_re, out_im]).reshape(2, row_count, led_count, unit_cols)
    return jnp.transpose(stacked, (2, 0, 1, 3)).reshape(led_count, 2 * row_count * unit_cols)


def general_shards(spectrum, intensities, led_of_slot, row_offset, col_offset, tile_mask, aberration):
    tile_count = lax.axis_size("tile")
    led_count = lax.axis_size("led")
    band_rows = M // tile_count
    unit_cols = M // led_count
    piece_cells = band_rows * unit_cols
    led_here = lax.axis_index("led")
    tile_here = lax.axis_index("tile")
    transform = dft_table(M)
    row_start = row_offset[led_of_slot] * TILE
    col_start = col_offset[led_of_slot] * TILE
    row_pos = tile_here * band_rows + jnp.arange(band_rows, dtype=jnp.int32)
    first_col_here = led_here * unit_cols
    row_group = (row_start[:, None] + (row_pos[None, :] - row_start[:, None]) % M) // M
    col_group = (col_start + (first_col_here - col_start) % M) // M
    row_group = row_group.reshape(led_count, L_DEV, band_rows)
    col_group = col_group.reshape(led_count, L_DEV, 1)
    line_ids = (
        (row_group * GC + col_group) * band_rows
        + jnp.arange(band_rows, dtype=jnp.int32)[None, None, :]
    ).reshape(-1)
    local_lines = jnp.transpose(
        spectrum.reshape(GR, GC, 2, band_rows, unit_cols), (0, 1, 3, 2, 4)
    ).reshape(GR * GC * band_rows, 2 * unit_cols)
    taken = local_lines[line_ids].reshape(led_count, L_DEV, band_rows, 2, unit_cols)
    outgoing = jnp.transpose(taken, (0, 1, 3, 2, 4)).reshape(led_count, L_DEV, 2 * piece_cells)
    incoming = lax.all_to_all(outgoing, "led", split_axis=0, concat_axis=0, tiled=True)
    col_all = jnp.arange(M, dtype=jnp.int32)
    slot_index = led_here * L_DEV + 0
    led_index = led_of_slot[slot_index]
    first_row = row_offset[led_index] * TILE
    first_col = col_offset[led_index] * TILE
    pupil_re, pupil_im = pupil_parts(
        aberration, tile_mask[led_index], (row_pos - first_row) % M, (col_all - first_col) % M
    )
    window = incoming[:, 0].reshape(led_count, 2, band_rows, unit_cols)
    window = jnp.transpose(window, (1, 2, 0, 3)).reshape(2, band_rows, M)
    field_re = pupil_re * window[0] - pupil_im * window[1]
    field_im = pupil_re * window[1] + pupil_im * window[0]
    fields = [jnp.stack([field_re, field_im])]
    pupils = (pupil_re, pupil_im)
    stacked_fields = jnp.stack(fields).reshape(L_DEV * 2 * band_rows, M)
    mixed = times_table(stacked_fields, transform).reshape(L_DEV, 2, band_rows, 2 * M)
    along_re = mixed[:, 0, :, :M] - mixed[:, 1, :, M:]
    along_im = mixed[:, 0, :, M:] + mixed[:, 1, :, :M]
    outbound = stack_blocks(along_re, along_im, tile_count, band_rows)
    columns = lax.all_to_all(outbound, "tile", split_axis=2, concat_axis=1, tiled=True).reshape(
        L_DEV, M, 2 * band_rows
    )
    flipped = jnp.swapaxes(columns, 1, 2)
    wave_re, wave_im = factor_dft(flipped[:, :band_rows], flipped[:, band_rows:], 1.0)
    wave_re = wave_re / M
    wave_im = wave_im / M
    measured = intensities.astype(jnp.float32)
    excess = wave_re * wave_re + wave_im * wave_im - measured
    back_re, back_im = factor_dft(excess * wave_re, excess * wave_im, -1.0)
    inbound = stack_blocks(back_re, back_im, tile_count, band_rows)
    rows_back = lax.all_to_all(inbound, "tile", split_axis=2, concat_axis=1, tiled=True).reshape(
        L_DEV, M, 2, band_rows
    )
    outgoing_all = jnp.stack(
        [finish_rows(rows_back[0], pupils[0], pupils[1], 0, band_rows, led_count, unit_cols)],
        axis=1,
    )
    received = lax.all_to_all(outgoing_all, "led", split_axis=0, concat_axis=0, tiled=True)
    grad_lines = jnp.transpose(
        received.reshape(led_count, L_DEV, 2, band_rows, unit_cols), (0, 1, 3, 2, 4)
    ).reshape(led_count * L_DEV * band_rows, 2 * unit_cols)
    grad_sum = jax.ops.segment_sum(grad_lines, line_ids, num_segments=GR * GC * band_rows)
    grad_sum = jnp.transpose(grad_sum.reshape(GR, GC, band_rows, 2, unit_cols), (0, 1, 3, 2, 4))
    updated = spectrum - STEP_SIZE * grad_sum.reshape(spectrum.shape)
    return updated


QUARTER = M // 4
HALF_LANES = 64
LANES = 128
SUB = 128
FORWARD_CUTS = (5, 3)
FORWARD_LED = (False, False)
BACKWARD_LED = (True, False)
FORWARD_TILE = (True, False)
BACKWARD_TILE = (False, False)
BACKWARD_CUTS = (4, 4)
MIDDLE_VMEM = 20
ROW_VMEM = 18
ANY = pl.ANY
HBM = pltpu.HBM
TABLES = HBM
COPY_AFTER = 2
FREE_MIDDLE = FREE_BACKWARD = True
F32 = jnp.float32
BF16 = jnp.bfloat16


def split_table(values):
    high = values.astype(np.float32).astype(jnp.bfloat16)
    low = (values - high.astype(np.float64)).astype(np.float32).astype(jnp.bfloat16)
    return high, low


def quarter_tables():
    run = np.arange(QUARTER)
    angle = 2.0 * math.pi * (run[:, None] * run[None, :] % QUARTER) / QUARTER
    cos, sin = np.cos(angle) / 32.0, np.sin(angle) / 32.0
    right = np.concatenate(split_table(np.concatenate([cos, sin], 0)), 0)
    left = np.concatenate(split_table(np.concatenate([cos, sin], 1)), 1)
    turns = 2.0 * math.pi * run[None, :] * np.arange(4)[:, None] / M
    twiddles = np.stack([np.cos(turns), np.sin(turns)], 1).reshape(8, QUARTER).astype(np.float32)
    return right, left, twiddles, np.ascontiguousarray(twiddles.T)


def times(re, im, cos, sin):
    return re * cos - im * sin, re * sin + im * cos


def halves(x):
    high = x.astype(BF16)
    low = (x - high.astype(F32)).astype(BF16)
    return high, low


def right_product(re, im, table):
    re_high, re_low = halves(re)
    im_high, im_low = halves(im)
    table = jnp.concatenate([table[: 2 * QUARTER], table], axis=0)
    top = jnp.concatenate([re_high, -im_high, re_low, -im_low, re_high, -im_high], axis=1)
    bottom = jnp.concatenate([im_high, re_high, im_low, re_low, im_high, re_high], axis=1)
    return (
        jnp.dot(top, table, preferred_element_type=F32),
        jnp.dot(bottom, table, preferred_element_type=F32),
    )


def left_product(re, im, table):
    re_high, re_low = halves(re)
    im_high, im_low = halves(im)
    table = jnp.concatenate([table[:, : 2 * QUARTER], table], axis=1)
    left = jnp.concatenate([re_high, -im_high, re_low, -im_low, re_high, -im_high], axis=0)
    right = jnp.concatenate([im_high, re_high, im_low, re_low, im_high, re_high], axis=0)
    return (
        jnp.dot(table, left, preferred_element_type=F32),
        jnp.dot(table, right, preferred_element_type=F32),
    )


def butterfly(parts, sign):
    (r0, i0), (r1, i1), (r2, i2), (r3, i3) = parts
    sr, si, dr, di = r0 + r2, i0 + i2, r0 - r2, i0 - i2
    tr, ti, er, ei = r1 + r3, i1 + i3, r1 - r3, i1 - i3
    if sign > 0:
        return ((sr + tr, si + ti), (dr - ei, di + er), (sr - tr, si - ti), (dr + ei, di - er))
    return ((sr + tr, si + ti), (dr + ei, di - er), (sr - tr, si - ti), (dr - ei, di + er))


def cos_sin(angle):
    turns = jnp.floor(angle * (2.0 / math.pi) + 0.5)
    rest = ((angle - turns * 1.5703125) - turns * 4.837512969970703125e-4) - turns * 7.549789948768648e-8
    square = rest * rest
    sine = rest + rest * square * (
        -1.6666654611e-1 + square * (8.3321608736e-3 - square * 1.9515295891e-4)
    )
    cosine = 1.0 - 0.5 * square + square * square * (
        4.166664568298827e-2 + square * (-1.388731625493765e-3 + square * 2.443315711809948e-5)
    )
    quarter = turns.astype(jnp.int32) & 3
    odd = (quarter & 1) == 1
    cos_out = jnp.where(odd, sine, cosine)
    sin_out = jnp.where(odd, cosine, sine)
    cos_out = jnp.where((quarter == 1) | (quarter == 2), -cos_out, cos_out)
    sin_out = jnp.where(quarter >= 2, -sin_out, sin_out)
    return cos_out, sin_out


def runs_of(band, cuts):
    unit = band // sum(cuts)
    runs, first = [], 0
    for cut in cuts:
        runs.append((first, cut * unit))
        first += cut * unit
    return runs


def spans_of(run):
    first, rows = run
    spans, last = [], first + rows
    while first < last:
        end = min(last, (first // TILE + 1) * TILE)
        spans.append((first, end - first))
        first = end
    return spans


def block_base(slot, row_first, col_first, band, lead, row_off, col_off):
    led = lead[slot]
    row_start = row_off[led] * TILE
    col_start = col_off[led] * TILE
    row_group = (row_start + ((row_first - row_start) & (M - 1))) // M
    col_group = (col_start + ((col_first - col_start) & (M - 1))) // M
    return (row_group * GC + col_group) * (2 * band)


def start_all(copies):
    for copy in copies:
        copy.start()


def wait_all(copies):
    for copy in copies:
        copy.wait()


def gather_kernel(sizes, run, packed, lead, row_off, col_off, spectrum, *refs):
    leds, tiles, band = sizes
    outs, (staged, sems_in, sems_out, scalars, sems_scalar) = refs[:-5], refs[-5:]
    me, tile = lax.axis_index("led"), lax.axis_index("tile")
    copies = [
        pltpu.make_async_copy(ref, scalars.at[n], sems_scalar.at[n])
        for n, ref in enumerate((lead, row_off, col_off))
    ]
    start_all(copies)
    wait_all(copies)
    lead, row_off, col_off = scalars.at[0], scalars.at[1], scalars.at[2]
    spans = spans_of(run)
    arriving = []
    for shift in range(leds):
        slot = shift if packed else lax.rem(me + shift, leds)
        for n, (first, rows) in enumerate(spans):
            base = block_base(slot, tile * band + first, me * LANES, band, lead, row_off, col_off)
            for part in range(2):
                line = pl.multiple_of(base + part * band + first, 8)
                arriving.append(
                    pltpu.make_async_copy(
                        spectrum.at[pl.ds(line, rows)],
                        staged.at[shift, part, first - run[0] : first - run[0] + rows],
                        sems_in.at[shift, n, part],
                    )
                )
    start_all(arriving)
    each = len(spans) * 2
    leaving = []
    for shift in range(leds):
        wait_all(arriving[shift * each : (shift + 1) * each])
        target = outs[0].at[shift] if packed else outs[shift]
        leaving.append(pltpu.make_async_copy(staged.at[shift], target, sems_out.at[shift]))
        leaving[-1].start()
    wait_all(leaving)


def prepare_kernel(sizes, lead, row_off, col_off, mask, aberration, intensities, pupil, images, turned):
    leds, tiles, band = sizes
    me, tile = lax.axis_index("led"), lax.axis_index("tile")
    led = lead[me]
    line = lax.broadcasted_iota(jnp.int32, (band, band), 0)
    place = lax.broadcasted_iota(jnp.int32, (band, band), 1)
    residue = 2 * (place // LANES) + (((place // HALF_LANES) & 1) ^ (tile & 1))
    wanted = residue + 4 * (place & (HALF_LANES - 1))
    chosen = (line == wanted).astype(BF16)
    for block in range(M // QUARTER):
        columns = lax.dot_general(
            intensities[:, block * QUARTER : (block + 1) * QUARTER],
            chosen,
            (((0,), (0,)), ((), ())),
            preferred_element_type=F32,
        )
        for side in range(band // LANES):
            turned[side, block * QUARTER : (block + 1) * QUARTER, :] = columns[
                :, side * LANES : (side + 1) * LANES
            ]
    for part in range(4):
        for side in range(band // LANES):
            images[part * QUARTER : (part + 1) * QUARTER, side * LANES : (side + 1) * LANES] = turned[
                side, pl.ds(part, QUARTER, 4), :
            ]
    half = M // 2
    run_p = lax.broadcasted_iota(jnp.int32, (TILE, TILE), 0)
    run_q = lax.broadcasted_iota(jnp.int32, (TILE, TILE), 1)
    tile_rows = band // TILE
    for i in range(tile_rows):
        row_tile = (tile * tile_rows + i - row_off[led]) & (M // TILE - 1)
        coord_p = (run_p + (row_tile * TILE - half)).astype(F32) / half
        for j in range(M // TILE):
            col_tile = (j - col_off[led]) & (M // TILE - 1)
            coord_q = (run_q + (col_tile * TILE - half)).astype(F32) / half
            gate = mask[led, row_tile, col_tile].astype(F32)
            cosine, sine = cos_sin(aberration_phase(aberration, coord_p, coord_q))
            where = (slice(i * TILE, (i + 1) * TILE), slice(j * TILE, (j + 1) * TILE))
            pupil[(0,) + where] = gate * cosine
            pupil[(1,) + where] = gate * sine


def forward_kernel(sizes, run, packed, piece_count, early, table, twiddles, pupil, *refs):
    leds, tiles, band = sizes
    run_first, rows = run
    pieces, refs = refs[:piece_count], refs[piece_count + early :]
    count = 1 if packed else tiles
    outs, refs = refs[:count], refs[count:]
    table_v, twiddles_v, pupil_v, window, result, sems, sems_out = refs
    me, tile = lax.axis_index("led"), lax.axis_index("tile")
    copies = []
    for shift in range(leds):
        if piece_count == 1:
            piece, first = pieces[0].at[shift], shift * LANES
        else:
            piece = pieces[shift]
            first = pl.multiple_of(lax.rem(me - shift + leds, leds) * LANES, LANES)
        copies.append(
            pltpu.make_async_copy(piece, window.at[:, :, pl.ds(first, LANES)], sems.at[shift])
        )
    copies.append(
        pltpu.make_async_copy(pupil.at[:, run_first : run_first + rows], pupil_v, sems.at[leds])
    )
    copies.append(pltpu.make_async_copy(table, table_v, sems.at[leds + 1]))
    copies.append(pltpu.make_async_copy(twiddles, twiddles_v, sems.at[leds + 2]))
    start_all(copies)
    wait_all(copies)
    parts = []
    for a in range(4):
        cells = slice(a * QUARTER, (a + 1) * QUARTER)
        parts.append(times(window[0, :, cells], window[1, :, cells], pupil_v[0, :, cells], pupil_v[1, :, cells]))
    mixed = [
        times(re, im, twiddles_v[2 * k : 2 * k + 1], twiddles_v[2 * k + 1 : 2 * k + 2])
        for k, (re, im) in enumerate(butterfly(parts, 1))
    ]
    lines = right_product(
        jnp.concatenate([re for re, _ in mixed], axis=0),
        jnp.concatenate([im for _, im in mixed], axis=0),
        table_v[...],
    )
    lane = lax.broadcasted_iota(jnp.int32, (rows, LANES), 1)
    leaving = []
    for k in (1, 3):
        places = slice((k // 2) * LANES, (k // 2 + 1) * LANES)
        for side in range(tiles // 2):
            block = slice(side * LANES, (side + 1) * LANES)
            for part in range(2):
                first = lines[part][(k - 1) * rows : k * rows, block]
                second = pltpu.roll(lines[part][k * rows : (k + 1) * rows, block], HALF_LANES, 1)
                result[2 * side, part, :, places] = jnp.where(lane < HALF_LANES, first, second)
                result[2 * side + 1, part, :, places] = jnp.where(lane < HALF_LANES, second, first)
        for shift in range(tiles):
            if packed:
                source, target = result.at[shift], outs[0].at[shift]
            else:
                source, target = result.at[tile ^ shift], outs[shift]
            leaving.append(
                pltpu.make_async_copy(
                    source.at[:, :, places], target.at[:, :, places], sems_out.at[shift, k // 2]
                )
            )
            leaving[-1].start()
    wait_all(leaving)


def tile_views(stack, run, packed, tile, tiles):
    first, rows = run
    cells = slice(first, first + rows)
    if packed:
        return [stack.at[:, :, cells]]
    return [stack.at[tile ^ shift, :, cells] for shift in range(tiles)]


def middle_kernel(sizes, runs_in, runs_out, table, twiddles, images, copied, *refs):
    leds, tiles, band = sizes
    tile = lax.axis_index("tile")
    table_v, twiddles_v, images_v, field, residual, sems, sems_out = refs[-7:]
    views = [v for run, packed in runs_in for v in tile_views(field, run, packed, tile, tiles)]
    leaving = [v for run, packed in runs_out for v in tile_views(field, run, packed, tile, tiles)]
    blocks, outs = refs[: len(views)], refs[len(views) : -7]
    count = len(views)
    copies = [pltpu.make_async_copy(b, v, sems.at[n]) for n, (b, v) in enumerate(zip(blocks, views))]
    copies.append(pltpu.make_async_copy(table, table_v, sems.at[count]))
    copies.append(pltpu.make_async_copy(twiddles, twiddles_v, sems.at[count + 1]))
    later = [
        pltpu.make_async_copy(
            images.at[k * QUARTER : (k + 1) * QUARTER],
            images_v.at[k * QUARTER : (k + 1) * QUARTER],
            sems.at[count + 2 + k],
        )
        for k in range(4)
    ]
    start_all(copies)
    start_all(later)
    wait_all(copies)
    mixed = butterfly([(field[a, 0], field[a, 1]) for a in range(4)], 1)
    for k, (re, im) in enumerate(mixed):
        cos, sin = twiddles_v[:, 2 * k : 2 * k + 1], twiddles_v[:, 2 * k + 1 : 2 * k + 2]
        wave_re, wave_im = left_product(*times(re, im, cos, sin), table_v[...])
        later[k].wait()
        measured = images_v[k * QUARTER : (k + 1) * QUARTER, :]
        excess = wave_re * wave_re + wave_im * wave_im - measured
        back_re, back_im = left_product(excess * wave_re, -(excess * wave_im), table_v[...])
        back_re, back_im = times(back_re, back_im, cos, sin)
        back_im = -back_im
        residual[k, 0] = back_re
        residual[k, 1] = back_im
    mixed = butterfly([(residual[k, 0], residual[k, 1]) for k in range(4)], -1)
    for a, (re, im) in enumerate(mixed):
        field[a, 0] = re
        field[a, 1] = im
    copies = [pltpu.make_async_copy(v, o, sems_out.at[n]) for n, (v, o) in enumerate(zip(leaving, outs))]
    start_all(copies)
    wait_all(copies)


def backward_kernel(sizes, run, packed, led_packed, held, table, twiddles, pupil, *refs):
    leds, tiles, band = sizes
    run_first, rows = run
    count = 1 if packed else tiles
    blocks, refs = refs[:count], refs[count + held :]
    sent = 1 if led_packed else leds
    outs, refs = refs[:sent], refs[sent + held :]
    table_v, twiddles_v, pupil_v, lines, result, sems, sems_out = refs
    me, tile = lax.axis_index("led"), lax.axis_index("tile")
    views = tile_views(lines, (0, rows), packed, tile, tiles)
    copies = [pltpu.make_async_copy(b, v, sems.at[n]) for n, (b, v) in enumerate(zip(blocks, views))]
    gate = pltpu.make_async_copy(pupil.at[:, run_first : run_first + rows], pupil_v, sems.at[tiles])
    copies.append(pltpu.make_async_copy(table, table_v, sems.at[tiles + 1]))
    copies.append(pltpu.make_async_copy(twiddles, twiddles_v, sems.at[tiles + 2]))
    start_all(copies + [gate])
    wait_all(copies)
    lane = lax.broadcasted_iota(jnp.int32, (rows, LANES), 1)
    stacked = [[], []]
    for k in range(4):
        cells = slice((k // 2) * LANES, (k // 2 + 1) * LANES)
        for part in range(2):
            joined = []
            for pair in range(tiles // 2):
                first, second = lines[2 * pair, part, :, cells], lines[2 * pair + 1, part, :, cells]
                if k % 2:
                    joined.append(pltpu.roll(jnp.where(lane < HALF_LANES, second, first), HALF_LANES, 1))
                else:
                    joined.append(jnp.where(lane < HALF_LANES, first, second))
            stacked[part].append(jnp.concatenate(joined, axis=1))
    all_re, all_im = right_product(
        jnp.concatenate(stacked[0], axis=0), -jnp.concatenate(stacked[1], axis=0), table_v[...]
    )
    parts = []
    for k in range(4):
        step = slice(k * rows, (k + 1) * rows)
        re, im = times(
            all_re[step], all_im[step], twiddles_v[2 * k : 2 * k + 1], twiddles_v[2 * k + 1 : 2 * k + 2]
        )
        parts.append((re, -im))
    gate.wait()
    copies = []
    for a, (re, im) in enumerate(butterfly(parts, -1)):
        cells = slice(a * QUARTER, (a + 1) * QUARTER)
        gate_re, gate_im = pupil_v[0, :, cells], pupil_v[1, :, cells]
        result[0, :, cells] = gate_re * re + gate_im * im
        result[1, :, cells] = gate_re * im - gate_im * re
        if led_packed:
            for led in range(2 * a, 2 * a + 2):
                copies.append(
                    pltpu.make_async_copy(
                        result.at[:, :, led * LANES : (led + 1) * LANES], outs[0].at[led], sems_out.at[led]
                    )
                )
                copies[-1].start()
    if not led_packed:
        for shift in range(leds):
            first = pl.multiple_of(lax.rem(me + shift, leds) * LANES, LANES)
            copies.append(
                pltpu.make_async_copy(
                    result.at[:, :, pl.ds(first, LANES)], outs[shift], sems_out.at[shift]
                )
            )
        start_all(copies)
    wait_all(copies)


def update_kernel(sizes, run, lead, row_off, col_off, spectrum, buffer, *refs):
    leds, tiles, band = sizes
    pieces = refs[:-6]
    updated, grads, cells, sems, sems_in, sems_out = refs[-6:]
    me, tile = lax.axis_index("led"), lax.axis_index("tile")
    run_first = run[0]
    arriving = []
    spans = spans_of(run)
    bases = [
        [
            block_base(slot, tile * band + first, me * LANES, band, lead, row_off, col_off)
            for first, rows in spans
        ]
        for slot in range(leds)
    ]

    def lines_at(ref, slot, n, part):
        first, rows = spans[n]
        return ref.at[pl.ds(pl.multiple_of(bases[slot][n] + part * band + first, 8), rows)]

    def cells_at(slot, n, part):
        first, rows = spans[n]
        return cells.at[slot, part, first - run_first : first - run_first + rows]

    every = [(n, part) for n in range(len(spans)) for part in range(2)]
    for slot in range(leds):
        for n, part in every:
            arriving.append(
                pltpu.make_async_copy(
                    lines_at(spectrum, slot, n, part), cells_at(slot, n, part), sems_in.at[slot, n, part]
                )
            )
    grads_arriving = []
    for slot in range(leds):
        if len(pieces) == 1:
            piece, place = pieces[0].at[slot], slot
        else:
            piece, place = pieces[slot], lax.rem(me - slot + leds, leds)
        grads_arriving.append(pltpu.make_async_copy(piece, grads.at[place], sems.at[place]))
    start_all(arriving)
    start_all(grads_arriving)
    shared = jnp.bool_(False)
    is_first = []
    for slot in range(leds):
        is_first.append([jnp.bool_(True)] * len(spans))
        for earlier in range(slot):
            for n in range(len(spans)):
                same = bases[earlier][n] == bases[slot][n]
                shared = jnp.logical_or(shared, same)
                is_first[slot][n] = jnp.logical_and(is_first[slot][n], jnp.logical_not(same))
    each = len(every)

    @pl.when(shared)
    def _():
        wait_all(arriving)
        wait_all(grads_arriving)
        for n, (first, rows) in enumerate(spans):
            where = slice(first - run_first, first - run_first + rows)
            for slot in range(leds):
                for later in range(slot + 1, leds):

                    @pl.when(jnp.logical_and(is_first[slot][n], bases[later][n] == bases[slot][n]))
                    def _():
                        grads[slot, :, where] = grads[slot, :, where] + grads[later, :, where]

    for waiting in (False, True):
        for slot in range(leds):
            if not waiting:

                @pl.when(jnp.logical_not(shared))
                def _():
                    wait_all(arriving[slot * each : (slot + 1) * each])
                    source = pieces[0].at[slot] if len(pieces) == 1 else pieces[0]
                    pltpu.make_async_copy(source, grads.at[slot], sems.at[slot]).wait()

                cells[slot] = cells[slot] - STEP_SIZE * grads[slot]
            for n in range(len(spans)):

                @pl.when(is_first[slot][n])
                def _():
                    for part in range(2):
                        copy = pltpu.make_async_copy(
                            cells_at(slot, n, part),
                            lines_at(updated, slot, n, part),
                            sems_out.at[slot, n, part],
                        )
                        if waiting:
                            copy.wait()
                        else:
                            copy.start()


COPY_LINES = 2048
COPY_SLOTS = 8


def copy_kernel(first, lines, after, spectrum, *refs):
    copied, staged, sems_in, sems_out = refs[-4:]
    count = lines // COPY_LINES

    def copy_in(n):
        return pltpu.make_async_copy(
            spectrum.at[pl.ds(first + n * COPY_LINES, COPY_LINES)],
            staged.at[n % COPY_SLOTS],
            sems_in.at[n % COPY_SLOTS],
        )

    def copy_out(n):
        return pltpu.make_async_copy(
            staged.at[n % COPY_SLOTS],
            copied.at[pl.ds(first + n * COPY_LINES, COPY_LINES)],
            sems_out.at[n % COPY_SLOTS],
        )

    lag = COPY_SLOTS // 2
    for n in range(count + lag):
        if n < count:
            if n >= COPY_SLOTS:
                copy_out(n - COPY_SLOTS).wait()
            copy_in(n).start()
        if n >= lag:
            copy_in(n - lag).wait()
            copy_out(n - lag).start()
    for n in range(max(count - COPY_SLOTS, 0), count):
        copy_out(n).wait()


def call(kernel, name, ins, outs, scratch, flops=0, moved=0, aliases=None, vmem=36, free=False):
    run = pl.pallas_call(
        kernel,
        name=name,
        out_shape=outs if free else jax.tree.map(lambda o: HBM(o.shape, o.dtype), outs),
        in_specs=[pl.BlockSpec(memory_space=place) for place in ins],
        out_specs=jax.tree.map(lambda _: pl.BlockSpec(memory_space=ANY if free else HBM), outs),
        scratch_shapes=scratch,
        input_output_aliases=aliases or {},
        cost_estimate=pl.CostEstimate(flops=flops, bytes_accessed=moved, transcendentals=0),
        compiler_params=pltpu.CompilerParams(vmem_limit_bytes=vmem * 2**20),
    )

    def pinned(*arrays):
        return run(
            *(
                pltpu.with_memory_space_constraint(x, HBM) if place == HBM else x
                for place, x in zip(ins, arrays)
            )
        )

    return pinned


def own_first(count, free=False):
    return [ANY] * count if count == 1 or free else [HBM] + [ANY] * (count - 1)


def unit_shards(spectrum, intensities, led_of_slot, row_offset, col_offset, tile_mask, aberration):
    tiles = lax.axis_size("tile")
    leds = lax.axis_size("led")
    band = M // tiles
    sizes = (leds, tiles, band)
    forward_runs = runs_of(band, FORWARD_CUTS)
    backward_runs = runs_of(band, BACKWARD_CUTS)
    forward_packed = FORWARD_TILE
    backward_packed = BACKWARD_TILE
    right, left, twiddles, twiddles_down = (jnp.asarray(t) for t in quarter_tables())
    flat = spectrum.reshape(-1, LANES)
    smem, vmem = pltpu.SMEM, pltpu.VMEM
    dma = pltpu.SemaphoreType.DMA
    part = functools.partial

    def f32(*shape):
        return jax.ShapeDtypeStruct(shape, F32)

    def over_led(arrays, packed):
        if packed:
            return [lax.all_to_all(arrays[0], "led", split_axis=0, concat_axis=0, tiled=True)]
        moved = [arrays[0]]
        for shift in range(1, leds):
            moved.append(
                lax.ppermute(arrays[shift], "led", [(i, (i + shift) % leds) for i in range(leds)])
            )
        return moved

    def over_tile(arrays, packed):
        if packed:
            return [lax.all_to_all(arrays[0], "tile", split_axis=0, concat_axis=0, tiled=True)]
        moved = [arrays[0]]
        for shift in range(1, tiles):
            moved.append(lax.ppermute(arrays[shift], "tile", [(i, i ^ shift) for i in range(tiles)]))
        return moved

    def pieces_of(run, packed):
        if packed:
            return [f32(leds, 2, run[1], LANES)]
        return [f32(2, run[1], LANES)] * leds

    def blocks_of(run, packed):
        if packed:
            return [f32(tiles, 2, run[1], band)]
        return [f32(2, run[1], band)] * tiles

    arrived = []
    for number, (run, packed) in enumerate(zip(forward_runs, FORWARD_LED)):
        taken = call(
            part(gather_kernel, sizes, run, packed), f"gather_{number}",
            [HBM] * 4, pieces_of(run, packed),
            [
                pltpu.VMEM((leds, 2, run[1], LANES), F32), dma((leds, len(spans_of(run)), 2)), dma((leds,)),
                pltpu.SMEM((3, leds), jnp.int32), dma((3,)),
            ],
            moved=2**22, vmem=8,
        )(led_of_slot, row_offset, col_offset, flat)
        arrived.append(over_led(taken, packed))
    pupil, images = pl.pallas_call(
        part(prepare_kernel, sizes),
        name="prepare",
        out_shape=[f32(2, band, M), f32(M, band)],
        in_specs=[pl.BlockSpec(memory_space=smem)] * 5 + [pl.BlockSpec(memory_space=vmem)],
        out_specs=[pl.BlockSpec(memory_space=vmem)] * 2,
        scratch_shapes=[pltpu.VMEM((band // LANES, M, LANES), F32)],
        compiler_params=pltpu.CompilerParams(vmem_limit_bytes=16 * 2**20),
        cost_estimate=pl.CostEstimate(flops=2 * 10**9, bytes_accessed=4 * 10**6, transcendentals=0),
    )(led_of_slot, row_offset, col_offset, tile_mask, aberration, intensities[0])
    def copy_part(number, after, so_far, place=HBM, also=()):
        lines = flat.shape[0] // 4
        return call(
            part(copy_kernel, number * lines, lines), f"copy_{number}",
            [place] + [HBM] * (1 + len(so_far) + len(also)), f32(*flat.shape),
            [pltpu.VMEM((COPY_SLOTS, COPY_LINES, LANES), F32), dma((COPY_SLOTS,)), dma((COPY_SLOTS,))],
            moved=2 * flat.size, aliases={2: 0} if so_far else None, vmem=16,
        )(after, flat, *so_far, *also)

    right_v = [pltpu.VMEM(right.shape, BF16), pltpu.VMEM(twiddles.shape, F32)]
    left_v = [pltpu.VMEM(left.shape, BF16), pltpu.VMEM(twiddles_down.shape, F32)]
    received, copied = [], None
    for number, (run, packed, pieces) in enumerate(zip(forward_runs, forward_packed, arrived)):
        rows = run[1]
        so_far = [copied] if number else []
        copied = copy_part(number, lines[0] if number else arrived[0][COPY_AFTER], so_far, HBM if number else ANY, () if number else arrived[1][:1])
        early = [copied]
        pieces_count = len(pieces)
        lines = call(
            part(forward_kernel, sizes, run, packed, pieces_count, len(early)), f"forward_{run[0]}", [TABLES] * 2 + [ANY] + own_first(pieces_count) + [HBM] * len(early),
            blocks_of(run, packed),
            [
                *right_v, pltpu.VMEM((2, rows, M), F32),
                pltpu.VMEM((2, rows, M), F32), pltpu.VMEM((tiles, 2, rows, band), F32),
                dma((leds + 5,)), dma((tiles, 2)),
            ],
            flops=24 * rows * M * QUARTER, moved=2**23, vmem=ROW_VMEM,
        )(right, twiddles, pupil, *pieces, *early)
        received += over_tile(lines, packed)

    copied = copy_part(2, lines[0], [copied])
    arrays_in, arrays_out = len(received), sum(1 if p else tiles for p in backward_packed)
    returned = call(
        part(middle_kernel, sizes, list(zip(forward_runs, forward_packed)), list(zip(backward_runs, backward_packed))),
        "middle", [TABLES] * 2 + [ANY, HBM] + [HBM] * arrays_in,
        [b for run, packed in zip(backward_runs, backward_packed) for b in blocks_of(run, packed)],
        [
            *left_v,
            pltpu.VMEM((M, band), F32), pltpu.VMEM((4, 2, QUARTER, band), F32),
            pltpu.VMEM((4, 2, QUARTER, band), F32), dma((arrays_in + 12,)), dma((arrays_out,)),
        ],
        flops=48 * band * M * QUARTER, moved=2**24, vmem=MIDDLE_VMEM, free=FREE_MIDDLE,
    )(left, twiddles_down, images, copied, *received)
    updated = copy_part(3, returned[0], [copied], ANY if FREE_MIDDLE else HBM)
    count = 1 if backward_packed[0] else tiles
    returned, later = returned[:count], returned[count:]
    for number, (run, packed, led_packed) in enumerate(zip(backward_runs, backward_packed, BACKWARD_LED)):
        rows = run[1]
        sent = 1 if led_packed else leds
        lines = over_tile(returned if number == 0 else later, packed)
        held, through = (list(later), [updated]) if number == 0 else ([], [])
        count = len(lines)
        results = call(
            part(backward_kernel, sizes, run, packed, led_packed, len(held + through)), f"backward_{run[0]}",
            [TABLES] * 2 + [ANY] + own_first(count, FREE_MIDDLE) + [ANY] * len(held) + [HBM] * len(through),
            pieces_of(run, led_packed) + [f32(*h.shape) for h in held + through],
            [
                *right_v, pltpu.VMEM((2, rows, M), F32),
                pltpu.VMEM((tiles, 2, rows, band), F32), pltpu.VMEM((2, rows, M), F32),
                dma((tiles + 5,)), dma((leds,)),
            ],
            flops=24 * rows * M * QUARTER, moved=2**23, vmem=ROW_VMEM, free=FREE_BACKWARD and not (led_packed or through),
            aliases={3 + count + n: sent + n for n in range(len(held + through))},
        )(right, twiddles, pupil, *lines, *held, *through)
        pieces, later = over_led(results[:sent], led_packed), results[sent : sent + len(held)]
        updated = results[-1] if through else updated
        spans = len(spans_of(run))
        updated = call(
            part(update_kernel, sizes, run), f"update_{run[0]}", [smem] * 3 + [HBM] * 2 + own_first(sent, FREE_BACKWARD and not led_packed),
            f32(*flat.shape),
            [
                pltpu.VMEM((leds, 2, rows, LANES), F32), pltpu.VMEM((leds, 2, rows, LANES), F32),
                dma((leds,)), dma((leds, spans, 2)), dma((leds, spans, 2)),
            ],
            moved=2**22, aliases={4: 0}, vmem=16,
        )(led_of_slot, row_offset, col_offset, flat, updated, *pieces)
    return updated.reshape(spectrum.shape)


def solution(mesh):
    placed = (P(None, None, "tile", "led", None), P("led", "tile", None), P(), P(), P(), P(), P())
    whole_units = mesh.shape["tile"] == 4 and M // mesh.shape["led"] == LANES
    return jax.shard_map(
        unit_shards if whole_units else general_shards,
        mesh=mesh,
        in_specs=placed,
        out_specs=P(None, None, "tile", "led", None),
        check_vma=False,
    )
```

```python
import functools
import math

import jax
import jax.numpy as jnp
import numpy as np
from jax import lax
from jax.experimental import pallas as pl
from jax.experimental.pallas import tpu as pltpu
from jax.sharding import PartitionSpec as P

M = 1024
TILE = 128
GR = 16
GC = 8
L_DEV = 1


STEP_SIZE = 0.25
HIGHEST_MODE = lax.Precision.HIGHEST


def aberration_phase(aberration, coord_p, coord_q):
    radial = coord_p * coord_p + coord_q * coord_q
    return (
        aberration[0] * (2.0 * radial - 1.0)
        + aberration[1] * (coord_p * coord_p - coord_q * coord_q)
        + aberration[2] * (2.0 * coord_p * coord_q)
        + aberration[3] * ((3.0 * radial - 2.0) * coord_p)
        + aberration[4] * ((3.0 * radial - 2.0) * coord_q)
    )


def dft_table(length):
    index_run = jnp.arange(length, dtype=jnp.int32)
    column_run = jnp.arange(2 * length, dtype=jnp.int32)
    product_mod = index_run[:, None] * (column_run % length)[None, :] % length
    shifted = (column_run >= length).astype(jnp.float32) * (0.5 * math.pi)
    angles = product_mod.astype(jnp.float32) * (2.0 * math.pi / length) - shifted[None, :]
    return jnp.cos(angles)


def small_tables(rows_len, cols_len, modulus, sign):
    first_run = jnp.arange(rows_len, dtype=jnp.int32)
    second_run = jnp.arange(cols_len, dtype=jnp.int32)
    product_mod = first_run[:, None] * second_run[None, :] % modulus
    angles = product_mod.astype(jnp.float32) * (2.0 * math.pi / modulus)
    return (jnp.cos(angles), sign * jnp.sin(angles))


def factor_dft(real_part, imag_part, sign):
    length = real_part.shape[-1]
    first = 1 << (length.bit_length() - 1) // 2
    second = length // first
    leading = real_part.shape[:-1]
    cos_first, sin_first = small_tables(first, first, first, sign)
    cos_second, sin_second = small_tables(second, second, second, sign)
    twid_cos, twid_sin = small_tables(first, second, length, sign)
    flat_re = real_part.reshape(-1, first, second)
    flat_im = imag_part.reshape(-1, first, second)

    def section_one(data, table):
        return jnp.einsum("rab,ak->rkb", data, table, precision=HIGHEST_MODE)

    def section_two(data, table):
        return jnp.einsum("rkb,bl->rlk", data, table, precision=HIGHEST_MODE)

    mid_re = section_one(flat_re, cos_first) - section_one(flat_im, sin_first)
    mid_im = section_one(flat_im, cos_first) + section_one(flat_re, sin_first)
    turned_re = mid_re * twid_cos[None] - mid_im * twid_sin[None]
    turned_im = mid_re * twid_sin[None] + mid_im * twid_cos[None]
    out_re = section_two(turned_re, cos_second) - section_two(turned_im, sin_second)
    out_im = section_two(turned_im, cos_second) + section_two(turned_re, sin_second)
    return (out_re.reshape(leading + (length,)), out_im.reshape(leading + (length,)))


def times_table(operand, transform):
    return jnp.dot(operand, transform, precision=HIGHEST_MODE, preferred_element_type=jnp.float32)


def pupil_parts(aberration, tile_gate, row_window, col_window):
    halfway = M // 2
    coord_p = ((row_window - halfway).astype(jnp.float32) / halfway)[:, None]
    coord_q = ((col_window - halfway).astype(jnp.float32) / halfway)[None, :]
    phase_map = aberration_phase(aberration, coord_p, coord_q)
    tiles_side = tile_gate.shape[0]
    tile_ids = jnp.arange(tiles_side, dtype=jnp.int32)
    pick_rows = ((row_window // TILE)[:, None] == tile_ids[None, :]).astype(jnp.float32)
    pick_cols = (tile_ids[:, None] == (col_window // TILE)[None, :]).astype(jnp.float32)
    gate_map = times_table(times_table(pick_rows, tile_gate.astype(jnp.float32)), pick_cols)
    return (gate_map * jnp.cos(phase_map), gate_map * jnp.sin(phase_map))


def stack_blocks(real_part, imag_part, tile_count, band_rows):
    slots_now = real_part.shape[0]
    rows_now = real_part.shape[1]
    stacked = jnp.stack(
        [
            real_part.reshape(slots_now, rows_now, tile_count, band_rows),
            imag_part.reshape(slots_now, rows_now, tile_count, band_rows),
        ],
        axis=3,
    )
    return stacked.reshape(slots_now, rows_now, tile_count, 2 * band_rows)


def finish_rows(rows_back, pupil_re, pupil_im, row_first, row_count, led_count, unit_cols):
    image_side = rows_back.shape[0]
    part_re = jnp.transpose(rows_back[:, 0, row_first : row_first + row_count])
    part_im = jnp.transpose(rows_back[:, 1, row_first : row_first + row_count])
    grad_re, grad_im = factor_dft(part_re, part_im, -1.0)
    grad_re = grad_re / image_side
    grad_im = grad_im / image_side
    out_re = pupil_re * grad_re + pupil_im * grad_im
    out_im = pupil_re * grad_im - pupil_im * grad_re
    stacked = jnp.stack([out_re, out_im]).reshape(2, row_count, led_count, unit_cols)
    return jnp.transpose(stacked, (2, 0, 1, 3)).reshape(led_count, 2 * row_count * unit_cols)


def general_shards(spectrum, intensities, led_of_slot, row_offset, col_offset, tile_mask, aberration):
    tile_count = lax.axis_size("tile")
    led_count = lax.axis_size("led")
    band_rows = M // tile_count
    unit_cols = M // led_count
    piece_cells = band_rows * unit_cols
    led_here = lax.axis_index("led")
    tile_here = lax.axis_index("tile")
    transform = dft_table(M)
    row_start = row_offset[led_of_slot] * TILE
    col_start = col_offset[led_of_slot] * TILE
    row_pos = tile_here * band_rows + jnp.arange(band_rows, dtype=jnp.int32)
    first_col_here = led_here * unit_cols
    row_group = (row_start[:, None] + (row_pos[None, :] - row_start[:, None]) % M) // M
    col_group = (col_start + (first_col_here - col_start) % M) // M
    row_group = row_group.reshape(led_count, L_DEV, band_rows)
    col_group = col_group.reshape(led_count, L_DEV, 1)
    line_ids = (
        (row_group * GC + col_group) * band_rows
        + jnp.arange(band_rows, dtype=jnp.int32)[None, None, :]
    ).reshape(-1)
    local_lines = jnp.transpose(
        spectrum.reshape(GR, GC, 2, band_rows, unit_cols), (0, 1, 3, 2, 4)
    ).reshape(GR * GC * band_rows, 2 * unit_cols)
    taken = local_lines[line_ids].reshape(led_count, L_DEV, band_rows, 2, unit_cols)
    outgoing = jnp.transpose(taken, (0, 1, 3, 2, 4)).reshape(led_count, L_DEV, 2 * piece_cells)
    incoming = lax.all_to_all(outgoing, "led", split_axis=0, concat_axis=0, tiled=True)
    col_all = jnp.arange(M, dtype=jnp.int32)
    slot_index = led_here * L_DEV + 0
    led_index = led_of_slot[slot_index]
    first_row = row_offset[led_index] * TILE
    first_col = col_offset[led_index] * TILE
    pupil_re, pupil_im = pupil_parts(
        aberration, tile_mask[led_index], (row_pos - first_row) % M, (col_all - first_col) % M
    )
    window = incoming[:, 0].reshape(led_count, 2, band_rows, unit_cols)
    window = jnp.transpose(window, (1, 2, 0, 3)).reshape(2, band_rows, M)
    field_re = pupil_re * window[0] - pupil_im * window[1]
    field_im = pupil_re * window[1] + pupil_im * window[0]
    fields = [jnp.stack([field_re, field_im])]
    pupils = (pupil_re, pupil_im)
    stacked_fields = jnp.stack(fields).reshape(L_DEV * 2 * band_rows, M)
    mixed = times_table(stacked_fields, transform).reshape(L_DEV, 2, band_rows, 2 * M)
    along_re = mixed[:, 0, :, :M] - mixed[:, 1, :, M:]
    along_im = mixed[:, 0, :, M:] + mixed[:, 1, :, :M]
    outbound = stack_blocks(along_re, along_im, tile_count, band_rows)
    columns = lax.all_to_all(outbound, "tile", split_axis=2, concat_axis=1, tiled=True).reshape(
        L_DEV, M, 2 * band_rows
    )
    flipped = jnp.swapaxes(columns, 1, 2)
    wave_re, wave_im = factor_dft(flipped[:, :band_rows], flipped[:, band_rows:], 1.0)
    wave_re = wave_re / M
    wave_im = wave_im / M
    measured = intensities.astype(jnp.float32)
    excess = wave_re * wave_re + wave_im * wave_im - measured
    back_re, back_im = factor_dft(excess * wave_re, excess * wave_im, -1.0)
    inbound = stack_blocks(back_re, back_im, tile_count, band_rows)
    rows_back = lax.all_to_all(inbound, "tile", split_axis=2, concat_axis=1, tiled=True).reshape(
        L_DEV, M, 2, band_rows
    )
    outgoing_all = jnp.stack(
        [finish_rows(rows_back[0], pupils[0], pupils[1], 0, band_rows, led_count, unit_cols)],
        axis=1,
    )
    received = lax.all_to_all(outgoing_all, "led", split_axis=0, concat_axis=0, tiled=True)
    grad_lines = jnp.transpose(
        received.reshape(led_count, L_DEV, 2, band_rows, unit_cols), (0, 1, 3, 2, 4)
    ).reshape(led_count * L_DEV * band_rows, 2 * unit_cols)
    grad_sum = jax.ops.segment_sum(grad_lines, line_ids, num_segments=GR * GC * band_rows)
    grad_sum = jnp.transpose(grad_sum.reshape(GR, GC, band_rows, 2, unit_cols), (0, 1, 3, 2, 4))
    updated = spectrum - STEP_SIZE * grad_sum.reshape(spectrum.shape)
    return updated


QUARTER = M // 4
HALF_LANES = 64
LANES = 128
SUB = 128
FORWARD_CUTS = (5, 3)
FORWARD_LED = (False, False)
BACKWARD_LED = (False, False)
FORWARD_TILE = (True, False)
BACKWARD_TILE = (False, True)
BACKWARD_CUTS = (4, 4)
MIDDLE_VMEM = 20
ROW_VMEM = 18
ANY = pl.ANY
HBM = pltpu.HBM
TABLES = HBM
COPY_AFTER = 2
FREE_MIDDLE = FREE_BACKWARD = True
F32 = jnp.float32
BF16 = jnp.bfloat16


def split_table(values):
    high = values.astype(np.float32).astype(jnp.bfloat16)
    low = (values - high.astype(np.float64)).astype(np.float32).astype(jnp.bfloat16)
    return high, low


def quarter_tables():
    run = np.arange(QUARTER)
    angle = 2.0 * math.pi * (run[:, None] * run[None, :] % QUARTER) / QUARTER
    cos, sin = np.cos(angle) / 32.0, np.sin(angle) / 32.0
    right = np.concatenate(split_table(np.concatenate([cos, sin], 0)), 0)
    left = np.concatenate(split_table(np.concatenate([cos, sin], 1)), 1)
    turns = 2.0 * math.pi * run[None, :] * np.arange(4)[:, None] / M
    twiddles = np.stack([np.cos(turns), np.sin(turns)], 1).reshape(8, QUARTER).astype(np.float32)
    return right, left, twiddles, np.ascontiguousarray(twiddles.T)


def times(re, im, cos, sin):
    return re * cos - im * sin, re * sin + im * cos


def halves(x):
    high = x.astype(BF16)
    low = (x - high.astype(F32)).astype(BF16)
    return high, low


def right_product(re, im, table):
    re_high, re_low = halves(re)
    im_high, im_low = halves(im)
    table = jnp.concatenate([table[: 2 * QUARTER], table], axis=0)
    top = jnp.concatenate([re_high, -im_high, re_low, -im_low, re_high, -im_high], axis=1)
    bottom = jnp.concatenate([im_high, re_high, im_low, re_low, im_high, re_high], axis=1)
    return (
        jnp.dot(top, table, preferred_element_type=F32),
        jnp.dot(bottom, table, preferred_element_type=F32),
    )


def left_product(re, im, table):
    re_high, re_low = halves(re)
    im_high, im_low = halves(im)
    table = jnp.concatenate([table[:, : 2 * QUARTER], table], axis=1)
    left = jnp.concatenate([re_high, -im_high, re_low, -im_low, re_high, -im_high], axis=0)
    right = jnp.concatenate([im_high, re_high, im_low, re_low, im_high, re_high], axis=0)
    return (
        jnp.dot(table, left, preferred_element_type=F32),
        jnp.dot(table, right, preferred_element_type=F32),
    )


def butterfly(parts, sign):
    (r0, i0), (r1, i1), (r2, i2), (r3, i3) = parts
    sr, si, dr, di = r0 + r2, i0 + i2, r0 - r2, i0 - i2
    tr, ti, er, ei = r1 + r3, i1 + i3, r1 - r3, i1 - i3
    if sign > 0:
        return ((sr + tr, si + ti), (dr - ei, di + er), (sr - tr, si - ti), (dr + ei, di - er))
    return ((sr + tr, si + ti), (dr + ei, di - er), (sr - tr, si - ti), (dr - ei, di + er))


def cos_sin(angle):
    turns = jnp.floor(angle * (2.0 / math.pi) + 0.5)
    rest = ((angle - turns * 1.5703125) - turns * 4.837512969970703125e-4) - turns * 7.549789948768648e-8
    square = rest * rest
    sine = rest + rest * square * (
        -1.6666654611e-1 + square * (8.3321608736e-3 - square * 1.9515295891e-4)
    )
    cosine = 1.0 - 0.5 * square + square * square * (
        4.166664568298827e-2 + square * (-1.388731625493765e-3 + square * 2.443315711809948e-5)
    )
    quarter = turns.astype(jnp.int32) & 3
    odd = (quarter & 1) == 1
    cos_out = jnp.where(odd, sine, cosine)
    sin_out = jnp.where(odd, cosine, sine)
    cos_out = jnp.where((quarter == 1) | (quarter == 2), -cos_out, cos_out)
    sin_out = jnp.where(quarter >= 2, -sin_out, sin_out)
    return cos_out, sin_out


def runs_of(band, cuts):
    unit = band // sum(cuts)
    runs, first = [], 0
    for cut in cuts:
        runs.append((first, cut * unit))
        first += cut * unit
    return runs


def spans_of(run):
    first, rows = run
    spans, last = [], first + rows
    while first < last:
        end = min(last, (first // TILE + 1) * TILE)
        spans.append((first, end - first))
        first = end
    return spans


def block_base(slot, row_first, col_first, band, lead, row_off, col_off):
    led = lead[slot]
    row_start = row_off[led] * TILE
    col_start = col_off[led] * TILE
    row_group = (row_start + ((row_first - row_start) & (M - 1))) // M
    col_group = (col_start + ((col_first - col_start) & (M - 1))) // M
    return (row_group * GC + col_group) * (2 * band)


def start_all(copies):
    for copy in copies:
        copy.start()


def wait_all(copies):
    for copy in copies:
        copy.wait()


def gather_kernel(sizes, run, packed, lead, row_off, col_off, spectrum, *refs):
    leds, tiles, band = sizes
    outs, (staged, sems_in, sems_out, scalars, sems_scalar) = refs[:-5], refs[-5:]
    me, tile = lax.axis_index("led"), lax.axis_index("tile")
    copies = [
        pltpu.make_async_copy(ref, scalars.at[n], sems_scalar.at[n])
        for n, ref in enumerate((lead, row_off, col_off))
    ]
    start_all(copies)
    wait_all(copies)
    lead, row_off, col_off = scalars.at[0], scalars.at[1], scalars.at[2]
    spans = spans_of(run)
    arriving = []
    for shift in range(leds):
        slot = shift if packed else lax.rem(me + shift, leds)
        for n, (first, rows) in enumerate(spans):
            base = block_base(slot, tile * band + first, me * LANES, band, lead, row_off, col_off)
            for part in range(2):
                line = pl.multiple_of(base + part * band + first, 8)
                arriving.append(
                    pltpu.make_async_copy(
                        spectrum.at[pl.ds(line, rows)],
                        staged.at[shift, part, first - run[0] : first - run[0] + rows],
                        sems_in.at[shift, n, part],
                    )
                )
    start_all(arriving)
    each = len(spans) * 2
    leaving = []
    for shift in range(leds):
        wait_all(arriving[shift * each : (shift + 1) * each])
        target = outs[0].at[shift] if packed else outs[shift]
        leaving.append(pltpu.make_async_copy(staged.at[shift], target, sems_out.at[shift]))
        leaving[-1].start()
    wait_all(leaving)


def prepare_kernel(sizes, lead, row_off, col_off, mask, aberration, intensities, pupil, images, turned):
    leds, tiles, band = sizes
    me, tile = lax.axis_index("led"), lax.axis_index("tile")
    led = lead[me]
    line = lax.broadcasted_iota(jnp.int32, (band, band), 0)
    place = lax.broadcasted_iota(jnp.int32, (band, band), 1)
    residue = 2 * (place // LANES) + (((place // HALF_LANES) & 1) ^ (tile & 1))
    wanted = residue + 4 * (place & (HALF_LANES - 1))
    chosen = (line == wanted).astype(BF16)
    for block in range(M // QUARTER):
        columns = lax.dot_general(
            intensities[:, block * QUARTER : (block + 1) * QUARTER],
            chosen,
            (((0,), (0,)), ((), ())),
            preferred_element_type=F32,
        )
        for side in range(band // LANES):
            turned[side, block * QUARTER : (block + 1) * QUARTER, :] = columns[
                :, side * LANES : (side + 1) * LANES
            ]
    for part in range(4):
        for side in range(band // LANES):
            images[part * QUARTER : (part + 1) * QUARTER, side * LANES : (side + 1) * LANES] = turned[
                side, pl.ds(part, QUARTER, 4), :
            ]
    half = M // 2
    run_p = lax.broadcasted_iota(jnp.int32, (TILE, TILE), 0)
    run_q = lax.broadcasted_iota(jnp.int32, (TILE, TILE), 1)
    tile_rows = band // TILE
    for i in range(tile_rows):
        row_tile = (tile * tile_rows + i - row_off[led]) & (M // TILE - 1)
        coord_p = (run_p + (row_tile * TILE - half)).astype(F32) / half
        for j in range(M // TILE):
            col_tile = (j - col_off[led]) & (M // TILE - 1)
            coord_q = (run_q + (col_tile * TILE - half)).astype(F32) / half
            gate = mask[led, row_tile, col_tile].astype(F32)
            cosine, sine = cos_sin(aberration_phase(aberration, coord_p, coord_q))
            where = (slice(i * TILE, (i + 1) * TILE), slice(j * TILE, (j + 1) * TILE))
            pupil[(0,) + where] = gate * cosine
            pupil[(1,) + where] = gate * sine


def forward_kernel(sizes, run, packed, piece_count, early, table, twiddles, pupil, *refs):
    leds, tiles, band = sizes
    run_first, rows = run
    pieces, refs = refs[:piece_count], refs[piece_count + early :]
    count = 1 if packed else tiles
    outs, refs = refs[:count], refs[count:]
    table_v, twiddles_v, pupil_v, window, result, sems, sems_out = refs
    me, tile = lax.axis_index("led"), lax.axis_index("tile")
    copies = []
    for shift in range(leds):
        if piece_count == 1:
            piece, first = pieces[0].at[shift], shift * LANES
        else:
            piece = pieces[shift]
            first = pl.multiple_of(lax.rem(me - shift + leds, leds) * LANES, LANES)
        copies.append(
            pltpu.make_async_copy(piece, window.at[:, :, pl.ds(first, LANES)], sems.at[shift])
        )
    copies.append(
        pltpu.make_async_copy(pupil.at[:, run_first : run_first + rows], pupil_v, sems.at[leds])
    )
    copies.append(pltpu.make_async_copy(table, table_v, sems.at[leds + 1]))
    copies.append(pltpu.make_async_copy(twiddles, twiddles_v, sems.at[leds + 2]))
    start_all(copies)
    wait_all(copies)
    parts = []
    for a in range(4):
        cells = slice(a * QUARTER, (a + 1) * QUARTER)
        parts.append(times(window[0, :, cells], window[1, :, cells], pupil_v[0, :, cells], pupil_v[1, :, cells]))
    mixed = [
        times(re, im, twiddles_v[2 * k : 2 * k + 1], twiddles_v[2 * k + 1 : 2 * k + 2])
        for k, (re, im) in enumerate(butterfly(parts, 1))
    ]
    lines = right_product(
        jnp.concatenate([re for re, _ in mixed], axis=0),
        jnp.concatenate([im for _, im in mixed], axis=0),
        table_v[...],
    )
    lane = lax.broadcasted_iota(jnp.int32, (rows, LANES), 1)
    leaving = []
    for k in (1, 3):
        places = slice((k // 2) * LANES, (k // 2 + 1) * LANES)
        for side in range(tiles // 2):
            block = slice(side * LANES, (side + 1) * LANES)
            for part in range(2):
                first = lines[part][(k - 1) * rows : k * rows, block]
                second = pltpu.roll(lines[part][k * rows : (k + 1) * rows, block], HALF_LANES, 1)
                result[2 * side, part, :, places] = jnp.where(lane < HALF_LANES, first, second)
                result[2 * side + 1, part, :, places] = jnp.where(lane < HALF_LANES, second, first)
        for shift in range(tiles):
            if packed:
                source, target = result.at[shift], outs[0].at[shift]
            else:
                source, target = result.at[tile ^ shift], outs[shift]
            leaving.append(
                pltpu.make_async_copy(
                    source.at[:, :, places], target.at[:, :, places], sems_out.at[shift, k // 2]
                )
            )
            leaving[-1].start()
    wait_all(leaving)


def tile_views(stack, run, packed, tile, tiles):
    first, rows = run
    cells = slice(first, first + rows)
    if packed:
        return [stack.at[:, :, cells]]
    return [stack.at[tile ^ shift, :, cells] for shift in range(tiles)]


def middle_kernel(sizes, runs_in, runs_out, table, twiddles, images, copied, *refs):
    leds, tiles, band = sizes
    tile = lax.axis_index("tile")
    table_v, twiddles_v, images_v, field, residual, sems, sems_out = refs[-7:]
    views = [v for run, packed in runs_in for v in tile_views(field, run, packed, tile, tiles)]
    leaving = [v for run, packed in runs_out for v in tile_views(field, run, packed, tile, tiles)]
    blocks, outs = refs[: len(views)], refs[len(views) : -7]
    count = len(views)
    copies = [pltpu.make_async_copy(b, v, sems.at[n]) for n, (b, v) in enumerate(zip(blocks, views))]
    copies.append(pltpu.make_async_copy(table, table_v, sems.at[count]))
    copies.append(pltpu.make_async_copy(twiddles, twiddles_v, sems.at[count + 1]))
    later = [
        pltpu.make_async_copy(
            images.at[k * QUARTER : (k + 1) * QUARTER],
            images_v.at[k * QUARTER : (k + 1) * QUARTER],
            sems.at[count + 2 + k],
        )
        for k in range(4)
    ]
    start_all(copies)
    start_all(later)
    wait_all(copies)
    mixed = butterfly([(field[a, 0], field[a, 1]) for a in range(4)], 1)
    for k, (re, im) in enumerate(mixed):
        cos, sin = twiddles_v[:, 2 * k : 2 * k + 1], twiddles_v[:, 2 * k + 1 : 2 * k + 2]
        wave_re, wave_im = left_product(*times(re, im, cos, sin), table_v[...])
        later[k].wait()
        measured = images_v[k * QUARTER : (k + 1) * QUARTER, :]
        excess = wave_re * wave_re + wave_im * wave_im - measured
        back_re, back_im = left_product(excess * wave_re, -(excess * wave_im), table_v[...])
        back_re, back_im = times(back_re, back_im, cos, sin)
        back_im = -back_im
        residual[k, 0] = back_re
        residual[k, 1] = back_im
    mixed = butterfly([(residual[k, 0], residual[k, 1]) for k in range(4)], -1)
    for a, (re, im) in enumerate(mixed):
        field[a, 0] = re
        field[a, 1] = im
    copies = [pltpu.make_async_copy(v, o, sems_out.at[n]) for n, (v, o) in enumerate(zip(leaving, outs))]
    start_all(copies)
    wait_all(copies)


def backward_kernel(sizes, run, packed, led_packed, held, table, twiddles, pupil, *refs):
    leds, tiles, band = sizes
    run_first, rows = run
    count = 1 if packed else tiles
    blocks, refs = refs[:count], refs[count + held :]
    sent = 1 if led_packed else leds
    outs, refs = refs[:sent], refs[sent + held :]
    table_v, twiddles_v, pupil_v, lines, result, sems, sems_out = refs
    me, tile = lax.axis_index("led"), lax.axis_index("tile")
    views = tile_views(lines, (0, rows), packed, tile, tiles)
    copies = [pltpu.make_async_copy(b, v, sems.at[n]) for n, (b, v) in enumerate(zip(blocks, views))]
    gate = pltpu.make_async_copy(pupil.at[:, run_first : run_first + rows], pupil_v, sems.at[tiles])
    copies.append(pltpu.make_async_copy(table, table_v, sems.at[tiles + 1]))
    copies.append(pltpu.make_async_copy(twiddles, twiddles_v, sems.at[tiles + 2]))
    start_all(copies + [gate])
    wait_all(copies)
    lane = lax.broadcasted_iota(jnp.int32, (rows, LANES), 1)
    stacked = [[], []]
    for k in range(4):
        cells = slice((k // 2) * LANES, (k // 2 + 1) * LANES)
        for part in range(2):
            joined = []
            for pair in range(tiles // 2):
                first, second = lines[2 * pair, part, :, cells], lines[2 * pair + 1, part, :, cells]
                if k % 2:
                    joined.append(pltpu.roll(jnp.where(lane < HALF_LANES, second, first), HALF_LANES, 1))
                else:
                    joined.append(jnp.where(lane < HALF_LANES, first, second))
            stacked[part].append(jnp.concatenate(joined, axis=1))
    all_re, all_im = right_product(
        jnp.concatenate(stacked[0], axis=0), -jnp.concatenate(stacked[1], axis=0), table_v[...]
    )
    parts = []
    for k in range(4):
        step = slice(k * rows, (k + 1) * rows)
        re, im = times(
            all_re[step], all_im[step], twiddles_v[2 * k : 2 * k + 1], twiddles_v[2 * k + 1 : 2 * k + 2]
        )
        parts.append((re, -im))
    gate.wait()
    copies = []
    for a, (re, im) in enumerate(butterfly(parts, -1)):
        cells = slice(a * QUARTER, (a + 1) * QUARTER)
        gate_re, gate_im = pupil_v[0, :, cells], pupil_v[1, :, cells]
        result[0, :, cells] = gate_re * re + gate_im * im
        result[1, :, cells] = gate_re * im - gate_im * re
        if led_packed:
            for led in range(2 * a, 2 * a + 2):
                copies.append(
                    pltpu.make_async_copy(
                        result.at[:, :, led * LANES : (led + 1) * LANES], outs[0].at[led], sems_out.at[led]
                    )
                )
                copies[-1].start()
    if not led_packed:
        for shift in range(leds):
            first = pl.multiple_of(lax.rem(me + shift, leds) * LANES, LANES)
            copies.append(
                pltpu.make_async_copy(
                    result.at[:, :, pl.ds(first, LANES)], outs[shift], sems_out.at[shift]
                )
            )
        start_all(copies)
    wait_all(copies)


def update_kernel(sizes, run, lead, row_off, col_off, spectrum, buffer, *refs):
    leds, tiles, band = sizes
    pieces = refs[:-6]
    updated, grads, cells, sems, sems_in, sems_out = refs[-6:]
    me, tile = lax.axis_index("led"), lax.axis_index("tile")
    run_first = run[0]
    arriving = []
    spans = spans_of(run)
    bases = [
        [
            block_base(slot, tile * band + first, me * LANES, band, lead, row_off, col_off)
            for first, rows in spans
        ]
        for slot in range(leds)
    ]

    def lines_at(ref, slot, n, part):
        first, rows = spans[n]
        return ref.at[pl.ds(pl.multiple_of(bases[slot][n] + part * band + first, 8), rows)]

    def cells_at(slot, n, part):
        first, rows = spans[n]
        return cells.at[slot, part, first - run_first : first - run_first + rows]

    every = [(n, part) for n in range(len(spans)) for part in range(2)]
    for slot in range(leds):
        for n, part in every:
            arriving.append(
                pltpu.make_async_copy(
                    lines_at(spectrum, slot, n, part), cells_at(slot, n, part), sems_in.at[slot, n, part]
                )
            )
    grads_arriving = []
    for slot in range(leds):
        if len(pieces) == 1:
            piece, place = pieces[0].at[slot], slot
        else:
            piece, place = pieces[slot], lax.rem(me - slot + leds, leds)
        grads_arriving.append(pltpu.make_async_copy(piece, grads.at[place], sems.at[place]))
    start_all(arriving)
    start_all(grads_arriving)
    shared = jnp.bool_(False)
    is_first = []
    for slot in range(leds):
        is_first.append([jnp.bool_(True)] * len(spans))
        for earlier in range(slot):
            for n in range(len(spans)):
                same = bases[earlier][n] == bases[slot][n]
                shared = jnp.logical_or(shared, same)
                is_first[slot][n] = jnp.logical_and(is_first[slot][n], jnp.logical_not(same))
    each = len(every)

    @pl.when(shared)
    def _():
        wait_all(arriving)
        wait_all(grads_arriving)
        for n, (first, rows) in enumerate(spans):
            where = slice(first - run_first, first - run_first + rows)
            for slot in range(leds):
                for later in range(slot + 1, leds):

                    @pl.when(jnp.logical_and(is_first[slot][n], bases[later][n] == bases[slot][n]))
                    def _():
                        grads[slot, :, where] = grads[slot, :, where] + grads[later, :, where]

    for waiting in (False, True):
        for slot in range(leds):
            if not waiting:

                @pl.when(jnp.logical_not(shared))
                def _():
                    wait_all(arriving[slot * each : (slot + 1) * each])
                    source = pieces[0].at[slot] if len(pieces) == 1 else pieces[0]
                    pltpu.make_async_copy(source, grads.at[slot], sems.at[slot]).wait()

                cells[slot] = cells[slot] - STEP_SIZE * grads[slot]
            for n in range(len(spans)):

                @pl.when(is_first[slot][n])
                def _():
                    for part in range(2):
                        copy = pltpu.make_async_copy(
                            cells_at(slot, n, part),
                            lines_at(updated, slot, n, part),
                            sems_out.at[slot, n, part],
                        )
                        if waiting:
                            copy.wait()
                        else:
                            copy.start()


COPY_LINES = 2048
COPY_SLOTS = 8


def copy_kernel(first, lines, after, spectrum, *refs):
    copied, staged, sems_in, sems_out = refs[-4:]
    count = lines // COPY_LINES

    def copy_in(n):
        return pltpu.make_async_copy(
            spectrum.at[pl.ds(first + n * COPY_LINES, COPY_LINES)],
            staged.at[n % COPY_SLOTS],
            sems_in.at[n % COPY_SLOTS],
        )

    def copy_out(n):
        return pltpu.make_async_copy(
            staged.at[n % COPY_SLOTS],
            copied.at[pl.ds(first + n * COPY_LINES, COPY_LINES)],
            sems_out.at[n % COPY_SLOTS],
        )

    lag = COPY_SLOTS // 2
    for n in range(count + lag):
        if n < count:
            if n >= COPY_SLOTS:
                copy_out(n - COPY_SLOTS).wait()
            copy_in(n).start()
        if n >= lag:
            copy_in(n - lag).wait()
            copy_out(n - lag).start()
    for n in range(max(count - COPY_SLOTS, 0), count):
        copy_out(n).wait()


def call(kernel, name, ins, outs, scratch, flops=0, moved=0, aliases=None, vmem=36, free=False):
    run = pl.pallas_call(
        kernel,
        name=name,
        out_shape=outs if free else jax.tree.map(lambda o: HBM(o.shape, o.dtype), outs),
        in_specs=[pl.BlockSpec(memory_space=place) for place in ins],
        out_specs=jax.tree.map(lambda _: pl.BlockSpec(memory_space=ANY if free else HBM), outs),
        scratch_shapes=scratch,
        input_output_aliases=aliases or {},
        cost_estimate=pl.CostEstimate(flops=flops, bytes_accessed=moved, transcendentals=0),
        compiler_params=pltpu.CompilerParams(vmem_limit_bytes=vmem * 2**20),
    )

    def pinned(*arrays):
        return run(
            *(
                pltpu.with_memory_space_constraint(x, HBM) if place == HBM else x
                for place, x in zip(ins, arrays)
            )
        )

    return pinned


def own_first(count, free=False):
    return [ANY] * count if count == 1 or free else [HBM] + [ANY] * (count - 1)


def unit_shards(spectrum, intensities, led_of_slot, row_offset, col_offset, tile_mask, aberration):
    tiles = lax.axis_size("tile")
    leds = lax.axis_size("led")
    band = M // tiles
    sizes = (leds, tiles, band)
    forward_runs = runs_of(band, FORWARD_CUTS)
    backward_runs = runs_of(band, BACKWARD_CUTS)
    forward_packed = FORWARD_TILE
    backward_packed = BACKWARD_TILE
    right, left, twiddles, twiddles_down = (jnp.asarray(t) for t in quarter_tables())
    flat = spectrum.reshape(-1, LANES)
    smem, vmem = pltpu.SMEM, pltpu.VMEM
    dma = pltpu.SemaphoreType.DMA
    part = functools.partial

    def f32(*shape):
        return jax.ShapeDtypeStruct(shape, F32)

    def over_led(arrays, packed):
        if packed:
            return [lax.all_to_all(arrays[0], "led", split_axis=0, concat_axis=0, tiled=True)]
        moved = [arrays[0]]
        for shift in range(1, leds):
            moved.append(
                lax.ppermute(arrays[shift], "led", [(i, (i + shift) % leds) for i in range(leds)])
            )
        return moved

    def over_tile(arrays, packed):
        if packed:
            return [lax.all_to_all(arrays[0], "tile", split_axis=0, concat_axis=0, tiled=True)]
        moved = [arrays[0]]
        for shift in range(1, tiles):
            moved.append(lax.ppermute(arrays[shift], "tile", [(i, i ^ shift) for i in range(tiles)]))
        return moved

    def pieces_of(run, packed):
        if packed:
            return [f32(leds, 2, run[1], LANES)]
        return [f32(2, run[1], LANES)] * leds

    def blocks_of(run, packed):
        if packed:
            return [f32(tiles, 2, run[1], band)]
        return [f32(2, run[1], band)] * tiles

    arrived = []
    for number, (run, packed) in enumerate(zip(forward_runs, FORWARD_LED)):
        taken = call(
            part(gather_kernel, sizes, run, packed), f"gather_{number}",
            [HBM] * 4, pieces_of(run, packed),
            [
                pltpu.VMEM((leds, 2, run[1], LANES), F32), dma((leds, len(spans_of(run)), 2)), dma((leds,)),
                pltpu.SMEM((3, leds), jnp.int32), dma((3,)),
            ],
            moved=2**22, vmem=8,
        )(led_of_slot, row_offset, col_offset, flat)
        arrived.append(over_led(taken, packed))
    pupil, images = pl.pallas_call(
        part(prepare_kernel, sizes),
        name="prepare",
        out_shape=[f32(2, band, M), f32(M, band)],
        in_specs=[pl.BlockSpec(memory_space=smem)] * 5 + [pl.BlockSpec(memory_space=vmem)],
        out_specs=[pl.BlockSpec(memory_space=vmem)] * 2,
        scratch_shapes=[pltpu.VMEM((band // LANES, M, LANES), F32)],
        compiler_params=pltpu.CompilerParams(vmem_limit_bytes=16 * 2**20),
        cost_estimate=pl.CostEstimate(flops=2 * 10**9, bytes_accessed=4 * 10**6, transcendentals=0),
    )(led_of_slot, row_offset, col_offset, tile_mask, aberration, intensities[0])
    def copy_part(number, after, so_far, place=HBM, also=()):
        lines = flat.shape[0] // 4
        return call(
            part(copy_kernel, number * lines, lines), f"copy_{number}",
            [place] + [HBM] * (1 + len(so_far) + len(also)), f32(*flat.shape),
            [pltpu.VMEM((COPY_SLOTS, COPY_LINES, LANES), F32), dma((COPY_SLOTS,)), dma((COPY_SLOTS,))],
            moved=2 * flat.size, aliases={2: 0} if so_far else None, vmem=16,
        )(after, flat, *so_far, *also)

    right_v = [pltpu.VMEM(right.shape, BF16), pltpu.VMEM(twiddles.shape, F32)]
    left_v = [pltpu.VMEM(left.shape, BF16), pltpu.VMEM(twiddles_down.shape, F32)]
    received, copied = [], None
    for number, (run, packed, pieces) in enumerate(zip(forward_runs, forward_packed, arrived)):
        rows = run[1]
        so_far = [copied] if number else []
        copied = copy_part(number, lines[0] if number else arrived[0][COPY_AFTER], so_far, HBM if number else ANY, () if number else arrived[1][:1])
        early = [copied]
        pieces_count = len(pieces)
        lines = call(
            part(forward_kernel, sizes, run, packed, pieces_count, len(early)), f"forward_{run[0]}", [TABLES] * 2 + [ANY] + own_first(pieces_count) + [HBM] * len(early),
            blocks_of(run, packed),
            [
                *right_v, pltpu.VMEM((2, rows, M), F32),
                pltpu.VMEM((2, rows, M), F32), pltpu.VMEM((tiles, 2, rows, band), F32),
                dma((leds + 5,)), dma((tiles, 2)),
            ],
            flops=24 * rows * M * QUARTER, moved=2**23, vmem=ROW_VMEM,
        )(right, twiddles, pupil, *pieces, *early)
        received += over_tile(lines, packed)

    copied = copy_part(2, lines[0], [copied])
    arrays_in, arrays_out = len(received), sum(1 if p else tiles for p in backward_packed)
    returned = call(
        part(middle_kernel, sizes, list(zip(forward_runs, forward_packed)), list(zip(backward_runs, backward_packed))),
        "middle", [TABLES] * 2 + [ANY, HBM] + [HBM] * arrays_in,
        [b for run, packed in zip(backward_runs, backward_packed) for b in blocks_of(run, packed)],
        [
            *left_v,
            pltpu.VMEM((M, band), F32), pltpu.VMEM((4, 2, QUARTER, band), F32),
            pltpu.VMEM((4, 2, QUARTER, band), F32), dma((arrays_in + 12,)), dma((arrays_out,)),
        ],
        flops=48 * band * M * QUARTER, moved=2**24, vmem=MIDDLE_VMEM, free=FREE_MIDDLE,
    )(left, twiddles_down, images, copied, *received)
    updated = copy_part(3, returned[0], [copied], ANY if FREE_MIDDLE else HBM)
    count = 1 if backward_packed[0] else tiles
    returned, later = returned[:count], returned[count:]
    for number, (run, packed, led_packed) in enumerate(zip(backward_runs, backward_packed, BACKWARD_LED)):
        rows = run[1]
        sent = 1 if led_packed else leds
        lines = over_tile(returned if number == 0 else later, packed)
        held, through = (list(later), [updated]) if number == 0 else ([], [])
        count = len(lines)
        results = call(
            part(backward_kernel, sizes, run, packed, led_packed, len(held + through)), f"backward_{run[0]}",
            [TABLES] * 2 + [ANY] + own_first(count, FREE_MIDDLE) + [ANY] * len(held) + [HBM] * len(through),
            pieces_of(run, led_packed) + [f32(*h.shape) for h in held + through],
            [
                *right_v, pltpu.VMEM((2, rows, M), F32),
                pltpu.VMEM((tiles, 2, rows, band), F32), pltpu.VMEM((2, rows, M), F32),
                dma((tiles + 5,)), dma((leds,)),
            ],
            flops=24 * rows * M * QUARTER, moved=2**23, vmem=ROW_VMEM, free=FREE_BACKWARD and not (led_packed or through),
            aliases={3 + count + n: sent + n for n in range(len(held + through))},
        )(right, twiddles, pupil, *lines, *held, *through)
        pieces, later = over_led(results[:sent], led_packed), results[sent : sent + len(held)]
        updated = results[-1] if through else updated
        spans = len(spans_of(run))
        updated = call(
            part(update_kernel, sizes, run), f"update_{run[0]}", [smem] * 3 + [HBM] * 2 + own_first(sent, FREE_BACKWARD and not led_packed),
            f32(*flat.shape),
            [
                pltpu.VMEM((leds, 2, rows, LANES), F32), pltpu.VMEM((leds, 2, rows, LANES), F32),
                dma((leds,)), dma((leds, spans, 2)), dma((leds, spans, 2)),
            ],
            moved=2**22, aliases={4: 0}, vmem=16,
        )(led_of_slot, row_offset, col_offset, flat, updated, *pieces)
    return updated.reshape(spectrum.shape)


def solution(mesh):
    placed = (P(None, None, "tile", "led", None), P("led", "tile", None), P(), P(), P(), P(), P())
    whole_units = mesh.shape["tile"] == 4 and M // mesh.shape["led"] == LANES
    return jax.shard_map(
        unit_shards if whole_units else general_shards,
        mesh=mesh,
        in_specs=placed,
        out_specs=P(None, None, "tile", "led", None),
        check_vma=False,
    )
```
